32 devices in a mesh: wide: 8 (over z, y), narrow: 4 (over x, core).
Axes of the slice: x: 2, y: 2, z: 4, core: 2. Of those that a mesh axis runs over, the one named last changes fastest.
Arguments:
- tokens: bfloat16 [8192, 1024], P('wide'), may hold values from -6 to 6
- gain_in: bfloat16 [1024], replicated, may hold values from 0.5 to 1.5
- gain_mid: bfloat16 [1024], replicated, may hold values from 0.5 to 1.5
- w_qkv: bfloat16 [1024, 3, 1024], P(None, None, 'narrow'), may hold values from -0.1875 to 0.1875
- w_gate: bfloat16 [1024, 16], replicated, may hold values from -0.1875 to 0.1875
- w_decay: bfloat16 [1024, 2], replicated, may hold values from -0.1875 to 0.1875
- conv_kernel: bfloat16 [3, 4, 1024], P(None, None, 'narrow'), may hold values from -3 to 3
- persistent: bfloat16 [2, 16, 1024], P(None, None, 'narrow'), may hold values from -1.5 to 1.5
- w_out: bfloat16 [1024, 1024], P('narrow'), may hold values from -0.5 to 0.5
- mem_in: bfloat16 [1024, 4096], P(None, 'narrow'), may hold values from -1.5 to 1.5
- mem_out: bfloat16 [4096, 1024], P('narrow'), may hold values from -0.09375 to 0.09375
- w_up: bfloat16 [1024, 2, 4096], P(None, None, 'narrow'), may hold values from -0.1875 to 0.1875
- w_down: bfloat16 [4096, 1024], P('narrow'), may hold values from -0.09375 to 0.09375
- doc_len: int32 [8, 8], P('wide'), may hold values from 1 to 512, 1024 in all within a row
- reset: int32 [8], P('wide'), may hold values 0 or 1
- cotangent: bfloat16 [8192, 1024], P('wide', 'narrow'), may hold values from -6 to 6
Outputs:
- output: bfloat16 [8192, 1024], P('wide', 'narrow')
- grad_input: float32 [8192, 1024], P('wide', 'narrow')
- grad_gain_in: float32 [1024], replicated
- grad_gain_mid: float32 [1024], replicated
- grad_w_qkv: float32 [1024, 3, 1024], P('wide', None, 'narrow')
- grad_w_gate: float32 [1024, 16], P('wide')
- grad_w_decay: float32 [1024, 2], replicated
- grad_conv: float32 [3, 4, 1024], replicated
- grad_persistent: float32 [2, 16, 1024], replicated
- grad_w_out: float32 [1024, 1024], P('narrow', 'wide')
- grad_mem_in: float32 [1024, 4096], P('wide', 'narrow')
- grad_mem_out: float32 [4096, 1024], P('narrow', 'wide')
- grad_w_up: float32 [1024, 2, 4096], P('wide', None, 'narrow')
- grad_w_down: float32 [4096, 1024], P('narrow', 'wide')
The draws below stay inside these ranges and needn't reach their ends.
Inputs may be any that keep to these rules, and one draw needn't show every extreme that they name: `doc_len`: in each row the 8 lengths sum to 1024, and the longest is exactly 512.
All inputs are finite; a program needn't handle non-finite values. No bound on the sum of `reset` on one device may be relied on, other than what follows from the above.
Results may differ from the reference program's by a relative error of at most 0.014.
Values may be sent and summed in bfloat16 or wider, within the bound.
No kernel may reach another device: no remote copies, remote signals or barrier semaphores. Data moves between devices by JAX's collectives and lax.ppermute only.
A program may use at most 256 MiB of HBM per device.

```python
import math
import jax
import jax.numpy as jnp
import numpy as np
from jax import lax

D = 1024
HEADS = 16
HD = 64
FM = 4096
FF = 4096
LEN = 1024
CH = 512
WIN = 512
NP = 16
KC = 4
NDOC = 8
MOST = 512
ROWS = 8
TOKENS = 8192


def place_ends(entries, own_key, low, largest):
    index_at = [jax.random.randint(jax.random.fold_in(own_key, axis), (), 0, length) for axis, length in enumerate(entries.shape)]
    longest = entries.shape.index(max(entries.shape))
    neighbour = index_at[:longest] + [(index_at[longest] + 1) % entries.shape[longest]] + index_at[longest + 1:]
    return entries.at[tuple(index_at)].set(low).at[tuple(neighbour)].set(largest)


def levels(own_key, extent, shards, least, largest):
    level = 1.0
    for position, shards_of in shards:
        draws = jax.random.uniform(jax.random.fold_in(jax.random.fold_in(own_key, 6), position), (shards_of,), jnp.float32, least / len(shards), largest / len(shards))
        level = level * jnp.repeat(jnp.exp(draws), extent[position] // shards_of).reshape((-1,) + (1,) * (len(extent) - 1 - position))
    return level


def length_profile(number_of, total, limit, slope):
    loads = [(1 << 20) // math.isqrt(standing ** slope) + 1 for standing in range(2, number_of + 1)]
    surplus, given = total - limit - (number_of - 1), [1] * (number_of - 1)
    while surplus > 0:
        movable = [i for i in range(number_of - 1) if given[i] < limit]
        pool, remaining = sum([loads[i] for i in movable]), surplus
        for i in movable:
            more = min(limit - given[i], max(1, remaining * loads[i] // pool), surplus)
            given[i] = given[i] + more
            surplus = surplus - more
    return np.array([limit] + given)


def ragged_sizes(key, number_of, total, reach, skew):
    if number_of == 2:
        one = jax.random.randint(key, (), max(1, total - reach), min(reach, total - 1) + 1)
        return jnp.stack([one, total - one])
    sizes = jnp.asarray(length_profile(number_of, total, reach, skew), jnp.int32)
    pairs = (number_of - 1) // 2
    source_of, sink = sizes[1:1 + 2 * pairs:2], sizes[2:2 + 2 * pairs:2]
    slack = jnp.minimum(source_of - 1, reach - sink)
    passed = jax.random.randint(jax.random.fold_in(key, 1), (pairs,), 0, 1 << 20) % (slack + 1)
    sizes = sizes.at[1:1 + 2 * pairs:2].set(source_of - passed).at[2:2 + 2 * pairs:2].set(sink + passed)
    return sizes[jax.random.permutation(jax.random.fold_in(key, 2), number_of)]


def scatter_about(rng, dims, scale, reach, pieces=(), kind=jnp.bfloat16):
    factor_of = levels(rng, dims, pieces, -0.22, 0.18) if pieces else 1.0
    drawn = jax.random.normal(rng, dims, jnp.float32) * scale * factor_of
    return jnp.minimum(jnp.maximum(drawn, -reach), reach).astype(kind)


def setup_inputs(seed: int = 0) -> dict:
    keys = jax.random.split(jax.random.key(seed), 17)
    tokens = scatter_about(keys[0], (TOKENS, D), 1.0, 6.0, ((0, 8),))
    gain_in = jnp.clip(1.0 + 0.1 * jax.random.normal(keys[1], (D,), jnp.float32), 0.5, 1.5).astype(jnp.bfloat16)
    gain_mid = jnp.clip(1.0 + 0.1 * jax.random.normal(keys[2], (D,), jnp.float32), 0.5, 1.5).astype(jnp.bfloat16)
    w_qkv = scatter_about(keys[3], (D, 3, D), D ** -0.5, 0.1875, ((2, 4),))
    w_gate = scatter_about(keys[4], (D, HEADS), D ** -0.5, 0.1875)
    w_decay = scatter_about(keys[5], (D, 2), D ** -0.5, 0.1875)
    conv_kernel = scatter_about(keys[6], (3, KC, D), 0.5, 3.0, ((2, 4),))
    persistent = scatter_about(keys[7], (2, NP, D), 0.25, 1.5, ((2, 4),))
    w_out = scatter_about(keys[8], (D, D), (D // 8) ** -0.5, 0.5, ((0, 4),))
    mem_in = scatter_about(keys[9], (D, FM), HEADS ** -0.5, 1.5, ((1, 4),))
    mem_out = scatter_about(keys[10], (FM, D), FM ** -0.5, 0.09375, ((0, 4),))
    w_up = scatter_about(keys[11], (D, 2, FF), D ** -0.5, 0.1875, ((2, 4),))
    w_down = scatter_about(keys[12], (FF, D), FF ** -0.5, 0.09375, ((0, 4),))
    doc_len = jax.vmap(lambda own: ragged_sizes(own, NDOC, LEN, MOST, 2))(jax.random.split(keys[13], ROWS)).reshape((ROWS, NDOC)).astype(jnp.int32)
    reset = place_ends((jax.random.randint(keys[14], (ROWS,), 0, 2) < 1).astype(jnp.int32), jax.random.fold_in(keys[14], 1), 0, 1)
    cotangent = scatter_about(keys[15], (TOKENS, D), 1.0, 6.0, ((0, 8), (1, 4)))
    return {"tokens": tokens, "gain_in": gain_in, "gain_mid": gain_mid, "w_qkv": w_qkv, "w_gate": w_gate, "w_decay": w_decay, "conv_kernel": conv_kernel, "persistent": persistent, "w_out": w_out, "mem_in": mem_in, "mem_out": mem_out, "w_up": w_up, "w_down": w_down, "doc_len": doc_len, "reset": reset, "cotangent": cotangent}


EPS = 1e-06
NEG = -1e+30
STEP_IN = 128.0
STEP_OUT = 0.5
HIGHEST = lax.Precision.HIGHEST

@jax.custom_vjp
def low(v):
    return lax.optimization_barrier(v.astype(jnp.bfloat16)).astype(jnp.float32)

@jax.custom_vjp
def low_back(v):
    return v

def low_keep(v):
    return (low(v), None)

def low_pass(kept, grad):
    return (grad,)

def back_keep(v):
    return (v, None)

def back_low(kept, grad):
    return (low(grad),)
low.defvjp(low_keep, low_pass)
low_back.defvjp(back_keep, back_low)

def segment_ids(lengths):
    doc_ends = jnp.cumsum(lengths).astype(jnp.int32)
    places = jnp.arange(LEN, dtype=jnp.int32)
    return lax.optimization_barrier(jnp.sum((places[:, None] >= doc_ends[None, :]).astype(jnp.int32), axis=1))

def mix_inputs(projected, kernel, segment):
    feat_width = projected.shape[2]
    summed = kernel[:, 0][None] * projected
    for offset in range(1, KC):
        shifted = jnp.concatenate([jnp.zeros((offset, 3, feat_width), projected.dtype), projected[:-offset]], 0)
        same_doc = jnp.concatenate([jnp.zeros((offset,), jnp.bool_), segment[offset:] == segment[:-offset]], 0)
        summed = summed + kernel[:, offset][None] * jnp.where(same_doc[:, None, None], shifted, 0.0)
    active = jax.nn.silu(summed)
    paired = active[:, :2].reshape(LEN, 2, feat_width // HD, HD)
    paired = paired * lax.rsqrt(lax.optimization_barrier(jnp.sum(paired * paired, -1, keepdims=True)) + EPS)
    return jnp.concatenate([paired.reshape(LEN, 2, feat_width), active[:, 2:]], 1)

def silu_slope(pre_act):
    sig_val = jax.nn.sigmoid(pre_act)
    return sig_val * (1.0 + pre_act * (1.0 - sig_val))

def attend_row(queries, key_rows, value_rows, pers_keys, pers_values, segment):
    places = jnp.arange(LEN, dtype=jnp.int32)
    score_scale = HD ** 0.5

    def attend_block(block_start):
        query_pos = block_start + jnp.arange(CH, dtype=jnp.int32)
        query_blk = lax.dynamic_slice_in_dim(queries, block_start, CH, 0)
        query_seg = lax.dynamic_slice_in_dim(segment, block_start, CH, 0)
        allowed = (places[None] <= query_pos[:, None]) & (query_pos[:, None] - places[None] < WIN) & (segment[None] == query_seg[:, None])
        scores = low_back(score_scale * jnp.einsum('qhd,khd->hqk', query_blk, key_rows, precision=HIGHEST))
        scores = jnp.where(allowed[None], scores, NEG)
        pers_scores = low_back(score_scale * jnp.einsum('qhd,khd->hqk', query_blk, pers_keys, precision=HIGHEST))
        row_peak = jnp.maximum(lax.optimization_barrier(jnp.max(scores, -1)), lax.optimization_barrier(jnp.max(pers_scores, -1)))[..., None]
        weights = jnp.exp(scores - row_peak)
        pers_weights = jnp.exp(pers_scores - row_peak)
        normal = lax.optimization_barrier(jnp.sum(weights, -1, keepdims=True)) + lax.optimization_barrier(jnp.sum(pers_weights, -1, keepdims=True))
        prob_low = low(weights / normal)
        pers_low = low(pers_weights / normal)
        return jnp.einsum('hqk,khd->qhd', prob_low, value_rows, precision=HIGHEST) + jnp.einsum('hqk,khd->qhd', pers_low, pers_values, precision=HIGHEST)
    starts = jnp.arange(LEN // CH, dtype=jnp.int32) * CH
    return lax.map(jax.checkpoint(attend_block), starts).reshape(LEN, HEADS * HD)

def reference(tokens, gain_in, gain_mid, w_qkv, w_gate, w_decay, conv_kernel, persistent, w_out, mem_in, mem_out, w_up, w_down, doc_len, reset, cotangent):
    segments = jax.vmap(segment_ids)(doc_len)
    keep_rows = 1.0 - reset.astype(jnp.float32)
    inputs = tokens.astype(jnp.float32).reshape(ROWS, LEN, D)
    weights_all = tuple((array_in.astype(jnp.float32) for array_in in (gain_in, gain_mid, w_qkv, w_gate, w_decay, conv_kernel, persistent, w_out, mem_in, mem_out, w_up, w_down)))

    def whole_layer(inputs, gain_in, gain_mid, w_qkv, w_gate, w_decay, conv_kernel, persistent, w_out, mem_in, mem_out, w_up, w_down):

        def normed(rows_x, gain_vec):
            return low(rows_x * lax.rsqrt(lax.optimization_barrier(jnp.mean(rows_x * rows_x, -1, keepdims=True)) + EPS) * gain_vec)

        def row_step(running, row_in):
            rows_x, segment, keep_one = row_in
            normed_in = normed(rows_x, gain_in)
            projected = low_back(jnp.dot(normed_in, w_qkv.reshape(D, 3 * D), precision=HIGHEST)).reshape(LEN, 3, D)
            active = low(mix_inputs(projected, conv_kernel, segment))
            queries = active[:, 0]
            key_rows = active[:, 1]
            value_rows = active[:, 2]
            key_blk = key_rows[:CH]
            value_blk = value_rows[:CH]
            key_pre = low_back(jnp.dot(key_blk, mem_in, precision=HIGHEST))
            key_hidden = low(jax.nn.silu(key_pre))
            predicted = low_back(jnp.dot(key_hidden, mem_out, precision=HIGHEST))
            error_low = low(predicted - value_blk)
            back_hidden = low_back(jnp.dot(error_low, mem_out.T, precision=HIGHEST))
            slope_low = low(back_hidden * silu_slope(key_pre))
            grad_in = low_back(jnp.dot(key_blk.T, slope_low, precision=HIGHEST) / CH)
            grad_out = low_back(jnp.dot(key_hidden.T, error_low, precision=HIGHEST) / CH)
            mem_gates = jax.nn.sigmoid(jnp.dot(normed_in, w_decay, precision=HIGHEST))
            decay_rate = jnp.mean(mem_gates[:CH, 0])
            step_rate = jnp.mean(mem_gates[:CH, 1])
            memory_in = mem_in - keep_one * (decay_rate * mem_in + step_rate * STEP_IN * grad_in)
            memory_out = mem_out - keep_one * (decay_rate * mem_out + step_rate * STEP_OUT * grad_out)

            def recall(query_blk, first_w, second_w):
                pre_act = low_back(jnp.dot(query_blk, first_w, precision=HIGHEST))
                return low_back(jnp.dot(low(jax.nn.silu(pre_act)), second_w, precision=HIGHEST))
            recalled = jnp.concatenate([recall(queries[:CH], mem_in, mem_out), recall(queries[CH:], low(memory_in), low(memory_out))], 0)
            heads_out = attend_row(queries.reshape(LEN, HEADS, HD), key_rows.reshape(LEN, HEADS, HD), value_rows.reshape(LEN, HEADS, HD), persistent[0].reshape(NP, HEADS, HD), persistent[1].reshape(NP, HEADS, HD), segment)
            attended = low(low_back(heads_out))
            mixed_out = low_back(jnp.dot(attended, w_out, precision=HIGHEST))
            gate_act = jax.nn.sigmoid(jnp.dot(normed_in, w_gate, precision=HIGHEST))
            middle = rows_x + mixed_out + jnp.repeat(gate_act, HD, axis=1) * recalled
            normed_mid = normed(middle, gain_mid)
            gate_up = low_back(jnp.dot(normed_mid, w_up.reshape(D, 2 * FF), precision=HIGHEST)).reshape(LEN, 2, FF)
            hidden = low(jax.nn.silu(gate_up[:, 0]) * gate_up[:, 1])
            return (running, middle + low_back(jnp.dot(hidden, w_down, precision=HIGHEST)))
        unused_carry, outputs = lax.scan(jax.checkpoint(row_step), jnp.zeros((), jnp.float32), (inputs, segments, keep_rows))
        return outputs
    outputs, pullback = jax.vjp(whole_layer, inputs, *weights_all)
    gradients = pullback(cotangent.astype(jnp.float32).reshape(ROWS, LEN, D))
    return (outputs.reshape(TOKENS, D).astype(jnp.bfloat16), gradients[0].reshape(TOKENS, D), gradients[1], gradients[2], gradients[3], gradients[4], gradients[5], gradients[6], gradients[7], gradients[8], gradients[9], gradients[10], gradients[11], gradients[12])
```

```python
import jax
import jax.numpy as jnp
from jax import lax
from jax.sharding import PartitionSpec as P

D = 1024
HEADS = 16
HD = 64
LEN = 1024
CH = 512
WIN = 512
NP = 16
KC = 4


EPS = 1e-06
NEG = -1e30
STEP_IN = 128.0
STEP_OUT = 0.5
HIGHEST = lax.Precision.HIGHEST
LOW = jnp.bfloat16
F32 = jnp.float32


def segment_ids(lengths):
    doc_ends = jnp.cumsum(lengths)
    places = jnp.arange(LEN, dtype=jnp.int32)
    return jnp.sum((places[:, None] >= doc_ends[None, :]).astype(jnp.int32), axis=1)


def mix_inputs(projected, kernel, segment):
    feat_width = projected.shape[2]
    summed = kernel[:, 0][None] * projected
    for offset in range(1, KC):
        shifted = jnp.concatenate(
            [jnp.zeros((offset, 3, feat_width), projected.dtype), projected[:-offset]], 0
        )
        same_doc = jnp.concatenate(
            [jnp.zeros((offset,), jnp.bool_), segment[offset:] == segment[:-offset]], 0
        )
        summed = summed + kernel[:, offset][None] * jnp.where(same_doc[:, None, None], shifted, 0.0)
    active = jax.nn.silu(summed)
    paired = active[:, :2].reshape(LEN, 2, feat_width // HD, HD)
    paired = paired * lax.rsqrt(jnp.sum(paired * paired, -1, keepdims=True) + EPS)
    return jnp.concatenate([paired.reshape(LEN, 2, feat_width), active[:, 2:]], 1)


def product(formula, left_op, right_op):
    return jnp.einsum(formula, left_op, right_op, preferred_element_type=jnp.float32)


def norm_back(grad_norm, unit_val, inverse, gain_vec):
    scaled = grad_norm * gain_vec
    return inverse * (scaled - unit_val * jnp.mean(scaled * unit_val, -1, keepdims=True))


def swish_parts(pre_act):
    sig_val = jax.nn.sigmoid(pre_act)
    return (sig_val, sig_val * (1.0 + pre_act * (1.0 - sig_val)))


def flip(v, axis, bit):
    size = lax.axis_size(axis)
    return lax.ppermute(v, axis, [(i, i ^ bit) for i in range(size)])


def bits_of(axis):
    size = lax.axis_size(axis)
    out = []
    bit = 1
    while bit < size:
        out.append(bit)
        bit *= 2
    assert bit == size
    return out


def pick(v, index, axis=0):
    return lax.dynamic_index_in_dim(v, index, axis, keepdims=False)


def cut(v, start, width, axis):
    return lax.dynamic_slice_in_dim(v, start, width, axis)


def gather_cols(v, axis="narrow"):
    me = lax.axis_index(axis)
    parts = {0: v}
    for bit in reversed(bits_of(axis)):
        for key in list(parts):
            parts[key ^ bit] = flip(parts[key], axis, bit)
    stack = jnp.stack([parts[i] for i in range(len(parts))])
    return jnp.concatenate([pick(stack, i ^ me) for i in range(len(parts))], -1)


def sum_all(v, axis="narrow"):
    me = lax.axis_index(axis)
    bits = bits_of(axis)
    half = v.shape[0] // 2
    mine = me & 1
    low = v.astype(LOW)
    run = cut(low, mine * half, half, 0).astype(F32) + flip(
        cut(low, (1 - mine) * half, half, 0), axis, 1
    ).astype(F32)
    for bit in bits[1:]:
        low = run.astype(LOW)
        run = low.astype(F32) + flip(low, axis, bit).astype(F32)
    low = run.astype(LOW)
    other = flip(low, axis, 1)
    top = jnp.where(mine == 0, low, other)
    bottom = jnp.where(mine == 0, other, low)
    return jnp.concatenate([top, bottom], 0)


def scatter_cols(v, axis="narrow"):
    me = lax.axis_index(axis)
    size = lax.axis_size(axis)
    bits = bits_of(axis)
    width = v.shape[-1] // size
    low = v.astype(LOW)
    mine = me & 1

    def every_other(which):
        return jnp.concatenate(
            [cut(low, (2 * i + which) * width, width, 1) for i in range(size // 2)], 1
        )

    run = every_other(mine).astype(F32) + flip(every_other(1 - mine), axis, 1).astype(F32)
    for bit in reversed(bits[1:]):
        half = run.shape[1] // 2
        mine = (me // bit) & 1
        send = cut(run, (1 - mine) * half, half, 1).astype(LOW)
        run = cut(run, mine * half, half, 1) + flip(send, axis, bit).astype(F32)
    return run


def scatter_rows(v, axis="wide"):
    me = lax.axis_index(axis)
    size = lax.axis_size(axis)
    tail = v.shape[1:]
    run = v.astype(LOW).reshape((size, v.shape[0] // size) + tail)
    for bit in bits_of(axis):
        mine = (me // bit) & 1
        run = run.reshape((run.shape[0] // 2, 2) + run.shape[1:])
        send = pick(run, 1 - mine, 1).astype(LOW)
        run = pick(run, mine, 1).astype(F32) + flip(send, axis, bit).astype(F32)
    return run[0]


def sum_small(v, axes):
    for axis in axes:
        for bit in bits_of(axis):
            v = v + flip(v, axis, bit)
    return v


def window_mask(segments, block_start):
    places = jnp.arange(LEN, dtype=jnp.int32)
    query_pos = block_start + jnp.arange(CH, dtype=jnp.int32)
    query_seg = segments[block_start : block_start + CH]
    return (
        (places[None, :] <= query_pos[:, None])
        & (query_pos[:, None] - places[None, :] < WIN)
        & (segments[None, :] == query_seg[:, None])
    )


def body(
    tokens,
    gain_in,
    gain_mid,
    w_qkv,
    w_gate,
    w_decay,
    conv_kernel,
    persistent,
    w_out,
    mem_in,
    mem_out,
    w_up,
    w_down,
    doc_len,
    reset,
    cotangent,
):
    assert doc_len.shape[0] == 1
    width = w_qkv.shape[2]
    heads = width // HD
    ffn = w_up.shape[2]
    lead = lax.axis_index("narrow") * width
    score_scale = HD**0.5
    segment = segment_ids(doc_len[0])
    keep = 1.0 - reset.astype(F32)[0]
    gain_in_f = gain_in.astype(F32)
    gain_mid_f = gain_mid.astype(F32)
    mem_in_f = mem_in.astype(F32)
    mem_out_f = mem_out.astype(F32)
    inputs = tokens.astype(F32)
    inverse_in = lax.rsqrt(jnp.mean(inputs * inputs, -1, keepdims=True) + EPS)
    unit_in = inputs * inverse_in
    normed_in = (unit_in * gain_in_f).astype(LOW)
    w_qkv_t = w_qkv.transpose(1, 0, 2)
    projected = product("td,cdf->tcf", normed_in, w_qkv_t)

    def mixing(proj_in, kernel):
        return mix_inputs(proj_in, kernel, segment)

    mixed_act, mixing_back = jax.vjp(mixing, projected, conv_kernel.astype(F32))
    act_low = mixed_act.astype(LOW)
    query_loc, key_loc, value_loc = act_low[:, 0], act_low[:, 1], act_low[:, 2]
    key_value = gather_cols(jnp.stack([key_loc[:CH], value_loc[:CH]]))
    key_block, value_block = key_value[0], key_value[1]
    query_all = gather_cols(query_loc)
    cot_full = gather_cols(cotangent)
    mem_gates = jax.nn.sigmoid(product("td,dc->tc", normed_in, w_decay))
    decay_row = jnp.mean(mem_gates[:CH, 0])
    step_rate = jnp.mean(mem_gates[:CH, 1])
    gate_act = jax.nn.sigmoid(product("td,dh->th", normed_in, w_gate))
    gate_wide = jnp.repeat(gate_act, HD, axis=1)
    key_pre = product("cd,df->cf", key_block, mem_in)
    key_sig, key_slope = swish_parts(key_pre)
    key_hidden = (key_pre * key_sig).astype(LOW)
    predicted = sum_all(product("cf,fd->cd", key_hidden, mem_out)).astype(F32)
    first_pre = product("cd,df->cf", query_all[:CH], mem_in)
    first_sig, first_slope = swish_parts(first_pre)
    first_hidden = (first_pre * first_sig).astype(LOW)
    first_recall = product("cf,fd->cd", first_hidden, mem_out)
    query_h = query_loc.reshape(LEN, heads, HD)
    key_h = key_loc.reshape(LEN, heads, HD)
    value_h = value_loc.reshape(LEN, heads, HD)
    pers_keys = persistent[0].reshape(NP, heads, HD)
    pers_values = persistent[1].reshape(NP, heads, HD)

    def block_scores(start):
        query_blk = query_h[start : start + CH]
        allowed = window_mask(segment, start)[None]
        scores = jnp.where(allowed, score_scale * product("qhd,khd->hqk", query_blk, key_h), NEG)
        pers_scores = score_scale * product("qhd,khd->hqk", query_blk, pers_keys)
        return (query_blk, scores, pers_scores)

    peak_list = []
    normal_list = []
    mixed_list = []
    att_list = []
    for start in range(0, LEN, CH):
        query_blk, scores, pers_scores = block_scores(start)
        row_peak = jnp.maximum(jnp.max(scores, -1), jnp.max(pers_scores, -1))[..., None]
        weights = jnp.exp(scores - row_peak)
        pers_weights = jnp.exp(pers_scores - row_peak)
        normal = jnp.sum(weights, -1, keepdims=True) + jnp.sum(pers_weights, -1, keepdims=True)
        prob_low = (weights / normal).astype(LOW)
        pers_low = (pers_weights / normal).astype(LOW)
        att = product("hqk,khd->qhd", prob_low, value_h) + product(
            "hqk,khd->qhd", pers_low, pers_values
        )
        att = att.reshape(CH, width).astype(LOW)
        att_list.append(att)
        mixed_list.append(product("td,df->tf", att, w_out))
        peak_list.append(row_peak)
        normal_list.append(normal)
    attended = jnp.concatenate(att_list, 0)
    joined_first = sum_all(mixed_list[0] + gate_wide[:CH] * first_recall)
    error_low = (predicted - value_block.astype(F32)).astype(LOW)
    back_hidden = product("cd,fd->cf", error_low, mem_out)
    slope_low = (back_hidden * key_slope).astype(LOW)
    grad_in = product("cd,cf->df", key_block, slope_low) / CH
    grad_out = product("cf,cd->fd", key_hidden, error_low) / CH
    memory_in = mem_in_f - keep * (decay_row * mem_in_f + step_rate * STEP_IN * grad_in)
    memory_out = mem_out_f - keep * (decay_row * mem_out_f + step_rate * STEP_OUT * grad_out)
    memory_in_low = memory_in.astype(LOW)
    memory_out_low = memory_out.astype(LOW)
    second_pre = product("cd,df->cf", query_all[CH:], memory_in_low)
    second_sig, second_slope = swish_parts(second_pre)
    second_hidden = (second_pre * second_sig).astype(LOW)
    second_recall = product("cf,fd->cd", second_hidden, memory_out_low)
    joined_second = sum_all(mixed_list[1] + gate_wide[CH:] * second_recall)

    w_gate_up = w_up.transpose(1, 0, 2)

    def feed(part, joined):
        rows = slice(part * CH, part * CH + CH)
        middle = inputs[rows] + joined.astype(F32)
        inverse = lax.rsqrt(jnp.mean(middle * middle, -1, keepdims=True) + EPS)
        unit = middle * inverse
        normed = (unit * gain_mid_f).astype(LOW)
        gate_val = product("td,df->tf", normed, w_gate_up[0])
        up_val = product("td,df->tf", normed, w_gate_up[1])
        sig = jax.nn.sigmoid(gate_val)
        hidden = (gate_val * sig * up_val).astype(LOW)
        ffn_out = scatter_cols(product("tf,fd->td", hidden, w_down))
        output = (cut(middle, lead, width, 1) + ffn_out).astype(LOW)
        cot = cot_full[rows]
        grad_hidden = product("td,fd->tf", cot, w_down)
        grad_gate = (grad_hidden * up_val * sig * (1.0 + gate_val * (1.0 - sig))).astype(LOW)
        grad_up = (grad_hidden * gate_val * sig).astype(LOW)
        grad_norm = product("tf,df->td", grad_gate, w_gate_up[0]) + product(
            "tf,df->td", grad_up, w_gate_up[1]
        )
        gain_part = jnp.sum(grad_norm * unit, 0)
        summed = sum_all(norm_back(grad_norm, unit, inverse, gain_mid_f))
        grad_middle = summed.astype(F32) + cot.astype(F32)
        return output, normed, hidden, grad_gate, grad_up, gain_part, grad_middle

    out_a, norm_a, hid_a, gg_a, gu_a, gain_a, grad_mid_a = feed(0, joined_first)
    out_b, norm_b, hid_b, gg_b, gu_b, gain_b, grad_mid_b = feed(1, joined_second)
    output = jnp.concatenate([out_a, out_b], 0)
    gain_mid_part = gain_a + gain_b
    normed_mid = jnp.concatenate([norm_a, norm_b], 0)
    hidden = jnp.concatenate([hid_a, hid_b], 0)
    grad_down = scatter_rows(product("td,tf->df", cot_full, hidden))
    grad_up_gate = scatter_rows(
        product("td,tf->df", normed_mid, jnp.concatenate([gg_a, gg_b], 0))
    )
    grad_up_up = scatter_rows(product("td,tf->df", normed_mid, jnp.concatenate([gu_a, gu_b], 0)))
    grad_middle = jnp.concatenate([grad_mid_a, grad_mid_b], 0)

    def gate_terms(recall, grad_mid, gates):
        terms = jnp.sum((recall * grad_mid).reshape(CH, HEADS, HD), -1)
        return terms * gates * (1.0 - gates)

    second_grad = (gate_wide[CH:] * grad_mid_b).astype(LOW)
    grad_memory_out = product("cf,cd->fd", second_hidden, second_grad)
    grad_second_pre = (product("cd,fd->cf", second_grad, memory_out_low) * second_slope).astype(LOW)
    grad_memory_in = product("cd,cf->df", query_all[CH:], grad_second_pre)
    grad_query_second = product("cf,df->cd", grad_second_pre, memory_in_low)
    factor = -(keep * step_rate)
    grad_gin = (factor * STEP_IN * grad_memory_in).astype(LOW)
    grad_gout = (factor * STEP_OUT * grad_memory_out).astype(LOW)
    grad_slope = product("cd,df->cf", key_block, grad_gin) / CH
    grad_error = product("cf,fd->cd", key_hidden, grad_gout) / CH
    grad_back_low = (grad_slope * key_slope).astype(LOW)
    grad_error = grad_error + product("cf,fd->cd", grad_back_low, mem_out)
    grad_pred_low = sum_all(grad_error)
    grad_key_block = product("cf,df->cd", slope_low, grad_gin) / CH
    grad_key_hidden = product("cd,fd->cf", error_low, grad_gout) / CH
    first_grad = (gate_wide[:CH] * grad_mid_a).astype(LOW)
    grad_mem_out = product("cf,cd->fd", first_hidden, first_grad)
    grad_first_pre = (product("cd,fd->cf", first_grad, mem_out) * first_slope).astype(LOW)
    grad_mem_in = product("cd,cf->df", query_all[:CH], grad_first_pre)
    grad_query_first = product("cf,df->cd", grad_first_pre, mem_in)
    query_share = scatter_cols(jnp.concatenate([grad_query_first, grad_query_second], 0))
    grad_head_gate = jnp.concatenate(
        [
            gate_terms(first_recall, grad_mid_a, gate_act[:CH]),
            gate_terms(second_recall, grad_mid_b, gate_act[CH:]),
        ],
        0,
    )
    head_gate_low = grad_head_gate.astype(LOW)
    grad_gate_w = product("td,th->hd", normed_in, head_gate_low)
    grad_mixed_low = grad_middle.astype(LOW)
    grad_out_w = scatter_rows(product("td,tf->df", grad_mixed_low, attended))
    grad_att = product("td,fd->tf", grad_mixed_low, w_out).astype(LOW).reshape(LEN, heads, HD)
    grad_query_list = []
    grad_key_att = 0.0
    grad_value_att = 0.0
    grad_pers_key = 0.0
    grad_pers_value = 0.0
    for index, start in enumerate(range(0, LEN, CH)):
        query_blk, scores, pers_scores = block_scores(start)
        prob_full = jnp.exp(scores - peak_list[index]) / normal_list[index]
        pers_probs = jnp.exp(pers_scores - peak_list[index]) / normal_list[index]
        grad_blk = grad_att[start : start + CH]
        grad_probs = product("qhd,khd->hqk", grad_blk, value_h)
        grad_pers_probs = product("qhd,khd->hqk", grad_blk, pers_values)
        center = jnp.sum(prob_full * grad_probs, -1, keepdims=True) + jnp.sum(
            pers_probs * grad_pers_probs, -1, keepdims=True
        )
        grad_scores = (prob_full * (grad_probs - center)).astype(LOW)
        grad_pers_scores = (pers_probs * (grad_pers_probs - center)).astype(LOW)
        grad_query_list.append(
            score_scale
            * (
                product("hqk,khd->qhd", grad_scores, key_h)
                + product("hqk,khd->qhd", grad_pers_scores, pers_keys)
            )
        )
        grad_key_att = grad_key_att + score_scale * product("hqk,qhd->khd", grad_scores, query_blk)
        grad_value_att = grad_value_att + product("hqk,qhd->khd", prob_full.astype(LOW), grad_blk)
        grad_pers_key = grad_pers_key + score_scale * product(
            "hqk,qhd->khd", grad_pers_scores, query_blk
        )
        grad_pers_value = grad_pers_value + product("hqk,qhd->khd", pers_probs.astype(LOW), grad_blk)
    grad_query_att = jnp.concatenate(grad_query_list, 0).reshape(LEN, width)
    grad_key_att = grad_key_att.reshape(LEN, width)
    grad_value_att = grad_value_att.reshape(LEN, width)
    grad_pred = grad_pred_low.astype(F32)
    grad_key_hidden = grad_key_hidden + product("cd,fd->cf", grad_pred_low, mem_out)
    key_curve = key_sig * (1.0 - key_sig) * (2.0 + key_pre * (1.0 - 2.0 * key_sig))
    grad_key_pre = (grad_key_hidden * key_slope + grad_slope * back_hidden * key_curve).astype(LOW)
    grad_key_block = grad_key_block + product("cf,df->cd", grad_key_pre, mem_in)
    key_share = scatter_cols(grad_key_block)
    retain = 1.0 - keep * decay_row
    grad_mem_in = (
        grad_mem_in + retain * grad_memory_in + product("cd,cf->df", key_block, grad_key_pre)
    )
    grad_mem_out = (
        grad_mem_out
        + retain * grad_memory_out
        + product("cf,cd->fd", grad_back_low, error_low)
        + product("cf,cd->fd", key_hidden, grad_pred_low)
    )
    in_shard = scatter_rows(grad_mem_in)
    back_shard = scatter_rows(grad_mem_out.T)
    decay_part = -keep * (jnp.sum(mem_in_f * grad_memory_in) + jnp.sum(mem_out_f * grad_memory_out))
    step_part = -keep * (
        STEP_IN * jnp.sum(grad_in * grad_memory_in) + STEP_OUT * jnp.sum(grad_out * grad_memory_out)
    )
    value_share = -cut(grad_pred, lead, width, 1)
    tail_zeros = jnp.zeros((LEN - CH, width), F32)
    grad_act = jnp.stack(
        [
            grad_query_att + query_share,
            grad_key_att + jnp.concatenate([key_share, tail_zeros], 0),
            grad_value_att + jnp.concatenate([value_share, tail_zeros], 0),
        ],
        1,
    )
    grad_proj, grad_conv = mixing_back(grad_act)
    grad_proj_low = grad_proj.astype(LOW)
    grad_norm_part = product("tcf,cdf->td", grad_proj_low, w_qkv_t) + product(
        "th,dh->td", head_gate_low, w_gate
    )
    gate_slopes = mem_gates * (1.0 - mem_gates)
    in_first = (jnp.arange(LEN) < CH).astype(F32) / CH
    step_logit = step_part * gate_slopes[:, 1] * in_first
    decay_logit = decay_part * gate_slopes[:, 0] * in_first
    decay_w = w_decay.astype(F32)
    grad_norm_part = (
        grad_norm_part
        + step_logit[:, None] * decay_w[:, 1][None]
        + decay_logit[:, None] * decay_w[:, 0][None]
    )
    normed_f = normed_in.astype(F32)
    step_w = jnp.sum(normed_f * step_logit[:, None], 0)
    decay_w_part = jnp.sum(normed_f * decay_logit[:, None], 0)
    gain_in_part = jnp.sum(grad_norm_part * unit_in, 0)
    input_share = scatter_cols(norm_back(grad_norm_part, unit_in, inverse_in, gain_in_f))
    grad_input = input_share + cut(grad_middle, lead, width, 1)
    grad_qkv_w = [
        scatter_rows(product("td,tf->df", normed_in, grad_proj_low[:, i])) for i in range(3)
    ]
    pers_part = jnp.concatenate(
        [grad_pers_key.reshape(NP, width), grad_pers_value.reshape(NP, width)], 0
    )
    own_part = jnp.concatenate([grad_conv.reshape(3 * KC, width), pers_part], 0)
    own_all = gather_cols(sum_small(own_part, ("wide",)))
    vec_part = jnp.concatenate(
        [jnp.stack([gain_in_part, gain_mid_part, decay_w_part, step_w]), grad_gate_w], 0
    )
    vec_all = sum_small(vec_part, ("narrow", "wide"))
    conv_sum = own_all[: 3 * KC].reshape(3, KC, D)
    pers_sum = own_all[3 * KC :].reshape(2, NP, D)
    gate_rows = D // lax.axis_size("wide")
    gate_shard = cut(vec_all[4:], lax.axis_index("wide") * gate_rows, gate_rows, 1).T
    return (
        output,
        grad_input,
        vec_all[0],
        vec_all[1],
        jnp.stack(grad_qkv_w, 1),
        gate_shard,
        vec_all[2:4].T,
        conv_sum,
        pers_sum,
        grad_out_w.T,
        in_shard,
        back_shard.T,
        jnp.stack([grad_up_gate, grad_up_up], 1),
        grad_down.T,
    )


def solution(mesh):
    in_specs = (
        P("wide", None),
        P(),
        P(),
        P(None, None, "narrow"),
        P(),
        P(),
        P(None, None, "narrow"),
        P(None, None, "narrow"),
        P("narrow", None),
        P(None, "narrow"),
        P("narrow", None),
        P(None, None, "narrow"),
        P("narrow", None),
        P("wide", None),
        P("wide"),
        P("wide", "narrow"),
    )
    out_specs = (
        P("wide", "narrow"),
        P("wide", "narrow"),
        P(),
        P(),
        P("wide", None, "narrow"),
        P("wide", None),
        P(),
        P(),
        P(),
        P("narrow", "wide"),
        P("wide", "narrow"),
        P("narrow", "wide"),
        P("wide", None, "narrow"),
        P("narrow", "wide"),
    )
    return jax.shard_map(body, mesh=mesh, in_specs=in_specs, out_specs=out_specs, check_vma=False)
```

```python
import jax
import jax.numpy as jnp
from jax import lax
from jax.experimental import pallas as pl
from jax.experimental.pallas import tpu as pltpu
from jax.sharding import PartitionSpec as P

D = 1024
HEADS = 16
HD = 64
LEN = 1024
CH = 512
WIN = 512
NP = 16
KC = 4


EPS = 1e-06
NEG = -1e30
STEP_IN = 128.0
STEP_OUT = 0.5
LOW = jnp.bfloat16
F32 = jnp.float32
VMEM = 12
VMEM_OF = {'pre': 16, 'mem1': 12, 'recall1': 15, 'mem2': 24, 'feed0': 28, 'feed1': 28, 'mem2_back': 32, 'recall1_back': 20, 'mem2_late': 15, 'mem1_back': 12, 'attend_back': 12}


def norm_back(grad_norm, unit_val, inverse, gain_vec):
    scaled = grad_norm * gain_vec
    return inverse * (scaled - unit_val * jnp.mean(scaled * unit_val, -1, keepdims=True))


def flip(v, axis, bit):
    size = lax.axis_size(axis)
    return lax.ppermute(v, axis, [(i, i ^ bit) for i in range(size)])


def bits_of(axis):
    size = lax.axis_size(axis)
    out = []
    bit = 1
    while bit < size:
        out.append(bit)
        bit *= 2
    assert bit == size
    return out


def pick(v, index, axis=0):
    return lax.dynamic_index_in_dim(v, index, axis, keepdims=False)


def cut(v, start, width, axis):
    return lax.dynamic_slice_in_dim(v, start, width, axis)


class Parts:
    def __init__(self, v):
        self.own, self.far, self.near = v, flip(v, "narrow", 2), flip(v, "narrow", 1)

    def end(self):
        far = tie(self.far)
        self.terms = [self.own, tie(self.near), far, flip(far, "narrow", 1)]
        return self.terms

    def settle(self):
        self.terms[3] = tie(self.terms[3])
        return self.terms


class Halves:
    def __init__(self, keep, send):
        self.keep, self.come = keep, flip(send, "narrow", 1)

    def middle(self):
        self.run = fold(self.keep, self.come, LOW)
        self.far = flip(self.run, "narrow", 2)
        self.near = flip(self.run, "narrow", 1)

    def end(self):
        far = tie(self.far)
        self.terms = [self.run, far, tie(self.near), flip(far, "narrow", 1)]
        return self.terms

    def settle(self):
        self.terms[3] = tie(self.terms[3])
        return self.terms


class Columns:
    def __init__(self, keep, *sends):
        self.keep, self.come = keep, [flip(send, "narrow", 1) for send in sends]

    def middle(self):
        self.run, away = fold_columns(self.keep, self.come)
        self.far = flip(away, "narrow", 2)

    def end(self):
        return [self.run[0], tie(self.far)[0]]


class Rows:
    def __init__(self, first, keep, send):
        self.keep, self.come = keep, flip(send, "wide", first)
        self.bits = [b for b in bits_of("wide") if b != first]

    def step(self):
        bit = self.bits.pop(0)
        self.keep, away = fold_pick(lambda: wide_bit(bit.bit_length() - 1), self.keep, self.come)
        self.come = flip(away, "wide", bit)

    def end(self):
        while self.bits:
            self.step()
        return fold(self.keep, self.come, F32)[0]


def place_own(v, rows, width, me):
    own = v[: rows * width // D].reshape(rows, width)
    own = lax.dynamic_update_slice(jnp.zeros((rows, D), F32), own, (0, me * width))
    return jnp.concatenate([own, v[rows * width // D :]], 0)


class Small:
    def __init__(self, v, axis):
        self.v = pinned(v)
        self.left = [(axis, b) for b in bits_of(axis)]
        self.send()

    def send(self):
        if self.left:
            self.come = flip(self.v, *self.left.pop(0))

    def step(self):
        self.v = pinned(self.v + tie(self.come))
        self.send()

    def end(self):
        while self.left:
            self.step()
        return self.v + tie(self.come)


def head_sum(v, ones_mat):
    high = v.astype(LOW)
    rest = (v - high.astype(F32)).astype(LOW)
    return jnp.dot(high, ones_mat, preferred_element_type=F32) + jnp.dot(
        rest, ones_mat, preferred_element_type=F32
    )


def same_head(width):
    row = lax.broadcasted_iota(jnp.int32, (width, width), 0) // HD
    col = lax.broadcasted_iota(jnp.int32, (width, width), 1) // HD
    return (row == col).astype(F32).astype(LOW)


def doc_start(doc_ref, places):
    start = jnp.zeros_like(places)
    end = 0
    for i in range(doc_ref.shape[1]):
        end = end + doc_ref[0, i]
        start = jnp.where(places >= end, end, start)
    return start


def conv_sum(pad_ref, taps_ref, age, first, rows):
    total = taps_ref[0, 0:1, :].astype(F32) * pad_ref[pl.ds(first + 8, rows), :]
    for i in range(1, KC):
        shifted = pad_ref[pl.ds(first + 8 - i, rows), :]
        total = total + taps_ref[0, i : i + 1, :].astype(F32) * jnp.where(age >= i, shifted, 0.0)
    return total


def ages(doc_ref, first, rows, width):
    places = first + lax.broadcasted_iota(jnp.int32, (rows, 128), 0)
    age = places - doc_start(doc_ref, places)
    return jnp.concatenate([age] * (width // 128), 1)


PRE_ROWS = 256


def pre_kernel(doc_ref, x_ref, gain_ref, w_ref, gate_ref, decay_ref, taps_ref, n_ref, gates_ref, rates_ref, p_ref, act_ref, q_ref, head_ref, pad):
    part = pl.program_id(0)
    width = w_ref.shape[2]

    @pl.when(part == 0)
    def _():
        pad[pl.ds(0, 8), :] = jnp.zeros((8, width), F32)
        total = jnp.zeros((1, 128), F32)
        for first in range(0, LEN, PRE_ROWS):
            rows = pl.ds(first, PRE_ROWS)
            x = x_ref[rows, :].astype(F32)
            inverse = lax.rsqrt(jnp.mean(x * x, -1, keepdims=True) + EPS)
            normed = (x * inverse * gain_row(gain_ref)).astype(LOW)
            n_ref[rows, :] = normed
            logits = [dot_nt(normed, gate_ref[...]), dot_nt(normed, decay_ref[...])]
            logits.append(jnp.zeros((PRE_ROWS, 128 - HEADS - 2), F32))
            gates = jax.nn.sigmoid(jnp.concatenate(logits, 1))
            gates_ref[rows, :] = gates
            if first < CH:
                total = total + jnp.sum(gates, 0, keepdims=True)
        rates_ref[...] = total * (1.0 / CH)

    for first in range(0, LEN, PRE_ROWS):
        rows = pl.ds(first, PRE_ROWS)
        p = jnp.dot(n_ref[rows, :], w_ref[0], preferred_element_type=F32)
        p_ref[0, rows, :] = p
        pad[pl.ds(first + 8, PRE_ROWS), :] = p
        age = ages(doc_ref, first, PRE_ROWS, width)
        c = conv_sum(pad, taps_ref, age, first, PRE_ROWS)
        a = c * jax.nn.sigmoid(c)

        @pl.when(part < 2)
        def _():
            out = a * lax.rsqrt(head_sum(a * a, same_head(width)) + EPS)
            act_ref[0, rows, :] = out.astype(LOW)

        @pl.when(part == 2)
        def _():
            act_ref[0, rows, :] = a.astype(LOW)

    head_ref[0] = act_ref[0, :CH, :]

    @pl.when(part == 0)
    def _():
        q_ref[...] = act_ref[0, CH:, :]


def pre(doc_len, tokens, gain, w_t, gate_t, decay_t, taps):
    width = w_t.shape[2]
    part = pl.BlockSpec((1, LEN, width), lambda i: (i, 0, 0))
    return run(
        "pre", pre_kernel, 3,
        [(doc_len, SMEM_SPEC), full(tokens), full(gain), (w_t, pl.BlockSpec((1, D, width), lambda i: (i, 0, 0))),
         full(gate_t), full(decay_t), (taps, pl.BlockSpec((1, KC, width), lambda i: (i, 0, 0)))],
        [far(out_full((LEN, D), LOW)), far(out_full((LEN, 128), F32)), far(out_full((1, 128), F32)),
         far(((3, LEN, width), F32, part)), far(((3, LEN, width), LOW, part)), out_full((CH, width), LOW),
         ((3, CH, width), LOW, pl.BlockSpec((1, CH, width), lambda i: (i, 0, 0)))],
        [pltpu.VMEM((LEN + 8, width), F32)], 13.0,
    )


def fetch_kernel(a, b, c, to_a, to_b, to_c):
    to_a[...] = a[...]
    to_b[...] = b[...]
    to_c[...] = c[...]


def fetch(mem_in, mem_out, w_down):
    arrays = [mem_in, mem_out, w_down]
    return run(
        "fetch", fetch_kernel, 4, [rows_of(a, a.shape[0] // 4) for a in arrays],
        [near((a.shape, LOW, pl.BlockSpec((a.shape[0] // 4, a.shape[1]), lambda i: (i, 0)))) for a in arrays], (), 2.0,
    )


QB = 256


def key_range(block):
    return max(0, (block - 2) * QB), (block + 1) * QB


def allowed(doc_ref, block, low_key, high_key):
    query = block * QB + lax.broadcasted_iota(jnp.int32, (8, QB), 1)
    low = jnp.maximum(doc_start(doc_ref, query), query - (WIN - 1))[0:1]
    key = low_key + lax.broadcasted_iota(jnp.int32, (high_key - low_key, QB), 0)
    return (key >= low) & (key <= query[0:1])


def scaled_head(q, index):
    lane = lax.broadcasted_iota(jnp.int32, q.shape, 1)
    return jnp.where(lane // HD == index, q * 8.0, 0.0).astype(LOW)


def one_head(v, index):
    lane = lax.broadcasted_iota(jnp.int32, v.shape, 1)
    return jnp.where(lane // HD == index, v, 0.0).astype(LOW)


def dot_nt(a, b):
    return lax.dot_general(a, b, (((1,), (1,)), ((), ())), preferred_element_type=F32)


def dot_nn(a, b):
    return jnp.dot(a, b, preferred_element_type=F32)


def dot_tn(a, b):
    return lax.dot_general(a, b, (((0,), (0,)), ((), ())), preferred_element_type=F32)


def flat(v):
    return v.astype(F32).T.astype(v.dtype)


def attend_kernel(doc_ref, q_ref, k_ref, v_ref, pk_ref, pv_ref, out_ref, peak_ref, inv_ref):
    k = k_ref[0]
    values_t = flat(v_ref[0])
    pk = pk_ref[0]
    pv_t = flat(pv_ref[0])
    for block in range(LEN // QB):
        low_key, high_key = key_range(block)
        ok = allowed(doc_ref, block, low_key, high_key)
        q = q_ref[0, pl.ds(block * QB, QB), :].astype(F32)
        outs = []
        for index in range(2):
            q_head = scaled_head(q, index)
            s = jnp.where(ok, dot_nt(k[low_key:high_key], q_head), NEG)
            sp = dot_nt(pk, q_head)
            peak = jnp.maximum(jnp.max(s, 0, keepdims=True), jnp.max(sp, 0, keepdims=True))
            e = jnp.exp(s - peak)
            ep = jnp.exp(sp - peak)
            inv = 1.0 / (jnp.sum(e, 0, keepdims=True) + jnp.sum(ep, 0, keepdims=True))
            feats = slice(index * HD, index * HD + HD)
            out = dot_nn(values_t[feats, low_key:high_key], e.astype(LOW)) + dot_nn(
                pv_t[feats], ep.astype(LOW)
            )
            outs.append(out * inv)
            peak_ref[0, index : index + 1, pl.ds(block * QB, QB)] = peak
            inv_ref[0, index : index + 1, pl.ds(block * QB, QB)] = inv
        out_ref[pl.ds(block * QB, QB), :] = jnp.concatenate(outs, 0).T.astype(LOW)


def attend(doc_len, act, persistent):
    width = act.shape[2]
    pairs = width // 128
    smem = pl.BlockSpec(memory_space=pltpu.SMEM)

    def part(i):
        return pl.BlockSpec((1, LEN, 128), lambda g: (i, 0, g))

    def pers(i):
        return pl.BlockSpec((1, NP, 128), lambda g: (i, 0, g))

    stat = pl.BlockSpec((1, 2, LEN), lambda g: (g, 0, 0))
    arrays = [doc_len, act, act, act, persistent, persistent]
    specs = [smem, part(0), part(1), part(2), pers(0), pers(1)]
    return run(
        "attend", attend_kernel, pairs, list(zip(arrays, specs)),
        [far(((LEN, width), LOW, pl.BlockSpec((LEN, 128), lambda g: (0, g)))), far(((pairs, 2, LEN), F32, stat)),
         far(((pairs, 2, LEN), F32, stat))],
        (), 9.3,
    )


SMEM_SPEC = pl.BlockSpec(memory_space=pltpu.SMEM)
STEPS = 2


def whole(shape):
    zeros = (0,) * len(shape)
    return pl.BlockSpec(tuple(shape), lambda *_: zeros, pipeline_mode=pl.Buffered(1))


LAST = []
PLACED = []


def placed(a):
    for other, space in PLACED:
        if other is a:
            return pltpu.with_memory_space_constraint(a, space)
    return a


def put(a, space):
    PLACED.append((a, space))
    return a


def chained(arrays, specs):
    arrays = [placed(a) for a in arrays]
    if LAST:
        return arrays + [placed(LAST[0])], specs + [pl.BlockSpec(memory_space=pl.ANY)]
    return arrays, specs


def remember(outs):
    LAST[:] = [min(outs, key=lambda o: o.size * o.dtype.itemsize)]
    return outs


def near(out):
    return (*out, pltpu.VMEM)


def far(out):
    return (*out, pltpu.HBM)


def shape_of(out):
    shape, kind = tuple(out[0]), out[1]
    return out[3](shape, kind) if len(out) > 3 else jax.ShapeDtypeStruct(shape, kind)


def run(name, kernel, steps, ins, outs, scratch=(), micros=0.0, held=(), aliases=(), room=0):
    used = len(ins)
    arrays = [a for a, _ in ins] + list(held)
    specs = [s for _, s in ins] + [pl.BlockSpec(memory_space=pl.ANY)] * len(held)
    arrays, specs = chained(arrays, specs)
    count = len(arrays)

    def inner(*refs):
        kernel(*refs[:used], *refs[count:])

    results = pl.pallas_call(
        inner,
        grid=(steps,),
        in_specs=specs,
        out_specs=[out[2] for out in outs],
        out_shape=[shape_of(out) for out in outs],
        scratch_shapes=list(scratch),
        input_output_aliases={used + k: v for k, v in dict(aliases).items()},
        compiler_params=pltpu.CompilerParams(vmem_limit_bytes=(VMEM_OF.get(name, VMEM) + room) << 20),
        cost_estimate=pl.CostEstimate(flops=1, bytes_accessed=1, transcendentals=0),
        name=name,
    )(*arrays)
    for result, out in zip(results, outs):
        if len(out) > 3:
            put(result, out[3])
    return remember(results)


def tie(v):
    space = next((space for other, space in PLACED if other is LAST[0]), None)
    v, LAST[0] = lax.optimization_barrier((v, LAST[0]))
    if space is not None:
        put(LAST[0], space)
    return v


def pinned(v):
    v = tie(v)
    LAST[:] = [v]
    return v


def fold_kernel(a, b, out):
    out[...] = (a[...].astype(F32) + b[...].astype(F32)).astype(out.dtype)


def fold(a, b, kind):
    zeros = (0,) * a.ndim
    spec = pl.BlockSpec(a.shape, lambda i: zeros)
    return run("fold", fold_kernel, 1, [(a, spec), (b, spec)], [far((a.shape, kind, spec)) if kind == F32 else (a.shape, kind, spec)])[0]


def fold_columns(keep, come):
    count = len(come)
    _, rows, width = keep.shape
    part = rows // count

    def kernel(keep_ref, *refs):
        chip = lax.axis_index("narrow") >> 1
        run_ref, away_ref = refs[count:]
        for i in range(count):
            at = pl.ds(i * part, part)
            run_ref[0, at, :] = (keep_ref[chip, at, :].astype(F32) + refs[i][chip].astype(F32)).astype(LOW)
            away_ref[0, at, :] = (keep_ref[1 - chip, at, :].astype(F32) + refs[i][1 - chip].astype(F32)).astype(LOW)

    one = out_full((1, rows, width), LOW)
    return run("fold_columns", kernel, 1, [full(keep)] + [full(c) for c in come], [one, one], (), 1.5)


def fold_pick(bit_of, a, b):
    pairs = a.shape[0] // 2
    tail = a.shape[1:]
    zeros = (0,) * len(tail)
    two = pl.BlockSpec((2,) + tail, lambda i: (i,) + zeros)
    one = ((pairs,) + tail, LOW, pl.BlockSpec((1,) + tail, lambda i: (i,) + zeros))

    def kernel(a_ref, b_ref, keep, send):
        bit = bit_of()
        keep[0] = (a_ref[bit].astype(F32) + b_ref[bit].astype(F32)).astype(LOW)
        send[0] = (a_ref[1 - bit].astype(F32) + b_ref[1 - bit].astype(F32)).astype(LOW)

    return run("fold_pick", kernel, pairs, [(a, two), (b, two)], [one, one], (), 1.5)


def full(a):
    return (a, whole(a.shape))


def out_full(shape, kind):
    return (shape, kind, whole(shape))


def cols_of(a, chunk):
    return (a, pl.BlockSpec((a.shape[0], chunk), lambda i: (0, i)))


def rows_of(a, chunk):
    return (a, pl.BlockSpec((chunk, a.shape[1]), lambda i: (i, 0)))


def half_of(a, half):
    return (a, pl.BlockSpec((CH, a.shape[1]), lambda i: (half, 0)))


def out_cols(rows, cols, kind, chunk):
    return ((rows, cols), kind, pl.BlockSpec((rows, chunk), lambda i: (0, i)))


def rates_of(reset, rates):
    kept = 1.0 - reset[0].astype(F32)
    return kept, rates[0:1, HEADS : HEADS + 1], rates[0:1, HEADS + 1 : HEADS + 2]


def my_place():
    me = lax.axis_index("narrow")
    return me, me & 1


def wide_bit(place):
    return (lax.axis_index("wide") >> place) & 1


def span(index, width):
    return pl.ds(pl.multiple_of(index * width, width), width)


def gain_row(ref):
    g = ref[...].astype(F32)
    return jnp.concatenate([g[i : i + 1] for i in range(g.shape[0])], 1)


def silu_slope(pre, sig):
    return sig * (1.0 + pre * (1.0 - sig))


def head_columns():
    head = lax.broadcasted_iota(jnp.int32, (128, D), 0)
    feat = lax.broadcasted_iota(jnp.int32, (128, D), 1) // HD
    return (head == feat).astype(F32).astype(LOW)


def two_terms(v):
    high = v.astype(LOW)
    return high, (v - high.astype(F32)).astype(LOW)


def widen(gates, columns):
    high, rest = two_terms(gates)
    return dot_nn(high, columns) + dot_nn(rest, columns)


def narrow_heads(v, columns):
    high, rest = two_terms(v)
    return dot_nt(high, columns) + dot_nt(rest, columns)


def halves(terms, core):
    run_ref, far, near, near_far = terms
    for a, b, which in ((run_ref, far, core), (near, near_far, 1 - core)):
        yield span(which, CH // 2), a[...].astype(F32) + b[...].astype(F32)


def put_halves(keep, send, v_ref, core):
    rows = CH // 2
    keep[...] = v_ref[span(core, rows), :].astype(LOW)
    send[...] = v_ref[span(1 - core, rows), :].astype(LOW)


def put_columns(keep, send, v_ref, core, width, rows=None):
    for i in range(2):
        own = v_ref[:, span(2 * i + core, width)].astype(LOW)
        other = v_ref[:, span(2 * i + 1 - core, width)].astype(LOW)
        if rows is None:
            keep[i] = own
            send[i] = other
        else:
            keep[i, rows, :] = own
            send[i, rows, :] = other


def add_to(acc, first, v):
    @pl.when(first)
    def _():
        acc[...] = v

    @pl.when(jnp.logical_not(first))
    def _():
        acc[...] += v


def halves_out():
    return [out_full((CH // 2, D), LOW), out_full((CH // 2, D), LOW)]


def scratch_half():
    return pltpu.VMEM((CH, D), F32)


def mem1_kernel(kv0, kv1, kv2, kv3, w_in, w_out, q, kc, vc, hk, ks, kcv, keep, send, acc):
    step = pl.program_id(0)
    me, core = my_place()
    width = kv0.shape[2]

    @pl.when(step == 0)
    def _():
        for r, part in enumerate((kv0, kv1, kv2, kv3)):
            cols = span(me ^ r, width)
            q[:, cols] = part[0]
            kc[:, cols] = part[1]
            vc[:, cols] = part[2]

    pre = dot_nn(kc[...], w_in[...])
    sig = jax.nn.sigmoid(pre)
    hidden = (pre * sig).astype(LOW)
    hk[...] = hidden
    ks[...] = silu_slope(pre, sig).astype(LOW)
    kcv[...] = (sig * (1.0 - sig) * (2.0 + pre * (1.0 - 2.0 * sig))).astype(LOW)
    add_to(acc, step == 0, dot_nn(hidden, w_out[...]))

    @pl.when(step == STEPS - 1)
    def _():
        put_halves(keep, send, acc, core)


def mem1(parts, mem_in, mem_out):
    units = mem_in.shape[1]
    chunk = units // STEPS
    return run(
        "mem1", mem1_kernel, STEPS,
        [] + [full(p) for p in parts] + [cols_of(mem_in, chunk), rows_of(mem_out, chunk)],
        [near(out_full((CH, D), LOW)) for _ in range(3)]
        + [near(out_cols(CH, units, LOW, chunk)) for _ in range(3)] + halves_out(),
        [scratch_half()], 8.4,
    )


def recall1_kernel(q, gates, att, w_o, w_in, w_out, hid, slope, rec, keep, send, acc):
    step = pl.program_id(0)
    core = my_place()[1]
    pre = dot_nn(q[...], w_in[...])
    sig = jax.nn.sigmoid(pre)
    hidden = (pre * sig).astype(LOW)
    hid[...] = hidden
    slope[...] = silu_slope(pre, sig).astype(LOW)
    add_to(acc, step == 0, dot_nn(hidden, w_out[...]))

    @pl.when(step == STEPS - 1)
    def _():
        rec[...] = acc[...].astype(LOW)
        acc[...] = acc[...] * widen(gates[...], head_columns()) + dot_nn(att[...], w_o[...])
        put_halves(keep, send, acc, core)


def recall1(q, gates, attended, w_o, mem_in, mem_out):
    units = mem_in.shape[1]
    chunk = units // STEPS
    return run(
        "recall1", recall1_kernel, STEPS,
        [] + [full(q), half_of(gates, 0), half_of(attended, 0), full(w_o), cols_of(mem_in, chunk), rows_of(mem_out, chunk)],
        [far(out_cols(CH, units, LOW, chunk)), far(out_cols(CH, units, LOW, chunk)),
         far(out_full((CH, D), LOW))]
        + halves_out(),
        [scratch_half()], 9.6,
    )


def mem2_kernel(
    reset, rates, s0, s1, s2, s3, q0, q1, q2, q3, vc, kc, hk, ks, kcv, gates, att, w_o, w_in, w_out,
    q, err, slope_low, bcurve, m_in, m_out, hid, slope, rec, keep, send, acc,
):
    step = pl.program_id(0)
    me, core = my_place()
    kept, decay, rate = rates_of(reset, rates)

    @pl.when(step == 0)
    def _():
        for r, part in enumerate((q0, q1, q2, q3)):
            q[:, span(me ^ r, part.shape[1])] = part[...]
        for rows, total in halves((s0, s1, s2, s3), core):
            err[rows, :] = (total - vc[rows, :].astype(F32)).astype(LOW)

    back = dot_nt(err[...], w_out[...])
    slopes = (back * ks[...].astype(F32)).astype(LOW)
    slope_low[...] = slopes
    bcurve[...] = (back * kcv[...].astype(F32)).astype(LOW)
    retain = 1.0 - kept * decay
    take_in = kept * rate * (STEP_IN / CH)
    take_out = kept * rate * (STEP_OUT / CH)
    now_in = (w_in[...].astype(F32) * retain - take_in * dot_tn(kc[...], slopes)).astype(LOW)
    m_in[...] = now_in
    pre = dot_nn(q[...], now_in)
    sig = jax.nn.sigmoid(pre)
    hidden = (pre * sig).astype(LOW)
    hid[...] = hidden
    slope[...] = silu_slope(pre, sig).astype(LOW)
    now_out = (w_out[...].astype(F32) * retain - take_out * dot_tn(hk[...], err[...])).astype(LOW)
    m_out[...] = now_out
    add_to(acc, step == 0, dot_nn(hidden, now_out))

    @pl.when(step == STEPS - 1)
    def _():
        rec[...] = acc[...].astype(LOW)
        acc[...] = acc[...] * widen(gates[...], head_columns()) + dot_nn(att[...], w_o[...])
        put_halves(keep, send, acc, core)


def mem2(reset, rates, terms, q_parts, vc, kc, hk, ks, kcv, gates, attended, w_o, mem_in, mem_out):
    units = mem_in.shape[1]
    chunk = units // STEPS
    piece = far(out_cols(CH, units, LOW, chunk))
    return run(
        "mem2", mem2_kernel, STEPS,
        [(reset, SMEM_SPEC), full(rates), *[full(t) for t in terms],
         *[full(p) for p in q_parts], full(vc), full(kc), cols_of(hk, chunk),
         cols_of(ks, chunk), cols_of(kcv, chunk), half_of(gates, 1), half_of(attended, 1), full(w_o),
         cols_of(mem_in, chunk), rows_of(mem_out, chunk)],
        [near(out_full((CH, D), LOW)), near(out_full((CH, D), LOW)), piece, piece, far(out_cols(D, units, LOW, chunk)),
         far(((units, D), LOW, pl.BlockSpec((chunk, D), lambda i: (i, 0)))), piece, piece, far(out_full((CH, D), LOW))]
        + halves_out(),
        [scratch_half()], 15.0,
    )


def feed_kernel(
    s0, s1, s2, s3, x, gain, w_up, w_down, c0, c1, c2, c3,
    normed, cot, hid, gg, gu, fkeep, fsend, midloc, gain_part, keep, send, mid, acc_out, acc_norm,
):
    step = pl.program_id(0)
    me, core = my_place()
    width = c0.shape[1]

    @pl.when(step == 0)
    def _():
        for r, part in enumerate((c0, c1, c2, c3)):
            cot[:, span(me ^ r, width)] = part[...]
        for rows, total in halves((s0, s1, s2, s3), core):
            middle = x[rows, :].astype(F32) + total
            mid[rows, :] = middle
            inverse = lax.rsqrt(jnp.mean(middle * middle, -1, keepdims=True) + EPS)
            normed[rows, :] = (middle * inverse * gain_row(gain)).astype(LOW)

    gate_val = dot_nn(normed[...], w_up[0])
    up_val = dot_nn(normed[...], w_up[1])
    grad_hid = dot_nt(cot[...], w_down[...])
    sig = jax.nn.sigmoid(gate_val)
    act = gate_val * sig
    hidden = (act * up_val).astype(LOW)
    hid[...] = hidden
    grad_gate = (grad_hid * up_val * silu_slope(gate_val, sig)).astype(LOW)
    grad_up = (grad_hid * act).astype(LOW)
    gg[...] = grad_gate
    gu[...] = grad_up
    add_to(acc_norm, step == 0, dot_nt(grad_gate, w_up[0]) + dot_nt(grad_up, w_up[1]))
    add_to(acc_out, step == 0, dot_nn(hidden, w_down[...]))

    @pl.when(step == STEPS - 1)
    def _():
        put_columns(fkeep, fsend, acc_out, core, width)
        midloc[...] = mid[:, span(me, width)]
        total = jnp.zeros((1, D), F32)
        for part in range(2):
            rows = pl.ds(part * (CH // 2), CH // 2)
            middle = mid[rows, :]
            inverse = lax.rsqrt(jnp.mean(middle * middle, -1, keepdims=True) + EPS)
            unit = middle * inverse
            grad = acc_norm[rows, :]
            total = total + jnp.sum(grad * unit, 0, keepdims=True)
            acc_norm[rows, :] = norm_back(grad, unit, inverse, gain_row(gain))
        gain_part[...] = total
        put_halves(keep, send, acc_norm, core)


def feed(half, terms, tokens, gain, w_gate_up, w_down, cot_parts, held=()):
    units = w_down.shape[0]
    chunk = units // STEPS
    width = cot_parts[0].shape[1]
    piece = near(out_cols(CH, units, LOW, chunk))
    quarter = ((2, LEN, width), LOW, pl.BlockSpec((2, CH, width), lambda i: (0, half, 0)))
    return run(
        "feed" + str(half), feed_kernel, STEPS,
        [*[full(t) for t in terms], half_of(tokens, half), full(gain),
         (w_gate_up, pl.BlockSpec((2, D, chunk), lambda i: (0, 0, i))), rows_of(w_down, chunk)]
        + [half_of(p, half) for p in cot_parts],
        [near(out_full((CH, D), LOW)), near(out_full((CH, D), LOW)), piece, piece, piece, quarter, quarter,
         far(out_full((CH, width), F32)), far(out_full((1, D), F32))] + halves_out(),
        [scratch_half(), scratch_half(), scratch_half()], 15.0, held, {0: 5, 1: 6} if held else {},
    )


ROW_STEPS = 4


def put_rows(keep, send, v, bit, size, place):
    block = D // size
    v = v.reshape(v.shape[0] // (2 * block << place), 2, 1 << place, block, v.shape[1])
    shape = (v.shape[0] << place, block, v.shape[4])
    keep[...] = jnp.where(bit == 0, v[:, 0], v[:, 1]).astype(LOW).reshape(shape)
    send[...] = jnp.where(bit == 0, v[:, 1], v[:, 0]).astype(LOW).reshape(shape)


def put_col_blocks(keep, send, v, bit, size, place):
    block = D // size
    for i in range(size // 2):
        first = ((i >> place) << (place + 1)) | (i & ((1 << place) - 1))
        second = first | (1 << place)
        zero = v[:, first * block : (first + 1) * block]
        one = v[:, second * block : (second + 1) * block]
        keep[i] = jnp.where(bit == 0, zero, one).astype(LOW)
        send[i] = jnp.where(bit == 0, one, zero).astype(LOW)


def row_out(size, units, steps):
    block = D // size
    return ((size // 2, block, units), LOW, pl.BlockSpec((size // 2 // steps, block, units), lambda i: (i, 0, 0)))


def col_out(size, units):
    block = D // size
    return ((size // 2, units, block), LOW, pl.BlockSpec((size // 2, units // ROW_STEPS, block), lambda i: (0, i, 0)))


def feed_weights_kernel(size, na, nb, gga, ggb, gua, gub, ca, cb, ha, hb, ukeep, usend, dkeep, dsend):
    bit = wide_bit(0)
    for which, (a, b) in enumerate(((gga, ggb), (gua, gub))):
        v = dot_tn(na[...], a[...]) + dot_tn(nb[...], b[...])
        put_rows(ukeep.at[:, which], usend.at[:, which], v, bit, size, 0)
    v = dot_tn(ha[...], ca[...]) + dot_tn(hb[...], cb[...])
    put_col_blocks(dkeep, dsend, v, bit, size, 0)


def feed_weights(size, na, nb, gga, ggb, gua, gub, ca, cb, ha, hb):
    units = ha.shape[1]
    block = D // ROW_STEPS
    rows = D // size
    per = block // rows
    half = ((size // 2, 2, rows, units), LOW, pl.BlockSpec((per // 2, 2, rows, units), lambda i: (i, 0, 0, 0)))
    cols = col_out(size, units)
    return run(
        "feed_weights", lambda *refs: feed_weights_kernel(size, *refs), ROW_STEPS,
        [cols_of(na, block), cols_of(nb, block), full(gga), full(ggb), full(gua), full(gub), full(ca), full(cb),
         cols_of(ha, units // ROW_STEPS), cols_of(hb, units // ROW_STEPS)],
        [far(half), far(half), far(cols), far(cols)], (), 11.7, room=0 if rows >= 128 else 24,
    )


def mid_grad(terms, cot, core, grad):
    for rows, total in halves(terms, core):
        grad[rows, :] = total + cot[rows, :].astype(F32)


def gate_side(gates, rec, grad, low, loc, head_grad, recall_grad, me, width):
    columns = head_columns()
    gates = gates[...]
    terms = narrow_heads(rec[...].astype(F32) * grad[...], columns)
    head_grad[...] = terms * gates * (1.0 - gates)
    recall_grad[...] = (widen(gates, columns) * grad[...]).astype(LOW)
    low[...] = grad[...].astype(LOW)
    loc[...] = grad[:, span(me, width)]


def recall1_back_kernel(
    s0, s1, s2, s3, cot, gates, rec, hid, slope, q, w_in, w_out,
    low, loc, head_grad, g_in, g_out, dq, grad, rgrad,
):
    step = pl.program_id(0)
    me, core = my_place()

    @pl.when(step == 0)
    def _():
        mid_grad((s0, s1, s2, s3), cot, core, grad)
        gate_side(gates, rec, grad, low, loc, head_grad, rgrad, me, loc.shape[1])

    rg = rgrad[...]
    dpre = (dot_nt(rg, w_out[...]) * slope[...].astype(F32)).astype(LOW)
    g_out[...] = dot_tn(hid[...], rg).astype(LOW)
    g_in[...] = dot_tn(q[...], dpre).astype(LOW)
    add_to(dq, step == 0, dot_nt(dpre, w_in[...]))


def recall1_back(width, terms, cot, gates, rec, hid, slope, q, mem_in, mem_out):
    units = mem_in.shape[1]
    chunk = units // STEPS
    return run(
        "recall1_back", recall1_back_kernel, STEPS,
        [*[full(t) for t in terms], full(cot), half_of(gates, 0), full(rec), cols_of(hid, chunk),
         cols_of(slope, chunk), full(q), cols_of(mem_in, chunk), rows_of(mem_out, chunk)],
        [near(out_full((CH, D), LOW)), far(out_full((CH, width), F32)), far(out_full((CH, 128), F32)),
         far(out_cols(D, units, LOW, chunk)), far(((units, D), LOW, pl.BlockSpec((chunk, D), lambda i: (i, 0)))),
         near(out_full((CH, D), F32))],
        [scratch_half(), pltpu.VMEM((CH, D), LOW)], 12.2,
    )


def mem2_back_kernel(
    reset, rates, s0, s1, s2, s3, cot, gates, rec, hid, slope, q, m_in, m_out, kc, hk, ks, bcurve, slope_low, w_in, w_out,
    low, loc, head_grad, d_in, d_out, dpre_out, dback, gsb, sums, keep, send, grad, rgrad, acc,
):
    step = pl.program_id(0)
    me, core = my_place()
    kept, _, rate = rates_of(reset, rates)

    @pl.when(step == 0)
    def _():
        mid_grad((s0, s1, s2, s3), cot, core, grad)
        gate_side(gates, rec, grad, low, loc, head_grad, rgrad, me, loc.shape[1])

    rg = rgrad[...]
    dpre = (dot_nt(rg, m_out[...]) * slope[...].astype(F32)).astype(LOW)
    dpre_out[...] = dpre
    dm_out = dot_tn(hid[...], rg)
    dm_out_low = dm_out.astype(LOW)
    d_out[...] = dm_out_low
    dm_in = dot_tn(q[...], dpre)
    dm_in_low = dm_in.astype(LOW)
    d_in[...] = dm_in_low
    decayed = jnp.sum(w_in[...].astype(F32) * dm_in, 0, keepdims=True)
    decayed_out = jnp.sum(w_out[...].astype(F32) * dm_out, 0, keepdims=True)
    t_in = dot_nn(kc[...], dm_in_low)
    stepped = jnp.sum(slope_low[...].astype(F32) * t_in, 0, keepdims=True)
    grad_slope = t_in * (-kept * rate * (STEP_IN / CH))
    gsb[...] = (grad_slope * bcurve[...].astype(F32)).astype(LOW)
    db = (grad_slope * ks[...].astype(F32)).astype(LOW)
    dback[...] = db
    sums[0:1, :] = decayed
    sums[1:2, :] = stepped
    chunk = decayed.shape[1]
    sums[2:3, :] = sum(decayed_out[:, i * chunk : (i + 1) * chunk] for i in range(decayed_out.shape[1] // chunk))
    add_to(
        acc, step == 0,
        dot_nn(hk[...], dm_out_low) * (-kept * rate * (STEP_OUT / CH)) + dot_nn(db, w_out[...]),
    )

    @pl.when(step == STEPS - 1)
    def _():
        put_halves(keep, send, acc, core)


def mem2_back(
    width, reset, rates, terms, cot, gates, rec, hid, slope, q, m_in, m_out, kc, hk, ks, bcurve, slope_low,
    mem_in, mem_out,
):
    units = mem_in.shape[1]
    chunk = units // STEPS
    piece = near(out_cols(CH, units, LOW, chunk))
    return run(
        "mem2_back", mem2_back_kernel, STEPS,
        [(reset, SMEM_SPEC), full(rates), *[full(t) for t in terms], full(cot), half_of(gates, 1), full(rec),
         cols_of(hid, chunk), cols_of(slope, chunk), full(q), cols_of(m_in, chunk), rows_of(m_out, chunk),
         full(kc), cols_of(hk, chunk), cols_of(ks, chunk), cols_of(bcurve, chunk), cols_of(slope_low, chunk),
         cols_of(mem_in, chunk), rows_of(mem_out, chunk)],
        [near(out_full((CH, D), LOW)), far(out_full((CH, width), F32)), far(out_full((CH, 128), F32)),
         near(out_cols(D, units, LOW, chunk)), near(((units, D), LOW, pl.BlockSpec((chunk, D), lambda i: (i, 0)))),
         piece, piece, piece, far(out_cols(3, units, F32, chunk))] + halves_out(),
        [scratch_half(), pltpu.VMEM((CH, D), LOW), scratch_half()], 18.0,
    )


def mem2_late_kernel(reset, rates, err, hk, ks, gsb, slope_low, d_in, d_out, dpre, m_in, base, sums, dq, dk):
    step = pl.program_id(0)
    kept, _, rate = rates_of(reset, rates)
    t_out = dot_nt(err[...], d_out[...])
    sums[...] = jnp.sum(hk[...].astype(F32) * t_out, 0, keepdims=True)
    base[...] = (t_out * (-kept * rate * (STEP_OUT / CH)) * ks[...].astype(F32) + gsb[...].astype(F32)).astype(LOW)
    add_to(dk, step == 0, dot_nt(slope_low[...], d_in[...]) * (-kept * rate * (STEP_IN / CH)))
    add_to(dq, step == 0, dot_nt(dpre[...], m_in[...]))


def mem2_late(reset, rates, err, hk, ks, gsb, slope_low, d_in, d_out, dpre, m_in):
    units = hk.shape[1]
    chunk = units // STEPS
    return run(
        "mem2_late", mem2_late_kernel, STEPS,
        [(reset, SMEM_SPEC), full(rates), full(err), cols_of(hk, chunk), cols_of(ks, chunk), cols_of(gsb, chunk),
         cols_of(slope_low, chunk), cols_of(d_in, chunk), rows_of(d_out, chunk), cols_of(dpre, chunk),
         cols_of(m_in, chunk)],
        [near(out_cols(CH, units, LOW, chunk)), far(out_cols(1, units, F32, chunk)), near(out_full((CH, D), F32)),
         near(out_full((CH, D), F32))],
        (), 10.6,
    )


def query_split_kernel(reset, n, gates, heads_a, heads_b, sums, sums_out, dq1, dq2, keep, send_a, send_b, heads, small):
    core = my_place()[1]
    width = keep.shape[2]
    for part, (ref, send) in enumerate(((dq1, send_a), (dq2, send_b))):
        for i in range(2):
            keep[i, pl.ds(part * CH, CH), :] = ref[:, span(2 * i + core, width)].astype(LOW)
            send[i] = ref[:, span(2 * i + 1 - core, width)].astype(LOW)
    kept = 1.0 - reset[0].astype(F32)
    decay_part = jnp.sum(sums[0:1, :] + sums[2:3, :], 1, keepdims=True) * (-kept / CH)
    step_part = jnp.sum(STEP_IN * sums[1:2, :] + STEP_OUT * sums_out[...], 1, keepdims=True) * (-kept / (CH * CH))
    lane = lax.broadcasted_iota(jnp.int32, (1, 128), 1)
    logit = jnp.where(lane == HEADS, decay_part, 0.0) + jnp.where(lane == HEADS + 1, step_part, 0.0)
    g = gates[...]
    heads[:CH, :] = (heads_a[...] + g * (1.0 - g) * logit).astype(LOW)
    heads[CH:, :] = heads_b[...].astype(LOW)
    small[...] = dot_tn(heads[...], n[...])


def query_split(width, reset, normed, gates, heads_a, heads_b, sums, sums_out, dq1, dq2):
    quarter = out_full((2, LEN, width), LOW)
    half = out_full((2, CH, width), LOW)
    return run(
        "query_split", query_split_kernel, 1,
        [(reset, SMEM_SPEC), full(normed), half_of(gates, 0), full(heads_a), full(heads_b), full(sums), full(sums_out),
         full(dq1), full(dq2)],
        [quarter, half, half, out_full((LEN, 128), LOW), out_full((128, D), F32)], (), 5.0,
    )


def mem1_back_kernel(s0, s1, s2, s3, ks, base, dk, w_in, w_out, dpred, dpre_out, vshare, keep, send, acc):
    step = pl.program_id(0)
    me, core = my_place()
    width = vshare.shape[1]

    @pl.when(step == 0)
    def _():
        for rows, total in halves((s0, s1, s2, s3), core):
            dpred[rows, :] = total.astype(LOW)
        vshare[...] = -dpred[:, span(me, width)].astype(F32)
        acc[...] = dk[...]

    dpre = (dot_nt(dpred[...], w_out[...]) * ks[...].astype(F32) + base[...].astype(F32)).astype(LOW)
    dpre_out[...] = dpre
    acc[...] += dot_nt(dpre, w_in[...])

    @pl.when(step == STEPS - 1)
    def _():
        put_columns(keep, send, acc, core, width)


def mem1_back(width, terms, ks, base, dk, mem_in, mem_out):
    units = mem_in.shape[1]
    chunk = units // STEPS
    quarter = out_full((2, CH, width), LOW)
    return run(
        "mem1_back", mem1_back_kernel, STEPS,
        [*[full(t) for t in terms], cols_of(ks, chunk), cols_of(base, chunk), full(dk),
         cols_of(mem_in, chunk), rows_of(mem_out, chunk)],
        [near(out_full((CH, D), LOW)), near(out_cols(CH, units, LOW, chunk)), far(out_full((CH, width), F32)), quarter,
         quarter],
        [scratch_half()], 7.2,
    )


def mem_weights_kernel(size, reset, rates, g_in, g_out, d_in, d_out, kc, dpre, dback, err, hk, dpred, ikeep, isend, okeep, osend):
    bit = wide_bit(0)
    kept, decay, _ = rates_of(reset, rates)
    retain = 1.0 - kept * decay
    v = g_in[...].astype(F32) + retain * d_in[...].astype(F32) + dot_tn(kc[...], dpre[...])
    put_rows(ikeep, isend, v, bit, size, 0)
    v = (
        g_out[...].astype(F32) + retain * d_out[...].astype(F32)
        + dot_tn(dback[...], err[...]) + dot_tn(hk[...], dpred[...])
    )
    put_col_blocks(okeep, osend, v, bit, size, 0)


def mem_weights(size, reset, rates, g_in, g_out, d_in, d_out, kc, dpre, dback, err, hk, dpred):
    units = hk.shape[1]
    block = D // ROW_STEPS
    unit_block = units // ROW_STEPS
    r, c = row_out(size, units, ROW_STEPS), col_out(size, units)
    return run(
        "mem_weights", lambda *refs: mem_weights_kernel(size, *refs), ROW_STEPS,
        [(reset, SMEM_SPEC), full(rates), rows_of(g_in, block), rows_of(g_out, unit_block), rows_of(d_in, block),
         rows_of(d_out, unit_block), cols_of(kc, block), full(dpre), cols_of(dback, unit_block), full(err),
         cols_of(hk, unit_block), full(dpred)],
        [r, r, c, c], (), 9.4, room=0 if D // size >= 128 else 24,
    )


def weights1_kernel(size, n, gma, gmb, att, gv, keep, send):
    v_out = dot_tn(gma[...], att[:CH, :]) + dot_tn(gmb[...], att[CH:, :])
    v = jnp.concatenate([v_out, dot_tn(n[...], gv[...])], 1)
    put_rows(keep, send, v, wide_bit(0), size, 0)


def weights1(size, normed, gma, gmb, attended, gv):
    width = gv.shape[1]
    r = row_out(size, 2 * width, ROW_STEPS)
    block = D // ROW_STEPS
    return run(
        "weights1", lambda *refs: weights1_kernel(size, *refs), ROW_STEPS,
        [cols_of(normed, block), cols_of(gma, block), cols_of(gmb, block), full(attended), full(gv)],
        [r, r], (), 7.0,
    )


def weights2_kernel(size, n, gq, gk, keep, send):
    v = jnp.concatenate([dot_tn(n[...], gq[...]), dot_tn(n[...], gk[...])], 1)
    put_rows(keep, send, v, wide_bit(0), size, 0)


def weights2(size, normed, gq, gk):
    r = row_out(size, 2 * gq.shape[1], 2)
    return run(
        "weights2", lambda *refs: weights2_kernel(size, *refs), 2,
        [cols_of(normed, D // 2), full(gq), full(gk)], [r, r], (), 5.0,
    )


def last_kernel(gq, gk, gv, w, heads, gate_t, decay_t, x, gain, keep, send_a, send_b, gain_part):
    step = pl.program_id(0)
    core = my_place()[1]
    width = gq.shape[1]
    grad = dot_nn(heads[:, :HEADS], gate_t[...]) + dot_nn(heads[:, HEADS : HEADS + 2], decay_t[...])
    for i, ref in enumerate((gq, gk, gv)):
        grad = grad + dot_nt(ref[...], w[i])
    xf = x[...].astype(F32)
    inverse = lax.rsqrt(jnp.mean(xf * xf, -1, keepdims=True) + EPS)
    unit = xf * inverse
    add_to(gain_part, step == 0, jnp.sum(grad * unit, 0, keepdims=True))
    back = norm_back(grad, unit, inverse, gain_row(gain)).astype(LOW)
    for i in range(2):
        blocks = [back[:, (2 * i + b) * width : (2 * i + b + 1) * width] for b in range(2)]
        keep[i] = jnp.where(core == 0, blocks[0], blocks[1])
        away = jnp.where(core == 0, blocks[1], blocks[0])
        for part, send in enumerate((send_a, send_b)):

            @pl.when(step // 2 == part)
            def _():
                send[i] = away


def last(gq, gk, gv, w_t, heads, gate_t, decay_t, tokens, gain):
    width = gq.shape[1]
    rows = LEN // 4
    quarter = ((2, LEN, width), LOW, pl.BlockSpec((2, rows, width), lambda i: (0, i, 0)))

    def send(part):
        at = (lambda i: (0, jnp.minimum(i, 1), 0)) if part == 0 else (lambda i: (0, jnp.maximum(i - 2, 0), 0))
        return ((2, CH, width), LOW, pl.BlockSpec((2, rows, width), at))

    return run(
        "last", last_kernel, 4,
        [rows_of(gq, rows), rows_of(gk, rows), rows_of(gv, rows), full(w_t), rows_of(heads, rows),
         full(gate_t), full(decay_t), rows_of(tokens, rows), full(gain)],
        [quarter, send(0), send(1), out_full((1, D), F32)],
        (), 8.5,
    )


def attend_back_kernel(
    doc_ref, q_ref, k_ref, v_ref, pk_ref, pv_ref, gma, gmb, wo_ref, peak_ref, inv_ref,
    dq_ref, dk_ref, dv_ref, dpk_ref, dpv_ref, go_ref,
):
    k = k_ref[0]
    v = v_ref[0]
    keys_t = flat(k)
    pk = pk_ref[0]
    pv = pv_ref[0]
    pk_t = flat(pk)
    for ref in (dk_ref, dv_ref, dpk_ref, dpv_ref):
        ref[...] = jnp.zeros_like(ref)
    for half, gm in enumerate((gma, gmb)):
        rows = pl.ds(half * CH, CH)
        go_ref[rows, :] = dot_nt(gm[...], wo_ref[...]).astype(LOW)
    for block in range(LEN // QB):
        low_key, high_key = key_range(block)
        keys = pl.ds(low_key, high_key - low_key)
        rows = pl.ds(block * QB, QB)
        ok = allowed(doc_ref, block, low_key, high_key)
        q = q_ref[0, rows, :].astype(F32)
        go = go_ref[rows, :].astype(F32)
        outs = []
        for index in range(2):
            q_head = scaled_head(q, index)
            go_head = one_head(go, index)
            peak = peak_ref[0, index : index + 1, rows]
            inv = inv_ref[0, index : index + 1, rows]
            s = jnp.where(ok, dot_nt(k[low_key:high_key], q_head), NEG)
            sp = dot_nt(pk, q_head)
            prob = jnp.exp(s - peak) * inv
            prob_p = jnp.exp(sp - peak) * inv
            gp = dot_nt(v[low_key:high_key], go_head)
            gpp = dot_nt(pv, go_head)
            center = jnp.sum(prob * gp, 0, keepdims=True) + jnp.sum(prob_p * gpp, 0, keepdims=True)
            gs = (prob * (gp - center)).astype(LOW)
            gsp = (prob_p * (gpp - center)).astype(LOW)
            dk_ref[keys, :] += dot_nn(gs, q_head)
            dv_ref[keys, :] += dot_nn(prob.astype(LOW), go_head)
            dpk_ref[...] += dot_nn(gsp, q_head)
            dpv_ref[...] += dot_nn(prob_p.astype(LOW), go_head)
            feats = slice(index * HD, index * HD + HD)
            outs.append(dot_nn(keys_t[feats, low_key:high_key], gs) + dot_nn(pk_t[feats], gsp))
        dq_ref[rows, :] = jnp.concatenate(outs, 0).T * 8.0


def attend_back(doc_len, act, persistent, gma, gmb, w_o, peak, inv):
    width = act.shape[2]
    pairs = width // 128

    def part(i):
        return (act, pl.BlockSpec((1, LEN, 128), lambda g: (i, 0, g)))

    def pers(i):
        return (persistent, pl.BlockSpec((1, NP, 128), lambda g: (i, 0, g)))

    stat = pl.BlockSpec((1, 2, LEN), lambda g: (g, 0, 0))
    cols = near(((LEN, width), F32, pl.BlockSpec((LEN, 128), lambda g: (0, g))))
    small = far(((NP, width), F32, pl.BlockSpec((NP, 128), lambda g: (0, g))))
    return run(
        "attend_back", attend_back_kernel, pairs,
        [(doc_len, SMEM_SPEC), part(0), part(1), part(2), pers(0), pers(1), full(gma), full(gmb),
         rows_of(w_o, 128), (peak, stat), (inv, stat)],
        [cols, cols, cols, small, small],
        [pltpu.VMEM((LEN, 128), LOW)], 15.6,
    )


def conv_back_kernel(part, count, doc_ref, p_ref, taps_ref, datt_ref, *refs):
    extra, (gproj_ref, gtaps_ref, pad, padc) = refs[:count], refs[count:]
    width = p_ref.shape[2]
    pad[pl.ds(0, 8), :] = jnp.zeros((8, width), F32)
    padc[pl.ds(LEN, 8), :] = jnp.zeros((8, width), F32)
    pad[pl.ds(8, LEN), :] = p_ref[0]
    gt = [jnp.zeros((1, width), F32)] * KC
    ones_mat = same_head(width)
    for first in range(0, LEN, PRE_ROWS):
        rows = pl.ds(first, PRE_ROWS)
        age = ages(doc_ref, first, PRE_ROWS, width)
        c = conv_sum(pad, taps_ref, age, first, PRE_ROWS)
        sig = jax.nn.sigmoid(c)
        dy = datt_ref[rows, :]
        for ref in extra:
            if first < ref.shape[0]:
                dy = dy + ref[rows, :].astype(F32)
        if part < 2:
            a = c * sig
            inverse = lax.rsqrt(head_sum(a * a, ones_mat) + EPS)
            y = a * inverse
            dy = inverse * (dy - y * head_sum(dy * y, ones_mat))
        dc = dy * silu_slope(c, sig)
        padc[rows, :] = dc
        gt[0] = gt[0] + jnp.sum(dc * pad[pl.ds(first + 8, PRE_ROWS), :], 0, keepdims=True)
        for i in range(1, KC):
            shifted = jnp.where(age >= i, pad[pl.ds(first + 8 - i, PRE_ROWS), :], 0.0)
            gt[i] = gt[i] + jnp.sum(dc * shifted, 0, keepdims=True)
    gtaps_ref[...] = jnp.concatenate(gt, 0)
    for first in range(0, LEN, PRE_ROWS):
        total = taps_ref[0, 0:1, :].astype(F32) * padc[pl.ds(first, PRE_ROWS), :]
        for i in range(1, KC):
            age = ages(doc_ref, first + i, PRE_ROWS, width)
            total = total + taps_ref[0, i : i + 1, :].astype(F32) * jnp.where(
                age >= i, padc[pl.ds(first + i, PRE_ROWS), :], 0.0
            )
        gproj_ref[pl.ds(first, PRE_ROWS), :] = total.astype(LOW)


def conv_back(part, doc_len, p, taps, datt, extra):
    width = p.shape[2]
    count = len(extra)
    return run(
        "conv_back" + str(part), lambda *refs: conv_back_kernel(part, count, *refs), 1,
        [(doc_len, SMEM_SPEC), (p, pl.BlockSpec((1, LEN, width), lambda i: (part, 0, 0))),
         (taps, pl.BlockSpec((1, KC, width), lambda i: (part, 0, 0))), full(datt)] + [full(e) for e in extra],
        [near(out_full((LEN, width), LOW)), far(out_full((KC, width), F32))],
        [pltpu.VMEM((LEN + 8, width), F32), pltpu.VMEM((LEN + 8, width), F32)], 6.5,
    )


def body(
    tokens,
    gain_in,
    gain_mid,
    w_qkv,
    w_gate,
    w_decay,
    conv_kernel,
    persistent,
    w_out,
    mem_in,
    mem_out,
    w_up,
    w_down,
    doc_len,
    reset,
    cotangent,
):
    assert doc_len.shape[0] == 1 and lax.axis_size("narrow") == 4
    width = w_qkv.shape[2]
    size = lax.axis_size("wide")
    me = lax.axis_index("narrow")
    gain_in_f, gain_mid_f = gain_in.reshape(-1, 128), gain_mid.reshape(-1, 128)
    w_t = w_qkv.transpose(1, 0, 2)
    taps = conv_kernel
    gate_t, decay_t = w_gate.T, w_decay.T
    LAST.clear()
    PLACED.clear()
    for a in (tokens, w_t, w_out, mem_in, mem_out, w_down, persistent, gain_in_f, gain_mid_f, gate_t, decay_t, taps):
        put(a, pltpu.HBM)
    cot = Parts(cotangent)
    normed_in, gates, rates, projected, act, own_q, own_heads = pre(
        doc_len, tokens, gain_in_f, w_t, gate_t, decay_t, taps
    )

    cot.end()
    heads_in = Parts(own_heads)
    query = Parts(own_q)
    attended, peak, inv = attend(doc_len, act, persistent)
    cot_parts = [put(t, pltpu.HBM) for t in cot.settle()]
    w_gate_up = put(tie(w_up.transpose(1, 0, 2)), pltpu.VMEM)
    mem_in, mem_out, w_down = fetch(mem_in, mem_out, w_down)
    heads_in = heads_in.end()
    q_a, kc, vc, hk, ks, kcv, *pred = mem1(heads_in, mem_in, mem_out)
    pred = Halves(*pred)
    pred.middle()
    hid1, slope1, rec1, *join1 = recall1(q_a, gates, attended, w_out, mem_in, mem_out)
    join1 = Halves(*join1)
    query.end()
    pred = pred.end()
    join1.middle()
    q_parts = query.settle()
    q_b, err, slope_low, bcurve, m_in, m_out, hid2, slope2, rec2, *join2 = mem2(
        reset, rates, pred, q_parts, vc, kc, hk, ks, kcv, gates, attended, w_out, mem_in, mem_out
    )
    join2 = Halves(*join2)
    join1 = join1.end()
    join2.middle()
    na, cota, ha, gga, gua, fkeep, fsend, mloca, gain_a, *mid1 = feed(
        0, join1, tokens, gain_mid_f, w_gate_up, w_down, cot_parts
    )
    mid1 = Halves(*mid1)
    join2 = join2.end()
    mid1.middle()
    nb, cotb, hb, ggb, gub, fkeep, fsend, mlocb, gain_b, *mid2 = feed(
        1, join2, tokens, gain_mid_f, w_gate_up, w_down, cot_parts, (fkeep, fsend)
    )
    mid2 = Halves(*mid2)
    outs = Columns(fkeep, fsend)

    mid1.end()
    mid2.middle()
    mid1_terms = mid1.settle()
    ukeep, usend, dkeep, dsend = feed_weights(size, na, nb, gga, ggb, gua, gub, cota, cotb, ha, hb)
    up_sum = Rows(1, ukeep, usend)
    down_sum = Rows(1, dkeep, dsend)
    mid2 = mid2.end()
    gmb, locb, heads_b, d_in, d_out, dpre2, dback, gsb, sums, *gerr = mem2_back(
        width, reset, rates, mid2, cotb, gates, rec2, hid2, slope2, q_b, m_in, m_out, kc, hk, ks, bcurve, slope_low,
        mem_in, mem_out,
    )
    gerr = Halves(*gerr)
    gerr.middle()
    outs.middle()
    gma, loca, heads_a, g_in, g_out, dq1 = recall1_back(
        width, mid1_terms, cota, gates, rec1, hid1, slope1, q_a, mem_in, mem_out
    )
    gerr.end()
    dq, dka, dva, dpk, dpv = attend_back(doc_len, act, persistent, gma, gmb, w_out, peak, inv)
    outs = outs.end()
    gerr_terms = gerr.settle()
    base, sums_out, dq2, dk = mem2_late(reset, rates, err, hk, ks, gsb, slope_low, d_in, d_out, dpre2, m_in)
    up_sum.step()
    dpred, dpre1, v_share, kkeep, ksend = mem1_back(width, gerr_terms, ks, base, dk, mem_in, mem_out)
    k_share = Columns(kkeep, ksend)
    ikeep, isend, okeep, osend = mem_weights(
        size, reset, rates, g_in, g_out, d_in, d_out, kc, dpre1, dback, err, hk, dpred
    )
    in_sum = Rows(1, ikeep, isend)
    back_sum = Rows(1, okeep, osend)
    qkeep, qsend_a, qsend_b, heads, small_part = query_split(
        width, reset, normed_in, gates, heads_a, heads_b, sums, sums_out, dq1, dq2
    )
    q_share = Columns(qkeep, qsend_a, qsend_b)
    k_share.middle()
    down_sum.step()
    q_share.middle()
    gv, tap_v = conv_back(2, doc_len, projected, taps, dva, [v_share])
    up_sum.step()
    gk, tap_k = conv_back(1, doc_len, projected, taps, dka, k_share.end())
    wkeep, wsend = weights1(size, normed_in, gma, gmb, attended, gv)
    w_sum = Rows(1, wkeep, wsend)
    down_sum.step()
    gq, tap_q = conv_back(0, doc_len, projected, taps, dq, q_share.end())
    in_sum.step()
    qkeep, qsend = weights2(size, normed_in, gq, gk)
    q_sum = Rows(1, qkeep, qsend)
    down_grads = down_sum.end()
    up_grads = up_sum.end()
    in_sum.step()
    lkeep, lsend_a, lsend_b, gain_part = last(gq, gk, gv, w_t, heads, gate_t, decay_t, tokens, gain_in_f)
    in_share = Columns(lkeep, lsend_a, lsend_b)
    back_sum.step()
    in_share.middle()
    own = jnp.concatenate([dpk, dpv], 0).reshape(-1, D)
    taps_part = jnp.concatenate([tap_q, tap_k, tap_v], 0).reshape(-1, D)
    late = Small(
        jnp.concatenate([own, taps_part, gain_a + gain_b, small_part[: HEADS + 2], gain_part], 0), "wide"
    )
    in_grads = in_sum.end()
    w_sum.step()
    back_sum.step()
    q_sum.step()
    late.step()
    w_sum.step()
    up_grads = pinned(up_grads.transpose(1, 0, 2))
    output = pinned((jnp.concatenate([mloca, mlocb], 0) + outs[0].astype(F32) + outs[1].astype(F32)).astype(LOW))
    back_grads = back_sum.end()
    q_sum.step()
    late.step()
    in_share = in_share.end()
    grad_input = pinned(in_share[0].astype(F32) + in_share[1].astype(F32) + jnp.concatenate([loca, locb], 0))
    w_grads = w_sum.end()
    late = late.end()
    late = Small(place_own(late, 2 * NP + 3 * KC, width, me), "narrow")
    q_grads = q_sum.end()
    late.step()
    late = late.end()
    pers_sum = late[: 2 * NP].reshape(2, NP, D)
    conv_sum = late[2 * NP : 2 * NP + 3 * KC].reshape(3, KC, D)
    vecs = late[2 * NP + 3 * KC :]
    rows = D // size
    gate_shard = cut(vecs[1 : HEADS + 1], lax.axis_index("wide") * rows, rows, 1).T
    return (
        output,
        grad_input,
        vecs[HEADS + 3],
        vecs[0],
        jnp.stack([q_grads[:, :width], q_grads[:, width:], w_grads[:, width:]], 1),
        gate_shard,
        vecs[HEADS + 1 : HEADS + 3].T,
        conv_sum,
        pers_sum,
        w_grads[:, :width].T,
        in_grads,
        back_grads,
        up_grads,
        down_grads,
    )


def solution(mesh):
    in_specs = (
        P("wide", None),
        P(),
        P(),
        P(None, None, "narrow"),
        P(),
        P(),
        P(None, None, "narrow"),
        P(None, None, "narrow"),
        P("narrow", None),
        P(None, "narrow"),
        P("narrow", None),
        P(None, None, "narrow"),
        P("narrow", None),
        P("wide", None),
        P("wide"),
        P("wide", "narrow"),
    )
    out_specs = (
        P("wide", "narrow"),
        P("wide", "narrow"),
        P(),
        P(),
        P("wide", None, "narrow"),
        P("wide", None),
        P(),
        P(),
        P(),
        P("narrow", "wide"),
        P("wide", "narrow"),
        P("narrow", "wide"),
        P("wide", None, "narrow"),
        P("narrow", "wide"),
    )
    return jax.shard_map(body, mesh=mesh, in_specs=in_specs, out_specs=out_specs, check_vma=False)
```

```python
import jax
import jax.numpy as jnp
from jax import lax
from jax.experimental import pallas as pl
from jax.experimental.pallas import tpu as pltpu
from jax.sharding import PartitionSpec as P

D = 1024
HEADS = 16
HD = 64
LEN = 1024
CH = 512
WIN = 512
NP = 16
KC = 4


EPS = 1e-06
NEG = -1e30
STEP_IN = 128.0
STEP_OUT = 0.5
LOW = jnp.bfloat16
F32 = jnp.float32
VMEM = 12
VMEM_OF = {'pre': 16, 'mem1': 12, 'recall1': 15, 'mem2': 24, 'feed0': 28, 'feed1': 28, 'mem2_back': 32, 'recall1_back': 20, 'mem2_late': 15, 'mem1_back': 12, 'attend_back': 12}


def norm_back(grad_norm, unit_val, inverse, gain_vec):
    scaled = grad_norm * gain_vec
    return inverse * (scaled - unit_val * jnp.mean(scaled * unit_val, -1, keepdims=True))


def flip(v, axis, bit):
    size = lax.axis_size(axis)
    return lax.ppermute(v, axis, [(i, i ^ bit) for i in range(size)])


def bits_of(axis):
    size = lax.axis_size(axis)
    out = []
    bit = 1
    while bit < size:
        out.append(bit)
        bit *= 2
    assert bit == size
    return out


def pick(v, index, axis=0):
    return lax.dynamic_index_in_dim(v, index, axis, keepdims=False)


def cut(v, start, width, axis):
    return lax.dynamic_slice_in_dim(v, start, width, axis)


class Parts:
    def __init__(self, v):
        self.own, self.far, self.near = v, flip(v, "narrow", 2), flip(v, "narrow", 1)

    def end(self):
        far = tie(self.far)
        self.terms = [self.own, tie(self.near), far, flip(far, "narrow", 1)]
        return self.terms

    def settle(self):
        self.terms[3] = tie(self.terms[3])
        return self.terms


class Halves:
    def __init__(self, keep, *sends):
        self.keep, self.come = keep, [flip(send, "narrow", 1) for send in sends]

    def middle(self):
        self.run = fold_rows(self.keep, self.come)
        self.far = flip(self.run, "narrow", 2)
        self.near = flip(self.run, "narrow", 1)

    def end(self):
        far = tie(self.far)
        self.terms = [self.run, far, tie(self.near), flip(far, "narrow", 1)]
        return self.terms

    def settle(self):
        self.terms[3] = tie(self.terms[3])
        return self.terms


class Columns:
    def __init__(self, keep, *sends):
        self.keep, self.come = keep, [flip(send, "narrow", 1) for send in sends]

    def middle(self):
        self.run, away = fold_columns(self.keep, self.come)
        self.far = flip(away, "narrow", 2)

    def end(self):
        return [self.run[0], tie(self.far)[0]]


class Rows:
    def __init__(self, first, keep, send):
        self.keep, self.come = keep, flip(send, "wide", first)
        self.bits = [b for b in bits_of("wide") if b != first]

    def step(self):
        bit = self.bits.pop(0)
        self.keep, away = fold_pick(lambda: wide_bit(bit.bit_length() - 1), self.keep, self.come)
        self.come = flip(away, "wide", bit)

    def end(self):
        while self.bits:
            self.step()
        return fold(self.keep, self.come, F32)[0]


def place_own(v, rows, width, me):
    own = v[: rows * width // D].reshape(rows, width)
    own = lax.dynamic_update_slice(jnp.zeros((rows, D), F32), own, (0, me * width))
    return jnp.concatenate([own, v[rows * width // D :]], 0)


class Small:
    def __init__(self, v, axis):
        self.v = pinned(v)
        self.left = [(axis, b) for b in bits_of(axis)]
        self.send()

    def send(self):
        if self.left:
            self.come = flip(self.v, *self.left.pop(0))

    def step(self):
        self.v = pinned(self.v + tie(self.come))
        self.send()

    def end(self):
        while self.left:
            self.step()
        return self.v + tie(self.come)


def head_sum(v, ones_mat):
    high = v.astype(LOW)
    rest = (v - high.astype(F32)).astype(LOW)
    return jnp.dot(high, ones_mat, preferred_element_type=F32) + jnp.dot(
        rest, ones_mat, preferred_element_type=F32
    )


def same_head(width):
    row = lax.broadcasted_iota(jnp.int32, (width, width), 0) // HD
    col = lax.broadcasted_iota(jnp.int32, (width, width), 1) // HD
    return (row == col).astype(F32).astype(LOW)


def doc_start(doc_ref, places):
    start = jnp.zeros_like(places)
    end = 0
    for i in range(doc_ref.shape[1]):
        end = end + doc_ref[0, i]
        start = jnp.where(places >= end, end, start)
    return start


def conv_sum(pad_ref, taps_ref, age, first, rows):
    total = taps_ref[0, 0:1, :].astype(F32) * pad_ref[pl.ds(first + 8, rows), :]
    for i in range(1, KC):
        shifted = pad_ref[pl.ds(first + 8 - i, rows), :]
        total = total + taps_ref[0, i : i + 1, :].astype(F32) * jnp.where(age >= i, shifted, 0.0)
    return total


def ages(doc_ref, first, rows, width):
    places = first + lax.broadcasted_iota(jnp.int32, (rows, 128), 0)
    age = places - doc_start(doc_ref, places)
    return jnp.concatenate([age] * (width // 128), 1)


PRE_ROWS = 256


def pre_kernel(doc_ref, x_ref, gain_ref, w_ref, gate_ref, decay_ref, taps_ref, n_ref, gates_ref, rates_ref, p_ref, act_ref, q_ref, head_ref, pad):
    part = pl.program_id(0)
    width = w_ref.shape[2]

    @pl.when(part == 0)
    def _():
        pad[pl.ds(0, 8), :] = jnp.zeros((8, width), F32)
        total = jnp.zeros((1, 128), F32)
        for first in range(0, LEN, PRE_ROWS):
            rows = pl.ds(first, PRE_ROWS)
            x = x_ref[rows, :].astype(F32)
            inverse = lax.rsqrt(jnp.mean(x * x, -1, keepdims=True) + EPS)
            normed = (x * inverse * gain_row(gain_ref)).astype(LOW)
            n_ref[rows, :] = normed
            logits = [dot_nt(normed, gate_ref[...]), dot_nt(normed, decay_ref[...])]
            logits.append(jnp.zeros((PRE_ROWS, 128 - HEADS - 2), F32))
            gates = jax.nn.sigmoid(jnp.concatenate(logits, 1))
            gates_ref[rows, :] = gates
            if first < CH:
                total = total + jnp.sum(gates, 0, keepdims=True)
        rates_ref[...] = total * (1.0 / CH)

    for first in range(0, LEN, PRE_ROWS):
        rows = pl.ds(first, PRE_ROWS)
        p = jnp.dot(n_ref[rows, :], w_ref[0], preferred_element_type=F32)
        p_ref[0, rows, :] = p
        pad[pl.ds(first + 8, PRE_ROWS), :] = p
        age = ages(doc_ref, first, PRE_ROWS, width)
        c = conv_sum(pad, taps_ref, age, first, PRE_ROWS)
        a = c * jax.nn.sigmoid(c)

        @pl.when(part < 2)
        def _():
            out = a * lax.rsqrt(head_sum(a * a, same_head(width)) + EPS)
            act_ref[0, rows, :] = out.astype(LOW)

        @pl.when(part == 2)
        def _():
            act_ref[0, rows, :] = a.astype(LOW)

    head_ref[0] = act_ref[0, :CH, :]

    @pl.when(part == 0)
    def _():
        q_ref[...] = act_ref[0, CH:, :]


def pre(doc_len, tokens, gain, w_t, gate_t, decay_t, taps):
    width = w_t.shape[2]
    part = pl.BlockSpec((1, LEN, width), lambda i: (i, 0, 0))
    return run(
        "pre", pre_kernel, 3,
        [(doc_len, SMEM_SPEC), full(tokens), full(gain), (w_t, pl.BlockSpec((1, D, width), lambda i: (i, 0, 0))),
         full(gate_t), full(decay_t), (taps, pl.BlockSpec((1, KC, width), lambda i: (i, 0, 0)))],
        [far(out_full((LEN, D), LOW)), far(out_full((LEN, 128), F32)), far(out_full((1, 128), F32)),
         far(((3, LEN, width), F32, part)), far(((3, LEN, width), LOW, part)), out_full((CH, width), LOW),
         ((3, CH, width), LOW, pl.BlockSpec((1, CH, width), lambda i: (i, 0, 0)))],
        [pltpu.VMEM((LEN + 8, width), F32)], 13.0,
    )


def fetch_kernel(a, b, c, to_a, to_b, to_c):
    to_a[...] = a[...]
    to_b[...] = b[...]
    to_c[...] = c[...]


def fetch(mem_in, mem_out, w_down):
    arrays = [mem_in, mem_out, w_down]
    return run(
        "fetch", fetch_kernel, 4, [rows_of(a, a.shape[0] // 4) for a in arrays],
        [near((a.shape, LOW, pl.BlockSpec((a.shape[0] // 4, a.shape[1]), lambda i: (i, 0)))) for a in arrays], (), 2.0,
    )


QB = 256


def key_range(block):
    return max(0, (block - 2) * QB), (block + 1) * QB


def allowed(doc_ref, block, low_key, high_key):
    query = block * QB + lax.broadcasted_iota(jnp.int32, (8, QB), 1)
    low = jnp.maximum(doc_start(doc_ref, query), query - (WIN - 1))[0:1]
    key = low_key + lax.broadcasted_iota(jnp.int32, (high_key - low_key, QB), 0)
    return (key >= low) & (key <= query[0:1])


def scaled_head(q, index):
    lane = lax.broadcasted_iota(jnp.int32, q.shape, 1)
    return jnp.where(lane // HD == index, q * 8.0, 0.0).astype(LOW)


def one_head(v, index):
    lane = lax.broadcasted_iota(jnp.int32, v.shape, 1)
    return jnp.where(lane // HD == index, v, 0.0).astype(LOW)


def dot_nt(a, b):
    return lax.dot_general(a, b, (((1,), (1,)), ((), ())), preferred_element_type=F32)


def dot_nn(a, b):
    return jnp.dot(a, b, preferred_element_type=F32)


def dot_tn(a, b):
    return lax.dot_general(a, b, (((0,), (0,)), ((), ())), preferred_element_type=F32)


def flat(v):
    return v.astype(F32).T.astype(v.dtype)


def attend_kernel(doc_ref, q_ref, k_ref, v_ref, pk_ref, pv_ref, out_ref, peak_ref, inv_ref):
    k = k_ref[0]
    values_t = flat(v_ref[0])
    pk = pk_ref[0]
    pv_t = flat(pv_ref[0])
    for block in range(LEN // QB):
        low_key, high_key = key_range(block)
        ok = allowed(doc_ref, block, low_key, high_key)
        q = q_ref[0, pl.ds(block * QB, QB), :].astype(F32)
        outs = []
        for index in range(2):
            q_head = scaled_head(q, index)
            s = jnp.where(ok, dot_nt(k[low_key:high_key], q_head), NEG)
            sp = dot_nt(pk, q_head)
            peak = jnp.maximum(jnp.max(s, 0, keepdims=True), jnp.max(sp, 0, keepdims=True))
            e = jnp.exp(s - peak)
            ep = jnp.exp(sp - peak)
            inv = 1.0 / (jnp.sum(e, 0, keepdims=True) + jnp.sum(ep, 0, keepdims=True))
            feats = slice(index * HD, index * HD + HD)
            out = dot_nn(values_t[feats, low_key:high_key], e.astype(LOW)) + dot_nn(
                pv_t[feats], ep.astype(LOW)
            )
            outs.append(out * inv)
            peak_ref[0, index : index + 1, pl.ds(block * QB, QB)] = peak
            inv_ref[0, index : index + 1, pl.ds(block * QB, QB)] = inv
        out_ref[pl.ds(block * QB, QB), :] = jnp.concatenate(outs, 0).T.astype(LOW)


def attend(doc_len, act, persistent):
    width = act.shape[2]
    pairs = width // 128
    smem = pl.BlockSpec(memory_space=pltpu.SMEM)

    def part(i):
        return pl.BlockSpec((1, LEN, 128), lambda g: (i, 0, g))

    def pers(i):
        return pl.BlockSpec((1, NP, 128), lambda g: (i, 0, g))

    stat = pl.BlockSpec((1, 2, LEN), lambda g: (g, 0, 0))
    arrays = [doc_len, act, act, act, persistent, persistent]
    specs = [smem, part(0), part(1), part(2), pers(0), pers(1)]
    return run(
        "attend", attend_kernel, pairs, list(zip(arrays, specs)),
        [far(((LEN, width), LOW, pl.BlockSpec((LEN, 128), lambda g: (0, g)))), far(((pairs, 2, LEN), F32, stat)),
         far(((pairs, 2, LEN), F32, stat))],
        (), 9.3,
    )


SMEM_SPEC = pl.BlockSpec(memory_space=pltpu.SMEM)
STEPS = 2


def whole(shape):
    zeros = (0,) * len(shape)
    return pl.BlockSpec(tuple(shape), lambda *_: zeros, pipeline_mode=pl.Buffered(1))


LAST = []
PLACED = []


def placed(a):
    for other, space in PLACED:
        if other is a:
            return pltpu.with_memory_space_constraint(a, space)
    return a


def put(a, space):
    PLACED.append((a, space))
    return a


def chained(arrays, specs):
    arrays = [placed(a) for a in arrays]
    if LAST:
        return arrays + [placed(LAST[0])], specs + [pl.BlockSpec(memory_space=pl.ANY)]
    return arrays, specs


def remember(outs):
    LAST[:] = [min(outs, key=lambda o: o.size * o.dtype.itemsize)]
    return outs


def near(out):
    return (*out, pltpu.VMEM)


def far(out):
    return (*out, pltpu.HBM)


def shape_of(out):
    shape, kind = tuple(out[0]), out[1]
    return out[3](shape, kind) if len(out) > 3 else jax.ShapeDtypeStruct(shape, kind)


def run(name, kernel, steps, ins, outs, scratch=(), micros=0.0, held=(), aliases=(), room=0):
    used = len(ins)
    arrays = [a for a, _ in ins] + list(held)
    specs = [s for _, s in ins] + [pl.BlockSpec(memory_space=pl.ANY)] * len(held)
    arrays, specs = chained(arrays, specs)
    count = len(arrays)

    def inner(*refs):
        kernel(*refs[:used], *refs[count:])

    results = pl.pallas_call(
        inner,
        grid=(steps,),
        in_specs=specs,
        out_specs=[out[2] for out in outs],
        out_shape=[shape_of(out) for out in outs],
        scratch_shapes=list(scratch),
        input_output_aliases={used + k: v for k, v in dict(aliases).items()},
        compiler_params=pltpu.CompilerParams(vmem_limit_bytes=(VMEM_OF.get(name, VMEM) + room) << 20),
        cost_estimate=pl.CostEstimate(flops=1, bytes_accessed=1, transcendentals=0),
        name=name,
    )(*arrays)
    for result, out in zip(results, outs):
        if len(out) > 3:
            put(result, out[3])
    return remember(results)


def tie(v):
    space = next((space for other, space in PLACED if other is LAST[0]), None)
    v, LAST[0] = lax.optimization_barrier((v, LAST[0]))
    if space is not None:
        put(LAST[0], space)
    return v


def pinned(v):
    v = tie(v)
    LAST[:] = [v]
    return v


def fold_kernel(a, b, out):
    out[...] = (a[...].astype(F32) + b[...].astype(F32)).astype(out.dtype)


def fold(a, b, kind):
    zeros = (0,) * a.ndim
    spec = pl.BlockSpec(a.shape, lambda i: zeros)
    return run("fold", fold_kernel, 1, [(a, spec), (b, spec)], [far((a.shape, kind, spec)) if kind == F32 else (a.shape, kind, spec)])[0]


def fold_rows(keep, come):
    part = come[0].shape[0]

    def kernel(keep_ref, *refs):
        for i, ref in enumerate(refs[:-1]):
            at = pl.ds(i * part, part)
            refs[-1][at, :] = (keep_ref[at, :].astype(F32) + ref[...].astype(F32)).astype(LOW)

    return run("fold_rows", kernel, 1, [full(keep)] + [full(c) for c in come], [out_full(keep.shape, LOW)])[0]


def fold_columns(keep, come):
    count = len(come)
    _, rows, width = keep.shape
    part = rows // count

    def kernel(keep_ref, *refs):
        chip = lax.axis_index("narrow") >> 1
        run_ref, away_ref = refs[count:]
        for i in range(count):
            at = pl.ds(i * part, part)
            run_ref[0, at, :] = (keep_ref[chip, at, :].astype(F32) + refs[i][chip].astype(F32)).astype(LOW)
            away_ref[0, at, :] = (keep_ref[1 - chip, at, :].astype(F32) + refs[i][1 - chip].astype(F32)).astype(LOW)

    one = out_full((1, rows, width), LOW)
    return run("fold_columns", kernel, 1, [full(keep)] + [full(c) for c in come], [one, one], (), 1.5)


def fold_pick(bit_of, a, b):
    pairs = a.shape[0] // 2
    tail = a.shape[1:]
    zeros = (0,) * len(tail)
    two = pl.BlockSpec((2,) + tail, lambda i: (i,) + zeros)
    one = ((pairs,) + tail, LOW, pl.BlockSpec((1,) + tail, lambda i: (i,) + zeros))

    def kernel(a_ref, b_ref, keep, send):
        bit = bit_of()
        keep[0] = (a_ref[bit].astype(F32) + b_ref[bit].astype(F32)).astype(LOW)
        send[0] = (a_ref[1 - bit].astype(F32) + b_ref[1 - bit].astype(F32)).astype(LOW)

    return run("fold_pick", kernel, pairs, [(a, two), (b, two)], [one, one], (), 1.5)


def full(a):
    return (a, whole(a.shape))


def out_full(shape, kind):
    return (shape, kind, whole(shape))


def cols_of(a, chunk):
    return (a, pl.BlockSpec((a.shape[0], chunk), lambda i: (0, i)))


def rows_of(a, chunk):
    return (a, pl.BlockSpec((chunk, a.shape[1]), lambda i: (i, 0)))


def half_of(a, half):
    return (a, pl.BlockSpec((CH, a.shape[1]), lambda i: (half, 0)))


def out_cols(rows, cols, kind, chunk):
    return ((rows, cols), kind, pl.BlockSpec((rows, chunk), lambda i: (0, i)))


def rates_of(reset, rates):
    kept = 1.0 - reset[0].astype(F32)
    return kept, rates[0:1, HEADS : HEADS + 1], rates[0:1, HEADS + 1 : HEADS + 2]


def my_place():
    me = lax.axis_index("narrow")
    return me, me & 1


def wide_bit(place):
    return (lax.axis_index("wide") >> place) & 1


def span(index, width):
    return pl.ds(pl.multiple_of(index * width, width), width)


def gain_row(ref):
    g = ref[...].astype(F32)
    return jnp.concatenate([g[i : i + 1] for i in range(g.shape[0])], 1)


def silu_slope(pre, sig):
    return sig * (1.0 + pre * (1.0 - sig))


def head_columns():
    head = lax.broadcasted_iota(jnp.int32, (128, D), 0)
    feat = lax.broadcasted_iota(jnp.int32, (128, D), 1) // HD
    return (head == feat).astype(F32).astype(LOW)


def two_terms(v):
    high = v.astype(LOW)
    return high, (v - high.astype(F32)).astype(LOW)


def widen(gates, columns):
    high, rest = two_terms(gates)
    return dot_nn(high, columns) + dot_nn(rest, columns)


def narrow_heads(v, columns):
    high, rest = two_terms(v)
    return dot_nt(high, columns) + dot_nt(rest, columns)


def halves(terms, core):
    run_ref, far, near, near_far = terms
    for a, b, which in ((run_ref, far, core), (near, near_far, 1 - core)):
        yield span(which, CH // 2), a[...].astype(F32) + b[...].astype(F32)


def put_halves(keep, sends, v_ref, core):
    rows = CH // 2
    keep[...] = v_ref[span(core, rows), :].astype(LOW)
    part = rows // len(sends)
    for i, send in enumerate(sends):
        send[...] = v_ref[pl.ds(pl.multiple_of((1 - core) * rows + i * part, part), part), :].astype(LOW)


def put_columns(keep, send, v_ref, core, width, rows=None):
    for i in range(2):
        own = v_ref[:, span(2 * i + core, width)].astype(LOW)
        other = v_ref[:, span(2 * i + 1 - core, width)].astype(LOW)
        if rows is None:
            keep[i] = own
            send[i] = other
        else:
            keep[i, rows, :] = own
            send[i, rows, :] = other


def add_to(acc, first, v):
    @pl.when(first)
    def _():
        acc[...] = v

    @pl.when(jnp.logical_not(first))
    def _():
        acc[...] += v


def halves_out(parts=1):
    return [out_full((CH // 2, D), LOW)] + [out_full((CH // 2 // parts, D), LOW) for _ in range(parts)]


def scratch_half():
    return pltpu.VMEM((CH, D), F32)


def mem1_kernel(kv0, kv1, kv2, kv3, w_in, w_out, q, kc, vc, hk, ks, kcv, keep, *rest):
    step = pl.program_id(0)
    *sends, acc = rest
    me, core = my_place()
    width = kv0.shape[2]

    @pl.when(step == 0)
    def _():
        for r, part in enumerate((kv0, kv1, kv2, kv3)):
            cols = span(me ^ r, width)
            q[:, cols] = part[0]
            kc[:, cols] = part[1]
            vc[:, cols] = part[2]

    pre = dot_nn(kc[...], w_in[...])
    sig = jax.nn.sigmoid(pre)
    hidden = (pre * sig).astype(LOW)
    hk[...] = hidden
    ks[...] = silu_slope(pre, sig).astype(LOW)
    kcv[...] = (sig * (1.0 - sig) * (2.0 + pre * (1.0 - 2.0 * sig))).astype(LOW)
    add_to(acc, step == 0, dot_nn(hidden, w_out[...]))

    @pl.when(step == STEPS - 1)
    def _():
        put_halves(keep, sends, acc, core)


def mem1(parts, mem_in, mem_out):
    units = mem_in.shape[1]
    chunk = units // STEPS
    return run(
        "mem1", mem1_kernel, STEPS,
        [] + [full(p) for p in parts] + [cols_of(mem_in, chunk), rows_of(mem_out, chunk)],
        [near(out_full((CH, D), LOW)) for _ in range(3)]
        + [near(out_cols(CH, units, LOW, chunk)) for _ in range(3)] + halves_out(4),
        [scratch_half()], 8.4,
    )


def recall1_kernel(q, gates, att, w_o, w_in, w_out, hid, slope, rec, keep, send, acc):
    step = pl.program_id(0)
    core = my_place()[1]
    pre = dot_nn(q[...], w_in[...])
    sig = jax.nn.sigmoid(pre)
    hidden = (pre * sig).astype(LOW)
    hid[...] = hidden
    slope[...] = silu_slope(pre, sig).astype(LOW)
    add_to(acc, step == 0, dot_nn(hidden, w_out[...]))

    @pl.when(step == STEPS - 1)
    def _():
        rec[...] = acc[...].astype(LOW)
        acc[...] = acc[...] * widen(gates[...], head_columns()) + dot_nn(att[...], w_o[...])
        put_halves(keep, [send], acc, core)


def recall1(q, gates, attended, w_o, mem_in, mem_out):
    units = mem_in.shape[1]
    chunk = units // STEPS
    return run(
        "recall1", recall1_kernel, STEPS,
        [] + [full(q), half_of(gates, 0), half_of(attended, 0), full(w_o), cols_of(mem_in, chunk), rows_of(mem_out, chunk)],
        [far(out_cols(CH, units, LOW, chunk)), far(out_cols(CH, units, LOW, chunk)),
         far(out_full((CH, D), LOW))]
        + halves_out(),
        [scratch_half()], 9.6,
    )


def mem2_kernel(
    reset, rates, s0, s1, s2, s3, q0, q1, q2, q3, vc, kc, hk, ks, kcv, gates, att, w_o, w_in, w_out,
    q, err, slope_low, bcurve, m_in, m_out, hid, slope, rec, keep, send, acc,
):
    step = pl.program_id(0)
    me, core = my_place()
    kept, decay, rate = rates_of(reset, rates)

    @pl.when(step == 0)
    def _():
        for r, part in enumerate((q0, q1, q2, q3)):
            q[:, span(me ^ r, part.shape[1])] = part[...]
        for rows, total in halves((s0, s1, s2, s3), core):
            err[rows, :] = (total - vc[rows, :].astype(F32)).astype(LOW)

    back = dot_nt(err[...], w_out[...])
    slopes = (back * ks[...].astype(F32)).astype(LOW)
    slope_low[...] = slopes
    bcurve[...] = (back * kcv[...].astype(F32)).astype(LOW)
    retain = 1.0 - kept * decay
    take_in = kept * rate * (STEP_IN / CH)
    take_out = kept * rate * (STEP_OUT / CH)
    now_in = (w_in[...].astype(F32) * retain - take_in * dot_tn(kc[...], slopes)).astype(LOW)
    m_in[...] = now_in
    pre = dot_nn(q[...], now_in)
    sig = jax.nn.sigmoid(pre)
    hidden = (pre * sig).astype(LOW)
    hid[...] = hidden
    slope[...] = silu_slope(pre, sig).astype(LOW)
    now_out = (w_out[...].astype(F32) * retain - take_out * dot_tn(hk[...], err[...])).astype(LOW)
    m_out[...] = now_out
    add_to(acc, step == 0, dot_nn(hidden, now_out))

    @pl.when(step == STEPS - 1)
    def _():
        rec[...] = acc[...].astype(LOW)
        acc[...] = acc[...] * widen(gates[...], head_columns()) + dot_nn(att[...], w_o[...])
        put_halves(keep, [send], acc, core)


def mem2(reset, rates, terms, q_parts, vc, kc, hk, ks, kcv, gates, attended, w_o, mem_in, mem_out):
    units = mem_in.shape[1]
    chunk = units // STEPS
    piece = far(out_cols(CH, units, LOW, chunk))
    return run(
        "mem2", mem2_kernel, STEPS,
        [(reset, SMEM_SPEC), full(rates), *[full(t) for t in terms],
         *[full(p) for p in q_parts], full(vc), full(kc), cols_of(hk, chunk),
         cols_of(ks, chunk), cols_of(kcv, chunk), half_of(gates, 1), half_of(attended, 1), full(w_o),
         cols_of(mem_in, chunk), rows_of(mem_out, chunk)],
        [near(out_full((CH, D), LOW)), near(out_full((CH, D), LOW)), piece, piece, far(out_cols(D, units, LOW, chunk)),
         far(((units, D), LOW, pl.BlockSpec((chunk, D), lambda i: (i, 0)))), piece, piece, far(out_full((CH, D), LOW))]
        + halves_out(),
        [scratch_half()], 15.0,
    )


def feed_kernel(
    s0, s1, s2, s3, x, gain, w_up, w_down, c0, c1, c2, c3,
    normed, cot, hid, gg, gu, fkeep, fsend, midloc, gain_part, keep, send, mid, acc_out, acc_norm,
):
    step = pl.program_id(0)
    me, core = my_place()
    width = c0.shape[1]

    @pl.when(step == 0)
    def _():
        for r, part in enumerate((c0, c1, c2, c3)):
            cot[:, span(me ^ r, width)] = part[...]
        for rows, total in halves((s0, s1, s2, s3), core):
            middle = x[rows, :].astype(F32) + total
            mid[rows, :] = middle
            inverse = lax.rsqrt(jnp.mean(middle * middle, -1, keepdims=True) + EPS)
            normed[rows, :] = (middle * inverse * gain_row(gain)).astype(LOW)

    gate_val = dot_nn(normed[...], w_up[0])
    up_val = dot_nn(normed[...], w_up[1])
    grad_hid = dot_nt(cot[...], w_down[...])
    sig = jax.nn.sigmoid(gate_val)
    act = gate_val * sig
    hidden = (act * up_val).astype(LOW)
    hid[...] = hidden
    grad_gate = (grad_hid * up_val * silu_slope(gate_val, sig)).astype(LOW)
    grad_up = (grad_hid * act).astype(LOW)
    gg[...] = grad_gate
    gu[...] = grad_up
    add_to(acc_norm, step == 0, dot_nt(grad_gate, w_up[0]) + dot_nt(grad_up, w_up[1]))
    add_to(acc_out, step == 0, dot_nn(hidden, w_down[...]))

    @pl.when(step == STEPS - 1)
    def _():
        put_columns(fkeep, fsend, acc_out, core, width)
        midloc[...] = mid[:, span(me, width)]
        total = jnp.zeros((1, D), F32)
        for part in range(2):
            rows = pl.ds(part * (CH // 2), CH // 2)
            middle = mid[rows, :]
            inverse = lax.rsqrt(jnp.mean(middle * middle, -1, keepdims=True) + EPS)
            unit = middle * inverse
            grad = acc_norm[rows, :]
            total = total + jnp.sum(grad * unit, 0, keepdims=True)
            acc_norm[rows, :] = norm_back(grad, unit, inverse, gain_row(gain))
        gain_part[...] = total
        put_halves(keep, [send], acc_norm, core)


def feed(half, terms, tokens, gain, w_gate_up, w_down, cot_parts, held=()):
    units = w_down.shape[0]
    chunk = units // STEPS
    width = cot_parts[0].shape[1]
    piece = near(out_cols(CH, units, LOW, chunk))
    quarter = ((2, LEN, width), LOW, pl.BlockSpec((2, CH, width), lambda i: (0, half, 0)))
    return run(
        "feed" + str(half), feed_kernel, STEPS,
        [*[full(t) for t in terms], half_of(tokens, half), full(gain),
         (w_gate_up, pl.BlockSpec((2, D, chunk), lambda i: (0, 0, i))), rows_of(w_down, chunk)]
        + [half_of(p, half) for p in cot_parts],
        [near(out_full((CH, D), LOW)), near(out_full((CH, D), LOW)), piece, piece, piece, quarter, quarter,
         far(out_full((CH, width), F32)), far(out_full((1, D), F32))] + halves_out(),
        [scratch_half(), scratch_half(), scratch_half()], 15.0, held, {0: 5, 1: 6} if held else {},
    )


ROW_STEPS = 4


def put_rows(keep, send, v, bit, size, place):
    block = D // size
    v = v.reshape(v.shape[0] // (2 * block << place), 2, 1 << place, block, v.shape[1])
    shape = (v.shape[0] << place, block, v.shape[4])
    keep[...] = jnp.where(bit == 0, v[:, 0], v[:, 1]).astype(LOW).reshape(shape)
    send[...] = jnp.where(bit == 0, v[:, 1], v[:, 0]).astype(LOW).reshape(shape)


def put_col_blocks(keep, send, v, bit, size, place):
    block = D // size
    for i in range(size // 2):
        first = ((i >> place) << (place + 1)) | (i & ((1 << place) - 1))
        second = first | (1 << place)
        zero = v[:, first * block : (first + 1) * block]
        one = v[:, second * block : (second + 1) * block]
        keep[i] = jnp.where(bit == 0, zero, one).astype(LOW)
        send[i] = jnp.where(bit == 0, one, zero).astype(LOW)


def row_out(size, units, steps):
    block = D // size
    return ((size // 2, block, units), LOW, pl.BlockSpec((size // 2 // steps, block, units), lambda i: (i, 0, 0)))


def col_out(size, units):
    block = D // size
    return ((size // 2, units, block), LOW, pl.BlockSpec((size // 2, units // ROW_STEPS, block), lambda i: (0, i, 0)))


def feed_weights_kernel(size, na, nb, gga, ggb, gua, gub, ca, cb, ha, hb, ukeep, usend, dkeep, dsend):
    bit = wide_bit(0)
    for which, (a, b) in enumerate(((gga, ggb), (gua, gub))):
        v = dot_tn(na[...], a[...]) + dot_tn(nb[...], b[...])
        put_rows(ukeep.at[:, which], usend.at[:, which], v, bit, size, 0)
    v = dot_tn(ha[...], ca[...]) + dot_tn(hb[...], cb[...])
    put_col_blocks(dkeep, dsend, v, wide_bit(1), size, 1)


def feed_weights(size, na, nb, gga, ggb, gua, gub, ca, cb, ha, hb):
    units = ha.shape[1]
    block = D // ROW_STEPS
    rows = D // size
    per = block // rows
    half = ((size // 2, 2, rows, units), LOW, pl.BlockSpec((per // 2, 2, rows, units), lambda i: (i, 0, 0, 0)))
    cols = col_out(size, units)
    return run(
        "feed_weights", lambda *refs: feed_weights_kernel(size, *refs), ROW_STEPS,
        [cols_of(na, block), cols_of(nb, block), full(gga), full(ggb), full(gua), full(gub), full(ca), full(cb),
         cols_of(ha, units // ROW_STEPS), cols_of(hb, units // ROW_STEPS)],
        [far(half), far(half), far(cols), far(cols)], (), 11.7, room=0 if rows >= 128 else 24,
    )


def mid_grad(terms, cot, core, grad):
    for rows, total in halves(terms, core):
        grad[rows, :] = total + cot[rows, :].astype(F32)


def gate_side(gates, rec, grad, low, loc, head_grad, recall_grad, me, width):
    columns = head_columns()
    gates = gates[...]
    terms = narrow_heads(rec[...].astype(F32) * grad[...], columns)
    head_grad[...] = terms * gates * (1.0 - gates)
    recall_grad[...] = (widen(gates, columns) * grad[...]).astype(LOW)
    low[...] = grad[...].astype(LOW)
    loc[...] = grad[:, span(me, width)]


def recall1_back_kernel(
    s0, s1, s2, s3, cot, gates, rec, hid, slope, q, w_in, w_out,
    low, loc, head_grad, g_in, g_out, dq, grad, rgrad,
):
    step = pl.program_id(0)
    me, core = my_place()

    @pl.when(step == 0)
    def _():
        mid_grad((s0, s1, s2, s3), cot, core, grad)
        gate_side(gates, rec, grad, low, loc, head_grad, rgrad, me, loc.shape[1])

    rg = rgrad[...]
    dpre = (dot_nt(rg, w_out[...]) * slope[...].astype(F32)).astype(LOW)
    g_out[...] = dot_tn(hid[...], rg).astype(LOW)
    g_in[...] = dot_tn(q[...], dpre).astype(LOW)
    add_to(dq, step == 0, dot_nt(dpre, w_in[...]))


def recall1_back(width, terms, cot, gates, rec, hid, slope, q, mem_in, mem_out):
    units = mem_in.shape[1]
    chunk = units // STEPS
    return run(
        "recall1_back", recall1_back_kernel, STEPS,
        [*[full(t) for t in terms], full(cot), half_of(gates, 0), full(rec), cols_of(hid, chunk),
         cols_of(slope, chunk), full(q), cols_of(mem_in, chunk), rows_of(mem_out, chunk)],
        [near(out_full((CH, D), LOW)), far(out_full((CH, width), F32)), far(out_full((CH, 128), F32)),
         far(out_cols(D, units, LOW, chunk)), far(((units, D), LOW, pl.BlockSpec((chunk, D), lambda i: (i, 0)))),
         near(out_full((CH, D), F32))],
        [scratch_half(), pltpu.VMEM((CH, D), LOW)], 12.2,
    )


def mem2_back_kernel(
    reset, rates, s0, s1, s2, s3, cot, gates, rec, hid, slope, q, m_in, m_out, kc, hk, ks, bcurve, slope_low, w_in, w_out,
    low, loc, head_grad, d_in, d_out, dpre_out, dback, gsb, sums, keep, *rest,
):
    step = pl.program_id(0)
    *sends, grad, rgrad, acc = rest
    me, core = my_place()
    kept, _, rate = rates_of(reset, rates)

    @pl.when(step == 0)
    def _():
        mid_grad((s0, s1, s2, s3), cot, core, grad)
        gate_side(gates, rec, grad, low, loc, head_grad, rgrad, me, loc.shape[1])

    rg = rgrad[...]
    dpre = (dot_nt(rg, m_out[...]) * slope[...].astype(F32)).astype(LOW)
    dpre_out[...] = dpre
    dm_out = dot_tn(hid[...], rg)
    dm_out_low = dm_out.astype(LOW)
    d_out[...] = dm_out_low
    dm_in = dot_tn(q[...], dpre)
    dm_in_low = dm_in.astype(LOW)
    d_in[...] = dm_in_low
    decayed = jnp.sum(w_in[...].astype(F32) * dm_in, 0, keepdims=True)
    decayed_out = jnp.sum(w_out[...].astype(F32) * dm_out, 0, keepdims=True)
    t_in = dot_nn(kc[...], dm_in_low)
    stepped = jnp.sum(slope_low[...].astype(F32) * t_in, 0, keepdims=True)
    grad_slope = t_in * (-kept * rate * (STEP_IN / CH))
    gsb[...] = (grad_slope * bcurve[...].astype(F32)).astype(LOW)
    db = (grad_slope * ks[...].astype(F32)).astype(LOW)
    dback[...] = db
    sums[0:1, :] = decayed
    sums[1:2, :] = stepped
    chunk = decayed.shape[1]
    sums[2:3, :] = sum(decayed_out[:, i * chunk : (i + 1) * chunk] for i in range(decayed_out.shape[1] // chunk))
    add_to(
        acc, step == 0,
        dot_nn(hk[...], dm_out_low) * (-kept * rate * (STEP_OUT / CH)) + dot_nn(db, w_out[...]),
    )

    @pl.when(step == STEPS - 1)
    def _():
        put_halves(keep, sends, acc, core)


def mem2_back(
    width, reset, rates, terms, cot, gates, rec, hid, slope, q, m_in, m_out, kc, hk, ks, bcurve, slope_low,
    mem_in, mem_out,
):
    units = mem_in.shape[1]
    chunk = units // STEPS
    piece = near(out_cols(CH, units, LOW, chunk))
    return run(
        "mem2_back", mem2_back_kernel, STEPS,
        [(reset, SMEM_SPEC), full(rates), *[full(t) for t in terms], full(cot), half_of(gates, 1), full(rec),
         cols_of(hid, chunk), cols_of(slope, chunk), full(q), cols_of(m_in, chunk), rows_of(m_out, chunk),
         full(kc), cols_of(hk, chunk), cols_of(ks, chunk), cols_of(bcurve, chunk), cols_of(slope_low, chunk),
         cols_of(mem_in, chunk), rows_of(mem_out, chunk)],
        [near(out_full((CH, D), LOW)), far(out_full((CH, width), F32)), far(out_full((CH, 128), F32)),
         near(out_cols(D, units, LOW, chunk)), near(((units, D), LOW, pl.BlockSpec((chunk, D), lambda i: (i, 0)))),
         piece, piece, piece, far(out_cols(3, units, F32, chunk))] + halves_out(2),
        [scratch_half(), pltpu.VMEM((CH, D), LOW), scratch_half()], 18.0,
    )


def mem2_late_kernel(reset, rates, err, hk, ks, gsb, slope_low, d_in, d_out, dpre, m_in, base, sums, dq, dk):
    step = pl.program_id(0)
    kept, _, rate = rates_of(reset, rates)
    t_out = dot_nt(err[...], d_out[...])
    sums[...] = jnp.sum(hk[...].astype(F32) * t_out, 0, keepdims=True)
    base[...] = (t_out * (-kept * rate * (STEP_OUT / CH)) * ks[...].astype(F32) + gsb[...].astype(F32)).astype(LOW)
    add_to(dk, step == 0, dot_nt(slope_low[...], d_in[...]) * (-kept * rate * (STEP_IN / CH)))
    add_to(dq, step == 0, dot_nt(dpre[...], m_in[...]))


def mem2_late(reset, rates, err, hk, ks, gsb, slope_low, d_in, d_out, dpre, m_in):
    units = hk.shape[1]
    chunk = units // STEPS
    return run(
        "mem2_late", mem2_late_kernel, STEPS,
        [(reset, SMEM_SPEC), full(rates), full(err), cols_of(hk, chunk), cols_of(ks, chunk), cols_of(gsb, chunk),
         cols_of(slope_low, chunk), cols_of(d_in, chunk), rows_of(d_out, chunk), cols_of(dpre, chunk),
         cols_of(m_in, chunk)],
        [near(out_cols(CH, units, LOW, chunk)), far(out_cols(1, units, F32, chunk)), near(out_full((CH, D), F32)),
         near(out_full((CH, D), F32))],
        (), 10.6,
    )


def query_split_kernel(reset, n, gates, heads_a, heads_b, sums, sums_out, dq1, dq2, keep, send_a, send_b, heads, small):
    core = my_place()[1]
    width = keep.shape[2]
    for part, (ref, send) in enumerate(((dq1, send_a), (dq2, send_b))):
        for i in range(2):
            keep[i, pl.ds(part * CH, CH), :] = ref[:, span(2 * i + core, width)].astype(LOW)
            send[i] = ref[:, span(2 * i + 1 - core, width)].astype(LOW)
    kept = 1.0 - reset[0].astype(F32)
    decay_part = jnp.sum(sums[0:1, :] + sums[2:3, :], 1, keepdims=True) * (-kept / CH)
    step_part = jnp.sum(STEP_IN * sums[1:2, :] + STEP_OUT * sums_out[...], 1, keepdims=True) * (-kept / (CH * CH))
    lane = lax.broadcasted_iota(jnp.int32, (1, 128), 1)
    logit = jnp.where(lane == HEADS, decay_part, 0.0) + jnp.where(lane == HEADS + 1, step_part, 0.0)
    g = gates[...]
    heads[:CH, :] = (heads_a[...] + g * (1.0 - g) * logit).astype(LOW)
    heads[CH:, :] = heads_b[...].astype(LOW)
    small[...] = dot_tn(heads[...], n[...])


def query_split(width, reset, normed, gates, heads_a, heads_b, sums, sums_out, dq1, dq2):
    quarter = out_full((2, LEN, width), LOW)
    half = out_full((2, CH, width), LOW)
    return run(
        "query_split", query_split_kernel, 1,
        [(reset, SMEM_SPEC), full(normed), half_of(gates, 0), full(heads_a), full(heads_b), full(sums), full(sums_out),
         full(dq1), full(dq2)],
        [quarter, half, half, out_full((LEN, 128), LOW), out_full((128, D), F32)], (), 5.0,
    )


def mem1_back_kernel(s0, s1, s2, s3, ks, base, dk, w_in, w_out, dpred, dpre_out, vshare, keep, send_a, send_b, acc):
    step = pl.program_id(0)
    me, core = my_place()
    width = vshare.shape[1]

    @pl.when(step == 0)
    def _():
        for rows, total in halves((s0, s1, s2, s3), core):
            dpred[rows, :] = total.astype(LOW)
        vshare[...] = -dpred[:, span(me, width)].astype(F32)
        acc[...] = dk[...]

    dpre = (dot_nt(dpred[...], w_out[...]) * ks[...].astype(F32) + base[...].astype(F32)).astype(LOW)
    dpre_out[...] = dpre
    acc[...] += dot_nt(dpre, w_in[...])

    @pl.when(step == STEPS - 1)
    def _():
        for i in range(2):
            keep[i] = acc[:, span(2 * i + core, width)].astype(LOW)
            away = acc[:, span(2 * i + 1 - core, width)].astype(LOW)
            send_a[i] = away[: CH // 2]
            send_b[i] = away[CH // 2 :]


def mem1_back(width, terms, ks, base, dk, mem_in, mem_out):
    units = mem_in.shape[1]
    chunk = units // STEPS
    quarter = out_full((2, CH, width), LOW)
    half = out_full((2, CH // 2, width), LOW)
    return run(
        "mem1_back", mem1_back_kernel, STEPS,
        [*[full(t) for t in terms], cols_of(ks, chunk), cols_of(base, chunk), full(dk),
         cols_of(mem_in, chunk), rows_of(mem_out, chunk)],
        [near(out_full((CH, D), LOW)), near(out_cols(CH, units, LOW, chunk)), far(out_full((CH, width), F32)), quarter,
         half, half],
        [scratch_half()], 7.2,
    )


def mem_weights_kernel(size, reset, rates, g_in, g_out, d_in, d_out, kc, dpre, dback, err, hk, dpred, ikeep, isend, okeep, osend):
    bit = wide_bit(0)
    kept, decay, _ = rates_of(reset, rates)
    retain = 1.0 - kept * decay
    v = g_in[...].astype(F32) + retain * d_in[...].astype(F32) + dot_tn(kc[...], dpre[...])
    put_rows(ikeep, isend, v, bit, size, 0)
    v = (
        g_out[...].astype(F32) + retain * d_out[...].astype(F32)
        + dot_tn(dback[...], err[...]) + dot_tn(hk[...], dpred[...])
    )
    put_col_blocks(okeep, osend, v, bit, size, 0)


def mem_weights(size, reset, rates, g_in, g_out, d_in, d_out, kc, dpre, dback, err, hk, dpred):
    units = hk.shape[1]
    block = D // ROW_STEPS
    unit_block = units // ROW_STEPS
    r, c = row_out(size, units, ROW_STEPS), col_out(size, units)
    return run(
        "mem_weights", lambda *refs: mem_weights_kernel(size, *refs), ROW_STEPS,
        [(reset, SMEM_SPEC), full(rates), rows_of(g_in, block), rows_of(g_out, unit_block), rows_of(d_in, block),
         rows_of(d_out, unit_block), cols_of(kc, block), full(dpre), cols_of(dback, unit_block), full(err),
         cols_of(hk, unit_block), full(dpred)],
        [r, r, c, c], (), 9.4, room=0 if D // size >= 128 else 24,
    )


def weights_kernel(size, n, gma, gmb, att, gq, gk, gv, akeep, asend, bkeep, bsend):
    v_out = dot_tn(gma[...], att[:CH, :]) + dot_tn(gmb[...], att[CH:, :])
    v = jnp.concatenate([v_out, dot_tn(n[...], gv[...])], 1)
    put_rows(akeep, asend, v, wide_bit(0), size, 0)
    v = dot_tn(n[...], jnp.concatenate([gq[...], gk[...]], 1))
    put_rows(bkeep, bsend, v, wide_bit(0), size, 0)


def weights(size, normed, gma, gmb, attended, gq, gk, gv):
    r = row_out(size, 2 * gq.shape[1], 2)
    block = D // 2
    return run(
        "weights", lambda *refs: weights_kernel(size, *refs), 2,
        [cols_of(normed, block), cols_of(gma, block), cols_of(gmb, block), full(attended), full(gq), full(gk), full(gv)],
        [r, r, r, r], (), 9.0, room=4,
    )


def last_kernel(gq, gk, gv, w, heads, gate_t, decay_t, x, gain, keep, send_a, send_b, gain_part):
    step = pl.program_id(0)
    core = my_place()[1]
    width = gq.shape[1]
    grad = dot_nn(heads[:, :HEADS], gate_t[...]) + dot_nn(heads[:, HEADS : HEADS + 2], decay_t[...])
    for i, ref in enumerate((gq, gk, gv)):
        grad = grad + dot_nt(ref[...], w[i])
    xf = x[...].astype(F32)
    inverse = lax.rsqrt(jnp.mean(xf * xf, -1, keepdims=True) + EPS)
    unit = xf * inverse
    add_to(gain_part, step == 0, jnp.sum(grad * unit, 0, keepdims=True))
    back = norm_back(grad, unit, inverse, gain_row(gain)).astype(LOW)
    for i in range(2):
        blocks = [back[:, (2 * i + b) * width : (2 * i + b + 1) * width] for b in range(2)]
        keep[i] = jnp.where(core == 0, blocks[0], blocks[1])
        away = jnp.where(core == 0, blocks[1], blocks[0])
        for part, send in enumerate((send_a, send_b)):

            @pl.when(step // 2 == part)
            def _():
                send[i] = away


def last(gq, gk, gv, w_t, heads, gate_t, decay_t, tokens, gain):
    width = gq.shape[1]
    rows = LEN // 4
    quarter = ((2, LEN, width), LOW, pl.BlockSpec((2, rows, width), lambda i: (0, i, 0)))


    def send(part):
        at = (lambda i: (0, jnp.minimum(i, 1), 0)) if part == 0 else (lambda i: (0, jnp.maximum(i - 2, 0), 0))
        return ((2, CH, width), LOW, pl.BlockSpec((2, rows, width), at))

    return run(
        "last", last_kernel, 4,
        [rows_of(gq, rows), rows_of(gk, rows), rows_of(gv, rows), full(w_t), rows_of(heads, rows),
         full(gate_t), full(decay_t), rows_of(tokens, rows), full(gain)],
        [quarter, send(0), send(1), out_full((1, D), F32)],
        (), 8.5,
    )


def attend_back_kernel(
    doc_ref, q_ref, k_ref, v_ref, pk_ref, pv_ref, gma, gmb, wo_ref, peak_ref, inv_ref,
    dq_ref, dk_ref, dv_ref, dpk_ref, dpv_ref, go_ref,
):
    k = k_ref[0]
    v = v_ref[0]
    keys_t = flat(k)
    pk = pk_ref[0]
    pv = pv_ref[0]
    pk_t = flat(pk)
    for ref in (dk_ref, dv_ref, dpk_ref, dpv_ref):
        ref[...] = jnp.zeros_like(ref)
    for half, gm in enumerate((gma, gmb)):
        rows = pl.ds(half * CH, CH)
        go_ref[rows, :] = dot_nt(gm[...], wo_ref[...]).astype(LOW)
    for block in range(LEN // QB):
        low_key, high_key = key_range(block)
        keys = pl.ds(low_key, high_key - low_key)
        rows = pl.ds(block * QB, QB)
        ok = allowed(doc_ref, block, low_key, high_key)
        q = q_ref[0, rows, :].astype(F32)
        go = go_ref[rows, :].astype(F32)
        outs = []
        for index in range(2):
            q_head = scaled_head(q, index)
            go_head = one_head(go, index)
            peak = peak_ref[0, index : index + 1, rows]
            inv = inv_ref[0, index : index + 1, rows]
            s = jnp.where(ok, dot_nt(k[low_key:high_key], q_head), NEG)
            sp = dot_nt(pk, q_head)
            prob = jnp.exp(s - peak) * inv
            prob_p = jnp.exp(sp - peak) * inv
            gp = dot_nt(v[low_key:high_key], go_head)
            gpp = dot_nt(pv, go_head)
            center = jnp.sum(prob * gp, 0, keepdims=True) + jnp.sum(prob_p * gpp, 0, keepdims=True)
            gs = (prob * (gp - center)).astype(LOW)
            gsp = (prob_p * (gpp - center)).astype(LOW)
            dk_ref[keys, :] += dot_nn(gs, q_head)
            dv_ref[keys, :] += dot_nn(prob.astype(LOW), go_head)
            dpk_ref[...] += dot_nn(gsp, q_head)
            dpv_ref[...] += dot_nn(prob_p.astype(LOW), go_head)
            feats = slice(index * HD, index * HD + HD)
            outs.append(dot_nn(keys_t[feats, low_key:high_key], gs) + dot_nn(pk_t[feats], gsp))
        dq_ref[rows, :] = jnp.concatenate(outs, 0).T * 8.0


def attend_back(doc_len, act, persistent, gma, gmb, w_o, peak, inv):
    width = act.shape[2]
    pairs = width // 128

    def part(i):
        return (act, pl.BlockSpec((1, LEN, 128), lambda g: (i, 0, g)))

    def pers(i):
        return (persistent, pl.BlockSpec((1, NP, 128), lambda g: (i, 0, g)))

    stat = pl.BlockSpec((1, 2, LEN), lambda g: (g, 0, 0))
    cols = near(((LEN, width), F32, pl.BlockSpec((LEN, 128), lambda g: (0, g))))
    small = far(((NP, width), F32, pl.BlockSpec((NP, 128), lambda g: (0, g))))
    return run(
        "attend_back", attend_back_kernel, pairs,
        [(doc_len, SMEM_SPEC), part(0), part(1), part(2), pers(0), pers(1), full(gma), full(gmb),
         rows_of(w_o, 128), (peak, stat), (inv, stat)],
        [cols, cols, cols, small, small],
        [pltpu.VMEM((LEN, 128), LOW)], 15.6,
    )


def conv_back_kernel(part, count, doc_ref, p_ref, taps_ref, datt_ref, *refs):
    extra, (gproj_ref, gtaps_ref, pad, padc) = refs[:count], refs[count:]
    width = p_ref.shape[2]
    pad[pl.ds(0, 8), :] = jnp.zeros((8, width), F32)
    padc[pl.ds(LEN, 8), :] = jnp.zeros((8, width), F32)
    pad[pl.ds(8, LEN), :] = p_ref[0]
    gt = [jnp.zeros((1, width), F32)] * KC
    ones_mat = same_head(width)
    for first in range(0, LEN, PRE_ROWS):
        rows = pl.ds(first, PRE_ROWS)
        age = ages(doc_ref, first, PRE_ROWS, width)
        c = conv_sum(pad, taps_ref, age, first, PRE_ROWS)
        sig = jax.nn.sigmoid(c)
        dy = datt_ref[rows, :]
        for ref in extra:
            if first < ref.shape[0]:
                dy = dy + ref[rows, :].astype(F32)
        if part < 2:
            a = c * sig
            inverse = lax.rsqrt(head_sum(a * a, ones_mat) + EPS)
            y = a * inverse
            dy = inverse * (dy - y * head_sum(dy * y, ones_mat))
        dc = dy * silu_slope(c, sig)
        padc[rows, :] = dc
        gt[0] = gt[0] + jnp.sum(dc * pad[pl.ds(first + 8, PRE_ROWS), :], 0, keepdims=True)
        for i in range(1, KC):
            shifted = jnp.where(age >= i, pad[pl.ds(first + 8 - i, PRE_ROWS), :], 0.0)
            gt[i] = gt[i] + jnp.sum(dc * shifted, 0, keepdims=True)
    gtaps_ref[...] = jnp.concatenate(gt, 0)
    for first in range(0, LEN, PRE_ROWS):
        total = taps_ref[0, 0:1, :].astype(F32) * padc[pl.ds(first, PRE_ROWS), :]
        for i in range(1, KC):
            age = ages(doc_ref, first + i, PRE_ROWS, width)
            total = total + taps_ref[0, i : i + 1, :].astype(F32) * jnp.where(
                age >= i, padc[pl.ds(first + i, PRE_ROWS), :], 0.0
            )
        gproj_ref[pl.ds(first, PRE_ROWS), :] = total.astype(LOW)


def conv_back(part, doc_len, p, taps, datt, extra):
    width = p.shape[2]
    count = len(extra)
    return run(
        "conv_back" + str(part), lambda *refs: conv_back_kernel(part, count, *refs), 1,
        [(doc_len, SMEM_SPEC), (p, pl.BlockSpec((1, LEN, width), lambda i: (part, 0, 0))),
         (taps, pl.BlockSpec((1, KC, width), lambda i: (part, 0, 0))), full(datt)] + [full(e) for e in extra],
        [near(out_full((LEN, width), LOW)), far(out_full((KC, width), F32))],
        [pltpu.VMEM((LEN + 8, width), F32), pltpu.VMEM((LEN + 8, width), F32)], 6.5,
    )


def body(
    tokens,
    gain_in,
    gain_mid,
    w_qkv,
    w_gate,
    w_decay,
    conv_kernel,
    persistent,
    w_out,
    mem_in,
    mem_out,
    w_up,
    w_down,
    doc_len,
    reset,
    cotangent,
):
    assert doc_len.shape[0] == 1 and lax.axis_size("narrow") == 4
    width = w_qkv.shape[2]
    size = lax.axis_size("wide")
    me = lax.axis_index("narrow")
    gain_in_f, gain_mid_f = gain_in.reshape(-1, 128), gain_mid.reshape(-1, 128)
    w_t = w_qkv.transpose(1, 0, 2)
    taps = conv_kernel
    gate_t, decay_t = w_gate.T, w_decay.T
    LAST.clear()
    PLACED.clear()
    for a in (tokens, w_t, w_out, mem_in, mem_out, w_down, persistent, gain_in_f, gain_mid_f, gate_t, decay_t, taps):
        put(a, pltpu.HBM)
    cot = Parts(cotangent)
    normed_in, gates, rates, projected, act, own_q, own_heads = pre(
        doc_len, tokens, gain_in_f, w_t, gate_t, decay_t, taps
    )

    cot.end()
    heads_in = Parts(own_heads)
    query = Parts(own_q)
    attended, peak, inv = attend(doc_len, act, persistent)
    cot_parts = [put(t, pltpu.HBM) for t in cot.settle()]
    w_gate_up = put(tie(w_up.transpose(1, 0, 2)), pltpu.VMEM)
    mem_in, mem_out, w_down = fetch(mem_in, mem_out, w_down)
    heads_in = heads_in.end()
    q_a, kc, vc, hk, ks, kcv, *pred = mem1(heads_in, mem_in, mem_out)
    pred = Halves(*pred)
    query.end()
    pred.middle()
    hid1, slope1, rec1, *join1 = recall1(q_a, gates, attended, w_out, mem_in, mem_out)
    join1 = Halves(*join1)
    pred = pred.end()
    join1.middle()
    q_parts = query.settle()
    q_b, err, slope_low, bcurve, m_in, m_out, hid2, slope2, rec2, *join2 = mem2(
        reset, rates, pred, q_parts, vc, kc, hk, ks, kcv, gates, attended, w_out, mem_in, mem_out
    )
    join2 = Halves(*join2)
    join1 = join1.end()
    join2.middle()
    na, cota, ha, gga, gua, fkeep, fsend, mloca, gain_a, *mid1 = feed(
        0, join1, tokens, gain_mid_f, w_gate_up, w_down, cot_parts
    )
    mid1 = Halves(*mid1)
    join2 = join2.end()
    mid1.middle()
    nb, cotb, hb, ggb, gub, fkeep, fsend, mlocb, gain_b, *mid2 = feed(
        1, join2, tokens, gain_mid_f, w_gate_up, w_down, cot_parts, (fkeep, fsend)
    )
    mid2 = Halves(*mid2)
    outs = Columns(fkeep, fsend)

    mid1.end()
    mid2.middle()
    mid1_terms = mid1.settle()
    ukeep, usend, dkeep, dsend = feed_weights(size, na, nb, gga, ggb, gua, gub, cota, cotb, ha, hb)
    up_sum = Rows(1, ukeep, usend)
    down_sum = Rows(2, dkeep, dsend)
    mid2 = mid2.end()
    gmb, locb, heads_b, d_in, d_out, dpre2, dback, gsb, sums, *gerr = mem2_back(
        width, reset, rates, mid2, cotb, gates, rec2, hid2, slope2, q_b, m_in, m_out, kc, hk, ks, bcurve, slope_low,
        mem_in, mem_out,
    )
    gerr = Halves(*gerr)
    gerr.middle()
    outs.middle()
    gma, loca, heads_a, g_in, g_out, dq1 = recall1_back(
        width, mid1_terms, cota, gates, rec1, hid1, slope1, q_a, mem_in, mem_out
    )
    down_sum.step()
    gerr.end()
    dq, dka, dva, dpk, dpv = attend_back(doc_len, act, persistent, gma, gmb, w_out, peak, inv)
    outs = outs.end()
    gerr_terms = gerr.settle()
    up_sum.step()
    base, sums_out, dq2, dk = mem2_late(reset, rates, err, hk, ks, gsb, slope_low, d_in, d_out, dpre2, m_in)
    down_sum.step()
    dpred, dpre1, v_share, kkeep, *ksends = mem1_back(width, gerr_terms, ks, base, dk, mem_in, mem_out)
    k_share = Columns(kkeep, *ksends)
    ikeep, isend, okeep, osend = mem_weights(
        size, reset, rates, g_in, g_out, d_in, d_out, kc, dpre1, dback, err, hk, dpred
    )
    in_sum = Rows(1, ikeep, isend)
    back_sum = Rows(1, okeep, osend)
    qkeep, qsend_a, qsend_b, heads, small_part = query_split(
        width, reset, normed_in, gates, heads_a, heads_b, sums, sums_out, dq1, dq2
    )
    q_share = Columns(qkeep, qsend_a, qsend_b)
    down_grads = down_sum.end()
    k_share.middle()
    q_share.middle()
    up_sum.step()
    gv, tap_v = conv_back(2, doc_len, projected, taps, dva, [v_share])
    gk, tap_k = conv_back(1, doc_len, projected, taps, dka, k_share.end())
    in_sum.step()
    gq, tap_q = conv_back(0, doc_len, projected, taps, dq, q_share.end())
    akeep, asend, bkeep, bsend = weights(size, normed_in, gma, gmb, attended, gq, gk, gv)
    w_sum = Rows(1, akeep, asend)
    q_sum = Rows(1, bkeep, bsend)
    up_grads = up_sum.end()
    lkeep, *lsends, gain_part = last(gq, gk, gv, w_t, heads, gate_t, decay_t, tokens, gain_in_f)
    in_share = Columns(lkeep, *lsends)
    own = jnp.concatenate([dpk, dpv], 0).reshape(-1, D)
    taps_part = jnp.concatenate([tap_q, tap_k, tap_v], 0).reshape(-1, D)
    late = jnp.concatenate([own, taps_part, gain_a + gain_b, small_part[: HEADS + 2], gain_part], 0)
    in_sum.step()
    back_sum.step()
    in_share.middle()
    up_grads = pinned(up_grads.transpose(1, 0, 2))
    output = pinned((jnp.concatenate([mloca, mlocb], 0) + outs[0].astype(F32) + outs[1].astype(F32)).astype(LOW))
    w_sum.step()
    late = Small(pinned(late), "wide")
    q_sum.step()
    in_grads = in_sum.end()
    late.step()
    back_sum.step()
    late.step()
    w_sum.step()
    late = late.end()
    late = Small(place_own(late, 2 * NP + 3 * KC, width, me), "narrow")
    q_sum.step()
    late.step()
    in_share = in_share.end()
    grad_input = pinned(in_share[0].astype(F32) + in_share[1].astype(F32) + jnp.concatenate([loca, locb], 0))
    back_grads = back_sum.end()
    late = late.end()
    w_grads = w_sum.end()
    q_grads = q_sum.end()
    pers_sum = late[: 2 * NP].reshape(2, NP, D)
    conv_sum = late[2 * NP : 2 * NP + 3 * KC].reshape(3, KC, D)
    vecs = late[2 * NP + 3 * KC :]
    rows = D // size
    gate_shard = cut(vecs[1 : HEADS + 1], lax.axis_index("wide") * rows, rows, 1).T
    return (
        output,
        grad_input,
        vecs[HEADS + 3],
        vecs[0],
        jnp.stack([q_grads[:, :width], q_grads[:, width:], w_grads[:, width:]], 1),
        gate_shard,
        vecs[HEADS + 1 : HEADS + 3].T,
        conv_sum,
        pers_sum,
        w_grads[:, :width].T,
        in_grads,
        back_grads,
        up_grads,
        down_grads,
    )


def solution(mesh):
    in_specs = (
        P("wide", None),
        P(),
        P(),
        P(None, None, "narrow"),
        P(),
        P(),
        P(None, None, "narrow"),
        P(None, None, "narrow"),
        P("narrow", None),
        P(None, "narrow"),
        P("narrow", None),
        P(None, None, "narrow"),
        P("narrow", None),
        P("wide", None),
        P("wide"),
        P("wide", "narrow"),
    )
    out_specs = (
        P("wide", "narrow"),
        P("wide", "narrow"),
        P(),
        P(),
        P("wide", None, "narrow"),
        P("wide", None),
        P(),
        P(),
        P(),
        P("narrow", "wide"),
        P("wide", "narrow"),
        P("narrow", "wide"),
        P("wide", None, "narrow"),
        P("narrow", "wide"),
    )
    return jax.shard_map(body, mesh=mesh, in_specs=in_specs, out_specs=out_specs, check_vma=False)
```

```python
import jax
import jax.numpy as jnp
from jax import lax
from jax.experimental import pallas as pl
from jax.experimental.pallas import tpu as pltpu
from jax.sharding import PartitionSpec as P

D = 1024
HEADS = 16
HD = 64
LEN = 1024
CH = 512
WIN = 512
NP = 16
KC = 4


EPS = 1e-06
NEG = -1e30
STEP_IN = 128.0
STEP_OUT = 0.5
LOW = jnp.bfloat16
F32 = jnp.float32
VMEM = 12
VMEM_OF = {'pre': 16, 'mem1': 12, 'recall1': 15, 'mem2': 24, 'feed0': 28, 'feed1': 28, 'mem2_back': 32, 'recall1_back': 20, 'mem2_late': 15, 'mem1_back': 12, 'attend_back': 12}


def norm_back(grad_norm, unit_val, inverse, gain_vec):
    scaled = grad_norm * gain_vec
    return inverse * (scaled - unit_val * jnp.mean(scaled * unit_val, -1, keepdims=True))


def flip(v, axis, bit):
    size = lax.axis_size(axis)
    return lax.ppermute(v, axis, [(i, i ^ bit) for i in range(size)])


def bits_of(axis):
    size = lax.axis_size(axis)
    out = []
    bit = 1
    while bit < size:
        out.append(bit)
        bit *= 2
    assert bit == size
    return out


def pick(v, index, axis=0):
    return lax.dynamic_index_in_dim(v, index, axis, keepdims=False)


def cut(v, start, width, axis):
    return lax.dynamic_slice_in_dim(v, start, width, axis)


class Parts:
    def __init__(self, v):
        self.own, self.far, self.near = v, flip(v, "narrow", 2), flip(v, "narrow", 1)

    def end(self):
        far = tie(self.far)
        self.terms = [self.own, tie(self.near), far, flip(far, "narrow", 1)]
        return self.terms

    def settle(self):
        self.terms[3] = tie(self.terms[3])
        return self.terms


class Halves:
    def __init__(self, keep, *sends):
        self.keep, self.come = keep, [flip(send, "narrow", 1) for send in sends]

    def middle(self):
        self.run = fold_rows(self.keep, self.come)
        self.far = flip(self.run, "narrow", 2)
        self.near = flip(self.run, "narrow", 1)

    def end(self):
        far = tie(self.far)
        self.terms = [self.run, far, tie(self.near), flip(far, "narrow", 1)]
        return self.terms

    def settle(self):
        self.terms[3] = tie(self.terms[3])
        return self.terms


class Columns:
    def __init__(self, keep, *sends):
        self.keep, self.come = keep, [flip(send, "narrow", 1) for send in sends]

    def middle(self):
        self.run, away = fold_columns(self.keep, self.come)
        self.far = flip(away, "narrow", 2)

    def end(self):
        return [self.run[0], tie(self.far)[0]]


class Rows:
    def __init__(self, first, keep, send):
        self.keep, self.come = keep, flip(send, "wide", first)
        self.bits = [b for b in bits_of("wide") if b != first]

    def step(self):
        bit = self.bits.pop(0)
        self.keep, away = fold_pick(lambda: wide_bit(bit.bit_length() - 1), self.keep, self.come)
        self.come = flip(away, "wide", bit)

    def end(self):
        while self.bits:
            self.step()
        return fold(self.keep, self.come, F32)[0]


def place_own(v, rows, width, me):
    own = v[: rows * width // D].reshape(rows, width)
    own = lax.dynamic_update_slice(jnp.zeros((rows, D), F32), own, (0, me * width))
    return jnp.concatenate([own, v[rows * width // D :]], 0)


class Small:
    def __init__(self, v, axis):
        self.v = pinned(v)
        self.left = [(axis, b) for b in bits_of(axis)]
        self.send()

    def send(self):
        if self.left:
            self.come = flip(self.v, *self.left.pop(0))

    def step(self):
        self.v = pinned(self.v + tie(self.come))
        self.send()

    def end(self):
        while self.left:
            self.step()
        return self.v + tie(self.come)


def head_sum(v, ones_mat):
    high = v.astype(LOW)
    rest = (v - high.astype(F32)).astype(LOW)
    return jnp.dot(high, ones_mat, preferred_element_type=F32) + jnp.dot(
        rest, ones_mat, preferred_element_type=F32
    )


def same_head(width):
    row = lax.broadcasted_iota(jnp.int32, (width, width), 0) // HD
    col = lax.broadcasted_iota(jnp.int32, (width, width), 1) // HD
    return (row == col).astype(F32).astype(LOW)


def doc_start(doc_ref, places):
    start = jnp.zeros_like(places)
    end = 0
    for i in range(doc_ref.shape[1]):
        end = end + doc_ref[0, i]
        start = jnp.where(places >= end, end, start)
    return start


def conv_sum(pad_ref, taps_ref, age, first, rows):
    total = taps_ref[0, 0:1, :].astype(F32) * pad_ref[pl.ds(first + 8, rows), :]
    for i in range(1, KC):
        shifted = pad_ref[pl.ds(first + 8 - i, rows), :]
        total = total + taps_ref[0, i : i + 1, :].astype(F32) * jnp.where(age >= i, shifted, 0.0)
    return total


def ages(doc_ref, first, rows, width):
    places = first + lax.broadcasted_iota(jnp.int32, (rows, 128), 0)
    age = places - doc_start(doc_ref, places)
    return jnp.concatenate([age] * (width // 128), 1)


PRE_ROWS = 256


def pre_kernel(doc_ref, x_ref, gain_ref, w_ref, gate_ref, decay_ref, taps_ref, n_ref, gates_ref, rates_ref, p_ref, act_ref, q_ref, head_ref, pad):
    part = pl.program_id(0)
    width = w_ref.shape[2]

    @pl.when(part == 0)
    def _():
        pad[pl.ds(0, 8), :] = jnp.zeros((8, width), F32)
        total = jnp.zeros((1, 128), F32)
        for first in range(0, LEN, PRE_ROWS):
            rows = pl.ds(first, PRE_ROWS)
            x = x_ref[rows, :].astype(F32)
            inverse = lax.rsqrt(jnp.mean(x * x, -1, keepdims=True) + EPS)
            normed = (x * inverse * gain_row(gain_ref)).astype(LOW)
            n_ref[rows, :] = normed
            logits = [dot_nt(normed, gate_ref[...]), dot_nt(normed, decay_ref[...])]
            logits.append(jnp.zeros((PRE_ROWS, 128 - HEADS - 2), F32))
            gates = jax.nn.sigmoid(jnp.concatenate(logits, 1))
            gates_ref[rows, :] = gates
            if first < CH:
                total = total + jnp.sum(gates, 0, keepdims=True)
        rates_ref[...] = total * (1.0 / CH)

    for first in range(0, LEN, PRE_ROWS):
        rows = pl.ds(first, PRE_ROWS)
        p = jnp.dot(n_ref[rows, :], w_ref[0], preferred_element_type=F32)
        p_ref[0, rows, :] = p
        pad[pl.ds(first + 8, PRE_ROWS), :] = p
        age = ages(doc_ref, first, PRE_ROWS, width)
        c = conv_sum(pad, taps_ref, age, first, PRE_ROWS)
        a = c * jax.nn.sigmoid(c)

        @pl.when(part < 2)
        def _():
            out = a * lax.rsqrt(head_sum(a * a, same_head(width)) + EPS)
            act_ref[0, rows, :] = out.astype(LOW)

        @pl.when(part == 2)
        def _():
            act_ref[0, rows, :] = a.astype(LOW)

    head_ref[0] = act_ref[0, :CH, :]

    @pl.when(part == 0)
    def _():
        q_ref[...] = act_ref[0, CH:, :]


def pre(doc_len, tokens, gain, w_t, gate_t, decay_t, taps):
    width = w_t.shape[2]
    part = pl.BlockSpec((1, LEN, width), lambda i: (i, 0, 0))
    return run(
        "pre", pre_kernel, 3,
        [(doc_len, SMEM_SPEC), full(tokens), full(gain), (w_t, pl.BlockSpec((1, D, width), lambda i: (i, 0, 0))),
         full(gate_t), full(decay_t), (taps, pl.BlockSpec((1, KC, width), lambda i: (i, 0, 0)))],
        [far(out_full((LEN, D), LOW)), far(out_full((LEN, 128), F32)), far(out_full((1, 128), F32)),
         far(((3, LEN, width), F32, part)), far(((3, LEN, width), LOW, part)), out_full((CH, width), LOW),
         ((3, CH, width), LOW, pl.BlockSpec((1, CH, width), lambda i: (i, 0, 0)))],
        [pltpu.VMEM((LEN + 8, width), F32)], 13.0,
    )


def fetch_kernel(a, b, c, to_a, to_b, to_c):
    to_a[...] = a[...]
    to_b[...] = b[...]
    to_c[...] = c[...]


def fetch(mem_in, mem_out, w_down):
    arrays = [mem_in, mem_out, w_down]
    return run(
        "fetch", fetch_kernel, 4, [rows_of(a, a.shape[0] // 4) for a in arrays],
        [near((a.shape, LOW, pl.BlockSpec((a.shape[0] // 4, a.shape[1]), lambda i: (i, 0)))) for a in arrays], (), 2.0,
    )


QB = 256


def key_range(block):
    return max(0, (block - 2) * QB), (block + 1) * QB


def allowed(doc_ref, block, low_key, high_key):
    query = block * QB + lax.broadcasted_iota(jnp.int32, (8, QB), 1)
    low = jnp.maximum(doc_start(doc_ref, query), query - (WIN - 1))[0:1]
    key = low_key + lax.broadcasted_iota(jnp.int32, (high_key - low_key, QB), 0)
    return (key >= low) & (key <= query[0:1])


def scaled_head(q, index):
    lane = lax.broadcasted_iota(jnp.int32, q.shape, 1)
    return jnp.where(lane // HD == index, q * 8.0, 0.0).astype(LOW)


def one_head(v, index):
    lane = lax.broadcasted_iota(jnp.int32, v.shape, 1)
    return jnp.where(lane // HD == index, v, 0.0).astype(LOW)


def dot_nt(a, b):
    return lax.dot_general(a, b, (((1,), (1,)), ((), ())), preferred_element_type=F32)


def dot_nn(a, b):
    return jnp.dot(a, b, preferred_element_type=F32)


def dot_tn(a, b):
    return lax.dot_general(a, b, (((0,), (0,)), ((), ())), preferred_element_type=F32)


def flat(v):
    return v.astype(F32).T.astype(v.dtype)


def attend_kernel(doc_ref, q_ref, k_ref, v_ref, pk_ref, pv_ref, out_ref, peak_ref, inv_ref):
    k = k_ref[0]
    values_t = flat(v_ref[0])
    pk = pk_ref[0]
    pv_t = flat(pv_ref[0])
    for block in range(LEN // QB):
        low_key, high_key = key_range(block)
        ok = allowed(doc_ref, block, low_key, high_key)
        q = q_ref[0, pl.ds(block * QB, QB), :].astype(F32)
        outs = []
        for index in range(2):
            q_head = scaled_head(q, index)
            s = jnp.where(ok, dot_nt(k[low_key:high_key], q_head), NEG)
            sp = dot_nt(pk, q_head)
            peak = jnp.maximum(jnp.max(s, 0, keepdims=True), jnp.max(sp, 0, keepdims=True))
            e = jnp.exp(s - peak)
            ep = jnp.exp(sp - peak)
            inv = 1.0 / (jnp.sum(e, 0, keepdims=True) + jnp.sum(ep, 0, keepdims=True))
            feats = slice(index * HD, index * HD + HD)
            out = dot_nn(values_t[feats, low_key:high_key], e.astype(LOW)) + dot_nn(
                pv_t[feats], ep.astype(LOW)
            )
            outs.append(out * inv)
            peak_ref[0, index : index + 1, pl.ds(block * QB, QB)] = peak
            inv_ref[0, index : index + 1, pl.ds(block * QB, QB)] = inv
        out_ref[pl.ds(block * QB, QB), :] = jnp.concatenate(outs, 0).T.astype(LOW)


def attend(doc_len, act, persistent):
    width = act.shape[2]
    pairs = width // 128
    smem = pl.BlockSpec(memory_space=pltpu.SMEM)

    def part(i):
        return pl.BlockSpec((1, LEN, 128), lambda g: (i, 0, g))

    def pers(i):
        return pl.BlockSpec((1, NP, 128), lambda g: (i, 0, g))

    stat = pl.BlockSpec((1, 2, LEN), lambda g: (g, 0, 0))
    arrays = [doc_len, act, act, act, persistent, persistent]
    specs = [smem, part(0), part(1), part(2), pers(0), pers(1)]
    return run(
        "attend", attend_kernel, pairs, list(zip(arrays, specs)),
        [far(((LEN, width), LOW, pl.BlockSpec((LEN, 128), lambda g: (0, g)))), far(((pairs, 2, LEN), F32, stat)),
         far(((pairs, 2, LEN), F32, stat))],
        (), 9.3,
    )


SMEM_SPEC = pl.BlockSpec(memory_space=pltpu.SMEM)
STEPS = 2


def whole(shape):
    zeros = (0,) * len(shape)
    return pl.BlockSpec(tuple(shape), lambda *_: zeros, pipeline_mode=pl.Buffered(1))


LAST = []
PLACED = []


def placed(a):
    for other, space in PLACED:
        if other is a:
            return pltpu.with_memory_space_constraint(a, space)
    return a


def put(a, space):
    PLACED.append((a, space))
    return a


def chained(arrays, specs):
    arrays = [placed(a) for a in arrays]
    if LAST:
        return arrays + [placed(LAST[0])], specs + [pl.BlockSpec(memory_space=pl.ANY)]
    return arrays, specs


def remember(outs):
    LAST[:] = [min(outs, key=lambda o: o.size * o.dtype.itemsize)]
    return outs


def near(out):
    return (*out, pltpu.VMEM)


def far(out):
    return (*out, pltpu.HBM)


def shape_of(out):
    shape, kind = tuple(out[0]), out[1]
    return out[3](shape, kind) if len(out) > 3 else jax.ShapeDtypeStruct(shape, kind)


def run(name, kernel, steps, ins, outs, scratch=(), micros=0.0, held=(), aliases=(), room=0):
    used = len(ins)
    arrays = [a for a, _ in ins] + list(held)
    specs = [s for _, s in ins] + [pl.BlockSpec(memory_space=pl.ANY)] * len(held)
    arrays, specs = chained(arrays, specs)
    count = len(arrays)

    def inner(*refs):
        kernel(*refs[:used], *refs[count:])

    results = pl.pallas_call(
        inner,
        grid=(steps,),
        in_specs=specs,
        out_specs=[out[2] for out in outs],
        out_shape=[shape_of(out) for out in outs],
        scratch_shapes=list(scratch),
        input_output_aliases={used + k: v for k, v in dict(aliases).items()},
        compiler_params=pltpu.CompilerParams(vmem_limit_bytes=(VMEM_OF.get(name, VMEM) + room) << 20),
        cost_estimate=pl.CostEstimate(flops=1, bytes_accessed=1, transcendentals=0),
        name=name,
    )(*arrays)
    for result, out in zip(results, outs):
        if len(out) > 3:
            put(result, out[3])
    return remember(results)


def tie(v):
    space = next((space for other, space in PLACED if other is LAST[0]), None)
    v, LAST[0] = lax.optimization_barrier((v, LAST[0]))
    if space is not None:
        put(LAST[0], space)
    return v


def pinned(v):
    v = tie(v)
    LAST[:] = [v]
    return v


def fold_kernel(a, b, out):
    out[...] = (a[...].astype(F32) + b[...].astype(F32)).astype(out.dtype)


def fold(a, b, kind):
    zeros = (0,) * a.ndim
    spec = pl.BlockSpec(a.shape, lambda i: zeros)
    return run("fold", fold_kernel, 1, [(a, spec), (b, spec)], [far((a.shape, kind, spec)) if kind == F32 else (a.shape, kind, spec)])[0]


def fold_rows(keep, come):
    part = come[0].shape[0]

    def kernel(keep_ref, *refs):
        for i, ref in enumerate(refs[:-1]):
            at = pl.ds(i * part, part)
            refs[-1][at, :] = (keep_ref[at, :].astype(F32) + ref[...].astype(F32)).astype(LOW)

    return run("fold_rows", kernel, 1, [full(keep)] + [full(c) for c in come], [out_full(keep.shape, LOW)])[0]


def fold_columns(keep, come):
    count = len(come)
    _, rows, width = keep.shape
    part = rows // count

    def kernel(keep_ref, *refs):
        chip = lax.axis_index("narrow") >> 1
        run_ref, away_ref = refs[count:]
        for i in range(count):
            at = pl.ds(i * part, part)
            run_ref[0, at, :] = (keep_ref[chip, at, :].astype(F32) + refs[i][chip].astype(F32)).astype(LOW)
            away_ref[0, at, :] = (keep_ref[1 - chip, at, :].astype(F32) + refs[i][1 - chip].astype(F32)).astype(LOW)

    one = out_full((1, rows, width), LOW)
    return run("fold_columns", kernel, 1, [full(keep)] + [full(c) for c in come], [one, one], (), 1.5)


def fold_pick(bit_of, a, b):
    pairs = a.shape[0] // 2
    tail = a.shape[1:]
    zeros = (0,) * len(tail)
    two = pl.BlockSpec((2,) + tail, lambda i: (i,) + zeros)
    one = ((pairs,) + tail, LOW, pl.BlockSpec((1,) + tail, lambda i: (i,) + zeros))

    def kernel(a_ref, b_ref, keep, send):
        bit = bit_of()
        keep[0] = (a_ref[bit].astype(F32) + b_ref[bit].astype(F32)).astype(LOW)
        send[0] = (a_ref[1 - bit].astype(F32) + b_ref[1 - bit].astype(F32)).astype(LOW)

    return run("fold_pick", kernel, pairs, [(a, two), (b, two)], [one, one], (), 1.5)


def full(a):
    return (a, whole(a.shape))


def out_full(shape, kind):
    return (shape, kind, whole(shape))


def cols_of(a, chunk):
    return (a, pl.BlockSpec((a.shape[0], chunk), lambda i: (0, i)))


def rows_of(a, chunk):
    return (a, pl.BlockSpec((chunk, a.shape[1]), lambda i: (i, 0)))


def half_of(a, half):
    return (a, pl.BlockSpec((CH, a.shape[1]), lambda i: (half, 0)))


def out_cols(rows, cols, kind, chunk):
    return ((rows, cols), kind, pl.BlockSpec((rows, chunk), lambda i: (0, i)))


def rates_of(reset, rates):
    kept = 1.0 - reset[0].astype(F32)
    return kept, rates[0:1, HEADS : HEADS + 1], rates[0:1, HEADS + 1 : HEADS + 2]


def my_place():
    me = lax.axis_index("narrow")
    return me, me & 1


def wide_bit(place):
    return (lax.axis_index("wide") >> place) & 1


def span(index, width):
    return pl.ds(pl.multiple_of(index * width, width), width)


def gain_row(ref):
    g = ref[...].astype(F32)
    return jnp.concatenate([g[i : i + 1] for i in range(g.shape[0])], 1)


def silu_slope(pre, sig):
    return sig * (1.0 + pre * (1.0 - sig))


def head_columns():
    head = lax.broadcasted_iota(jnp.int32, (128, D), 0)
    feat = lax.broadcasted_iota(jnp.int32, (128, D), 1) // HD
    return (head == feat).astype(F32).astype(LOW)


def two_terms(v):
    high = v.astype(LOW)
    return high, (v - high.astype(F32)).astype(LOW)


def widen(gates, columns):
    high, rest = two_terms(gates)
    return dot_nn(high, columns) + dot_nn(rest, columns)


def narrow_heads(v, columns):
    high, rest = two_terms(v)
    return dot_nt(high, columns) + dot_nt(rest, columns)


def halves(terms, core):
    run_ref, far, near, near_far = terms
    for a, b, which in ((run_ref, far, core), (near, near_far, 1 - core)):
        yield span(which, CH // 2), a[...].astype(F32) + b[...].astype(F32)


def put_halves(keep, sends, v_ref, core):
    rows = CH // 2
    keep[...] = v_ref[span(core, rows), :].astype(LOW)
    part = rows // len(sends)
    for i, send in enumerate(sends):
        send[...] = v_ref[pl.ds(pl.multiple_of((1 - core) * rows + i * part, part), part), :].astype(LOW)


def put_columns(keep, send, v_ref, core, width, rows=None):
    for i in range(2):
        own = v_ref[:, span(2 * i + core, width)].astype(LOW)
        other = v_ref[:, span(2 * i + 1 - core, width)].astype(LOW)
        if rows is None:
            keep[i] = own
            send[i] = other
        else:
            keep[i, rows, :] = own
            send[i, rows, :] = other


def add_to(acc, first, v):
    @pl.when(first)
    def _():
        acc[...] = v

    @pl.when(jnp.logical_not(first))
    def _():
        acc[...] += v


def halves_out(parts=1):
    return [out_full((CH // 2, D), LOW)] + [out_full((CH // 2 // parts, D), LOW) for _ in range(parts)]


def scratch_half():
    return pltpu.VMEM((CH, D), F32)


def mem1_kernel(kv0, kv1, kv2, kv3, w_in, w_out, q, kc, vc, hk, ks, kcv, keep, *rest):
    step = pl.program_id(0)
    *sends, acc = rest
    me, core = my_place()
    width = kv0.shape[2]

    @pl.when(step == 0)
    def _():
        for r, part in enumerate((kv0, kv1, kv2, kv3)):
            cols = span(me ^ r, width)
            q[:, cols] = part[0]
            kc[:, cols] = part[1]
            vc[:, cols] = part[2]

    pre = dot_nn(kc[...], w_in[...])
    sig = jax.nn.sigmoid(pre)
    hidden = (pre * sig).astype(LOW)
    hk[...] = hidden
    ks[...] = silu_slope(pre, sig).astype(LOW)
    kcv[...] = (sig * (1.0 - sig) * (2.0 + pre * (1.0 - 2.0 * sig))).astype(LOW)
    add_to(acc, step == 0, dot_nn(hidden, w_out[...]))

    @pl.when(step == STEPS - 1)
    def _():
        put_halves(keep, sends, acc, core)


def mem1(parts, mem_in, mem_out):
    units = mem_in.shape[1]
    chunk = units // STEPS
    return run(
        "mem1", mem1_kernel, STEPS,
        [] + [full(p) for p in parts] + [cols_of(mem_in, chunk), rows_of(mem_out, chunk)],
        [near(out_full((CH, D), LOW)) for _ in range(3)]
        + [near(out_cols(CH, units, LOW, chunk)) for _ in range(3)] + halves_out(4),
        [scratch_half()], 8.4,
    )


def recall1_kernel(q, gates, att, w_o, w_in, w_out, hid, slope, rec, keep, send, acc):
    step = pl.program_id(0)
    core = my_place()[1]
    pre = dot_nn(q[...], w_in[...])
    sig = jax.nn.sigmoid(pre)
    hidden = (pre * sig).astype(LOW)
    hid[...] = hidden
    slope[...] = silu_slope(pre, sig).astype(LOW)
    add_to(acc, step == 0, dot_nn(hidden, w_out[...]))

    @pl.when(step == STEPS - 1)
    def _():
        rec[...] = acc[...].astype(LOW)
        acc[...] = acc[...] * widen(gates[...], head_columns()) + dot_nn(att[...], w_o[...])
        put_halves(keep, [send], acc, core)


def recall1(q, gates, attended, w_o, mem_in, mem_out):
    units = mem_in.shape[1]
    chunk = units // STEPS
    return run(
        "recall1", recall1_kernel, STEPS,
        [] + [full(q), half_of(gates, 0), half_of(attended, 0), full(w_o), cols_of(mem_in, chunk), rows_of(mem_out, chunk)],
        [far(out_cols(CH, units, LOW, chunk)), far(out_cols(CH, units, LOW, chunk)),
         far(out_full((CH, D), LOW))]
        + halves_out(),
        [scratch_half()], 9.6,
    )


def mem2_kernel(
    reset, rates, s0, s1, s2, s3, q0, q1, q2, q3, vc, kc, hk, ks, kcv, gates, att, w_o, w_in, w_out,
    q, err, slope_low, bcurve, m_in, m_out, hid, slope, rec, keep, send, acc,
):
    step = pl.program_id(0)
    me, core = my_place()
    kept, decay, rate = rates_of(reset, rates)

    @pl.when(step == 0)
    def _():
        for r, part in enumerate((q0, q1, q2, q3)):
            q[:, span(me ^ r, part.shape[1])] = part[...]
        for rows, total in halves((s0, s1, s2, s3), core):
            err[rows, :] = (total - vc[rows, :].astype(F32)).astype(LOW)

    back = dot_nt(err[...], w_out[...])
    slopes = (back * ks[...].astype(F32)).astype(LOW)
    slope_low[...] = slopes
    bcurve[...] = (back * kcv[...].astype(F32)).astype(LOW)
    retain = 1.0 - kept * decay
    take_in = kept * rate * (STEP_IN / CH)
    take_out = kept * rate * (STEP_OUT / CH)
    now_in = (w_in[...].astype(F32) * retain - take_in * dot_tn(kc[...], slopes)).astype(LOW)
    m_in[...] = now_in
    pre = dot_nn(q[...], now_in)
    sig = jax.nn.sigmoid(pre)
    hidden = (pre * sig).astype(LOW)
    hid[...] = hidden
    slope[...] = silu_slope(pre, sig).astype(LOW)
    now_out = (w_out[...].astype(F32) * retain - take_out * dot_tn(hk[...], err[...])).astype(LOW)
    m_out[...] = now_out
    add_to(acc, step == 0, dot_nn(hidden, now_out))

    @pl.when(step == STEPS - 1)
    def _():
        rec[...] = acc[...].astype(LOW)
        acc[...] = acc[...] * widen(gates[...], head_columns()) + dot_nn(att[...], w_o[...])
        put_halves(keep, [send], acc, core)


def mem2(reset, rates, terms, q_parts, vc, kc, hk, ks, kcv, gates, attended, w_o, mem_in, mem_out):
    units = mem_in.shape[1]
    chunk = units // STEPS
    piece = far(out_cols(CH, units, LOW, chunk))
    return run(
        "mem2", mem2_kernel, STEPS,
        [(reset, SMEM_SPEC), full(rates), *[full(t) for t in terms],
         *[full(p) for p in q_parts], full(vc), full(kc), cols_of(hk, chunk),
         cols_of(ks, chunk), cols_of(kcv, chunk), half_of(gates, 1), half_of(attended, 1), full(w_o),
         cols_of(mem_in, chunk), rows_of(mem_out, chunk)],
        [near(out_full((CH, D), LOW)), near(out_full((CH, D), LOW)), piece, piece, far(out_cols(D, units, LOW, chunk)),
         far(((units, D), LOW, pl.BlockSpec((chunk, D), lambda i: (i, 0)))), piece, piece, far(out_full((CH, D), LOW))]
        + halves_out(),
        [scratch_half()], 15.0,
    )


def feed_kernel(
    s0, s1, s2, s3, x, gain, w_up, w_down, c0, c1, c2, c3,
    normed, cot, hid, gg, gu, fkeep, fsend, midloc, gain_part, keep, send, mid, acc_out, acc_norm,
):
    step = pl.program_id(0)
    me, core = my_place()
    width = c0.shape[1]

    @pl.when(step == 0)
    def _():
        for r, part in enumerate((c0, c1, c2, c3)):
            cot[:, span(me ^ r, width)] = part[...]
        for rows, total in halves((s0, s1, s2, s3), core):
            middle = x[rows, :].astype(F32) + total
            mid[rows, :] = middle
            inverse = lax.rsqrt(jnp.mean(middle * middle, -1, keepdims=True) + EPS)
            normed[rows, :] = (middle * inverse * gain_row(gain)).astype(LOW)

    gate_val = dot_nn(normed[...], w_up[0])
    up_val = dot_nn(normed[...], w_up[1])
    grad_hid = dot_nt(cot[...], w_down[...])
    sig = jax.nn.sigmoid(gate_val)
    act = gate_val * sig
    hidden = (act * up_val).astype(LOW)
    hid[...] = hidden
    grad_gate = (grad_hid * up_val * silu_slope(gate_val, sig)).astype(LOW)
    grad_up = (grad_hid * act).astype(LOW)
    gg[...] = grad_gate
    gu[...] = grad_up
    add_to(acc_norm, step == 0, dot_nt(grad_gate, w_up[0]) + dot_nt(grad_up, w_up[1]))
    add_to(acc_out, step == 0, dot_nn(hidden, w_down[...]))

    @pl.when(step == STEPS - 1)
    def _():
        put_columns(fkeep, fsend, acc_out, core, width)
        midloc[...] = mid[:, span(me, width)]
        total = jnp.zeros((1, D), F32)
        for part in range(2):
            rows = pl.ds(part * (CH // 2), CH // 2)
            middle = mid[rows, :]
            inverse = lax.rsqrt(jnp.mean(middle * middle, -1, keepdims=True) + EPS)
            unit = middle * inverse
            grad = acc_norm[rows, :]
            total = total + jnp.sum(grad * unit, 0, keepdims=True)
            acc_norm[rows, :] = norm_back(grad, unit, inverse, gain_row(gain))
        gain_part[...] = total
        put_halves(keep, [send], acc_norm, core)


def feed(half, terms, tokens, gain, w_gate_up, w_down, cot_parts, held=()):
    units = w_down.shape[0]
    chunk = units // STEPS
    width = cot_parts[0].shape[1]
    piece = near(out_cols(CH, units, LOW, chunk))
    quarter = ((2, LEN, width), LOW, pl.BlockSpec((2, CH, width), lambda i: (0, half, 0)))
    return run(
        "feed" + str(half), feed_kernel, STEPS,
        [*[full(t) for t in terms], half_of(tokens, half), full(gain),
         (w_gate_up, pl.BlockSpec((2, D, chunk), lambda i: (0, 0, i))), rows_of(w_down, chunk)]
        + [half_of(p, half) for p in cot_parts],
        [near(out_full((CH, D), LOW)), near(out_full((CH, D), LOW)), piece, piece, piece, quarter, quarter,
         far(out_full((CH, width), F32)), far(out_full((1, D), F32))] + halves_out(),
        [scratch_half(), scratch_half(), scratch_half()], 15.0, held, {0: 5, 1: 6} if held else {},
    )


ROW_STEPS = 4


def put_rows(keep, send, v, bit, size, place):
    block = D // size
    v = v.reshape(v.shape[0] // (2 * block << place), 2, 1 << place, block, v.shape[1])
    shape = (v.shape[0] << place, block, v.shape[4])
    keep[...] = jnp.where(bit == 0, v[:, 0], v[:, 1]).astype(LOW).reshape(shape)
    send[...] = jnp.where(bit == 0, v[:, 1], v[:, 0]).astype(LOW).reshape(shape)


def put_col_blocks(keep, send, v, bit, size, place):
    block = D // size
    for i in range(size // 2):
        first = ((i >> place) << (place + 1)) | (i & ((1 << place) - 1))
        second = first | (1 << place)
        zero = v[:, first * block : (first + 1) * block]
        one = v[:, second * block : (second + 1) * block]
        keep[i] = jnp.where(bit == 0, zero, one).astype(LOW)
        send[i] = jnp.where(bit == 0, one, zero).astype(LOW)


def row_out(size, units, steps):
    block = D // size
    return ((size // 2, block, units), LOW, pl.BlockSpec((size // 2 // steps, block, units), lambda i: (i, 0, 0)))


def col_out(size, units):
    block = D // size
    return ((size // 2, units, block), LOW, pl.BlockSpec((size // 2, units // ROW_STEPS, block), lambda i: (0, i, 0)))


def feed_weights_kernel(size, na, nb, gga, ggb, gua, gub, ca, cb, ha, hb, ukeep, usend, dkeep, dsend):
    bit = wide_bit(0)
    for which, (a, b) in enumerate(((gga, ggb), (gua, gub))):
        v = dot_tn(na[...], a[...]) + dot_tn(nb[...], b[...])
        put_rows(ukeep.at[:, which], usend.at[:, which], v, bit, size, 0)
    v = dot_tn(ha[...], ca[...]) + dot_tn(hb[...], cb[...])
    put_col_blocks(dkeep, dsend, v, wide_bit(1), size, 1)


def feed_weights(size, na, nb, gga, ggb, gua, gub, ca, cb, ha, hb):
    units = ha.shape[1]
    block = D // ROW_STEPS
    rows = D // size
    per = block // rows
    half = ((size // 2, 2, rows, units), LOW, pl.BlockSpec((per // 2, 2, rows, units), lambda i: (i, 0, 0, 0)))
    cols = col_out(size, units)
    return run(
        "feed_weights", lambda *refs: feed_weights_kernel(size, *refs), ROW_STEPS,
        [cols_of(na, block), cols_of(nb, block), full(gga), full(ggb), full(gua), full(gub), full(ca), full(cb),
         cols_of(ha, units // ROW_STEPS), cols_of(hb, units // ROW_STEPS)],
        [far(half), far(half), far(cols), far(cols)], (), 11.7, room=0 if rows >= 128 else 24,
    )


def mid_grad(terms, cot, core, grad):
    for rows, total in halves(terms, core):
        grad[rows, :] = total + cot[rows, :].astype(F32)


def gate_side(gates, rec, grad, low, loc, head_grad, recall_grad, me, width):
    columns = head_columns()
    gates = gates[...]
    terms = narrow_heads(rec[...].astype(F32) * grad[...], columns)
    head_grad[...] = terms * gates * (1.0 - gates)
    recall_grad[...] = (widen(gates, columns) * grad[...]).astype(LOW)
    low[...] = grad[...].astype(LOW)
    loc[...] = grad[:, span(me, width)]


def recall1_back_kernel(
    s0, s1, s2, s3, cot, gates, rec, hid, slope, q, w_in, w_out,
    low, loc, head_grad, g_in, g_out, dq, grad, rgrad,
):
    step = pl.program_id(0)
    me, core = my_place()

    @pl.when(step == 0)
    def _():
        mid_grad((s0, s1, s2, s3), cot, core, grad)
        gate_side(gates, rec, grad, low, loc, head_grad, rgrad, me, loc.shape[1])

    rg = rgrad[...]
    dpre = (dot_nt(rg, w_out[...]) * slope[...].astype(F32)).astype(LOW)
    g_out[...] = dot_tn(hid[...], rg).astype(LOW)
    g_in[...] = dot_tn(q[...], dpre).astype(LOW)
    add_to(dq, step == 0, dot_nt(dpre, w_in[...]))


def recall1_back(width, terms, cot, gates, rec, hid, slope, q, mem_in, mem_out):
    units = mem_in.shape[1]
    chunk = units // STEPS
    return run(
        "recall1_back", recall1_back_kernel, STEPS,
        [*[full(t) for t in terms], full(cot), half_of(gates, 0), full(rec), cols_of(hid, chunk),
         cols_of(slope, chunk), full(q), cols_of(mem_in, chunk), rows_of(mem_out, chunk)],
        [near(out_full((CH, D), LOW)), far(out_full((CH, width), F32)), far(out_full((CH, 128), F32)),
         far(out_cols(D, units, LOW, chunk)), far(((units, D), LOW, pl.BlockSpec((chunk, D), lambda i: (i, 0)))),
         near(out_full((CH, D), F32))],
        [scratch_half(), pltpu.VMEM((CH, D), LOW)], 12.2,
    )


def mem2_back_kernel(
    reset, rates, s0, s1, s2, s3, cot, gates, rec, hid, slope, q, m_in, m_out, kc, hk, ks, bcurve, slope_low, w_in, w_out,
    low, loc, head_grad, d_in, d_out, dpre_out, dback, gsb, sums, keep, *rest,
):
    step = pl.program_id(0)
    *sends, grad, rgrad, acc = rest
    me, core = my_place()
    kept, _, rate = rates_of(reset, rates)

    @pl.when(step == 0)
    def _():
        mid_grad((s0, s1, s2, s3), cot, core, grad)
        gate_side(gates, rec, grad, low, loc, head_grad, rgrad, me, loc.shape[1])

    rg = rgrad[...]
    dpre = (dot_nt(rg, m_out[...]) * slope[...].astype(F32)).astype(LOW)
    dpre_out[...] = dpre
    dm_out = dot_tn(hid[...], rg)
    dm_out_low = dm_out.astype(LOW)
    d_out[...] = dm_out_low
    dm_in = dot_tn(q[...], dpre)
    dm_in_low = dm_in.astype(LOW)
    d_in[...] = dm_in_low
    decayed = jnp.sum(w_in[...].astype(F32) * dm_in, 0, keepdims=True)
    decayed_out = jnp.sum(w_out[...].astype(F32) * dm_out, 0, keepdims=True)
    t_in = dot_nn(kc[...], dm_in_low)
    stepped = jnp.sum(slope_low[...].astype(F32) * t_in, 0, keepdims=True)
    grad_slope = t_in * (-kept * rate * (STEP_IN / CH))
    gsb[...] = (grad_slope * bcurve[...].astype(F32)).astype(LOW)
    db = (grad_slope * ks[...].astype(F32)).astype(LOW)
    dback[...] = db
    sums[0:1, :] = decayed
    sums[1:2, :] = stepped
    chunk = decayed.shape[1]
    sums[2:3, :] = sum(decayed_out[:, i * chunk : (i + 1) * chunk] for i in range(decayed_out.shape[1] // chunk))
    add_to(
        acc, step == 0,
        dot_nn(hk[...], dm_out_low) * (-kept * rate * (STEP_OUT / CH)) + dot_nn(db, w_out[...]),
    )

    @pl.when(step == STEPS - 1)
    def _():
        put_halves(keep, sends, acc, core)


def mem2_back(
    width, reset, rates, terms, cot, gates, rec, hid, slope, q, m_in, m_out, kc, hk, ks, bcurve, slope_low,
    mem_in, mem_out,
):
    units = mem_in.shape[1]
    chunk = units // STEPS
    piece = near(out_cols(CH, units, LOW, chunk))
    return run(
        "mem2_back", mem2_back_kernel, STEPS,
        [(reset, SMEM_SPEC), full(rates), *[full(t) for t in terms], full(cot), half_of(gates, 1), full(rec),
         cols_of(hid, chunk), cols_of(slope, chunk), full(q), cols_of(m_in, chunk), rows_of(m_out, chunk),
         full(kc), cols_of(hk, chunk), cols_of(ks, chunk), cols_of(bcurve, chunk), cols_of(slope_low, chunk),
         cols_of(mem_in, chunk), rows_of(mem_out, chunk)],
        [near(out_full((CH, D), LOW)), far(out_full((CH, width), F32)), far(out_full((CH, 128), F32)),
         near(out_cols(D, units, LOW, chunk)), near(((units, D), LOW, pl.BlockSpec((chunk, D), lambda i: (i, 0)))),
         piece, piece, piece, far(out_cols(3, units, F32, chunk))] + halves_out(2),
        [scratch_half(), pltpu.VMEM((CH, D), LOW), scratch_half()], 18.0,
    )


def mem2_late_kernel(reset, rates, err, hk, ks, gsb, slope_low, d_in, d_out, dpre, m_in, base, sums, dq, dk):
    step = pl.program_id(0)
    kept, _, rate = rates_of(reset, rates)
    t_out = dot_nt(err[...], d_out[...])
    sums[...] = jnp.sum(hk[...].astype(F32) * t_out, 0, keepdims=True)
    base[...] = (t_out * (-kept * rate * (STEP_OUT / CH)) * ks[...].astype(F32) + gsb[...].astype(F32)).astype(LOW)
    add_to(dk, step == 0, dot_nt(slope_low[...], d_in[...]) * (-kept * rate * (STEP_IN / CH)))
    add_to(dq, step == 0, dot_nt(dpre[...], m_in[...]))


def mem2_late(reset, rates, err, hk, ks, gsb, slope_low, d_in, d_out, dpre, m_in):
    units = hk.shape[1]
    chunk = units // STEPS
    return run(
        "mem2_late", mem2_late_kernel, STEPS,
        [(reset, SMEM_SPEC), full(rates), full(err), cols_of(hk, chunk), cols_of(ks, chunk), cols_of(gsb, chunk),
         cols_of(slope_low, chunk), cols_of(d_in, chunk), rows_of(d_out, chunk), cols_of(dpre, chunk),
         cols_of(m_in, chunk)],
        [near(out_cols(CH, units, LOW, chunk)), far(out_cols(1, units, F32, chunk)), near(out_full((CH, D), F32)),
         near(out_full((CH, D), F32))],
        (), 10.6,
    )


def query_split_kernel(reset, n, gates, heads_a, heads_b, sums, sums_out, dq1, dq2, keep, send_a, send_b, heads, small):
    core = my_place()[1]
    width = keep.shape[2]
    for part, (ref, send) in enumerate(((dq1, send_a), (dq2, send_b))):
        for i in range(2):
            keep[i, pl.ds(part * CH, CH), :] = ref[:, span(2 * i + core, width)].astype(LOW)
            send[i] = ref[:, span(2 * i + 1 - core, width)].astype(LOW)
    kept = 1.0 - reset[0].astype(F32)
    decay_part = jnp.sum(sums[0:1, :] + sums[2:3, :], 1, keepdims=True) * (-kept / CH)
    step_part = jnp.sum(STEP_IN * sums[1:2, :] + STEP_OUT * sums_out[...], 1, keepdims=True) * (-kept / (CH * CH))
    lane = lax.broadcasted_iota(jnp.int32, (1, 128), 1)
    logit = jnp.where(lane == HEADS, decay_part, 0.0) + jnp.where(lane == HEADS + 1, step_part, 0.0)
    g = gates[...]
    heads[:CH, :] = (heads_a[...] + g * (1.0 - g) * logit).astype(LOW)
    heads[CH:, :] = heads_b[...].astype(LOW)
    small[...] = dot_tn(heads[...], n[...])


def query_split(width, reset, normed, gates, heads_a, heads_b, sums, sums_out, dq1, dq2):
    quarter = out_full((2, LEN, width), LOW)
    half = out_full((2, CH, width), LOW)
    return run(
        "query_split", query_split_kernel, 1,
        [(reset, SMEM_SPEC), full(normed), half_of(gates, 0), full(heads_a), full(heads_b), full(sums), full(sums_out),
         full(dq1), full(dq2)],
        [quarter, half, half, out_full((LEN, 128), LOW), out_full((128, D), F32)], (), 5.0,
    )


def mem1_back_kernel(s0, s1, s2, s3, ks, base, dk, w_in, w_out, dpred, dpre_out, vshare, keep, send_a, send_b, acc):
    step = pl.program_id(0)
    me, core = my_place()
    width = vshare.shape[1]

    @pl.when(step == 0)
    def _():
        for rows, total in halves((s0, s1, s2, s3), core):
            dpred[rows, :] = total.astype(LOW)
        vshare[...] = -dpred[:, span(me, width)].astype(F32)
        acc[...] = dk[...]

    dpre = (dot_nt(dpred[...], w_out[...]) * ks[...].astype(F32) + base[...].astype(F32)).astype(LOW)
    dpre_out[...] = dpre
    acc[...] += dot_nt(dpre, w_in[...])

    @pl.when(step == STEPS - 1)
    def _():
        for i in range(2):
            keep[i] = acc[:, span(2 * i + core, width)].astype(LOW)
            away = acc[:, span(2 * i + 1 - core, width)].astype(LOW)
            send_a[i] = away[: CH // 2]
            send_b[i] = away[CH // 2 :]


def mem1_back(width, terms, ks, base, dk, mem_in, mem_out):
    units = mem_in.shape[1]
    chunk = units // STEPS
    quarter = out_full((2, CH, width), LOW)
    half = out_full((2, CH // 2, width), LOW)
    return run(
        "mem1_back", mem1_back_kernel, STEPS,
        [*[full(t) for t in terms], cols_of(ks, chunk), cols_of(base, chunk), full(dk),
         cols_of(mem_in, chunk), rows_of(mem_out, chunk)],
        [near(out_full((CH, D), LOW)), near(out_cols(CH, units, LOW, chunk)), far(out_full((CH, width), F32)), quarter,
         half, half],
        [scratch_half()], 7.2,
    )


def mem_weights_kernel(size, reset, rates, g_in, g_out, d_in, d_out, kc, dpre, dback, err, hk, dpred, ikeep, isend, okeep, osend):
    bit = wide_bit(0)
    kept, decay, _ = rates_of(reset, rates)
    retain = 1.0 - kept * decay
    v = g_in[...].astype(F32) + retain * d_in[...].astype(F32) + dot_tn(kc[...], dpre[...])
    put_rows(ikeep, isend, v, bit, size, 0)
    v = (
        g_out[...].astype(F32) + retain * d_out[...].astype(F32)
        + dot_tn(dback[...], err[...]) + dot_tn(hk[...], dpred[...])
    )
    put_col_blocks(okeep, osend, v, bit, size, 0)


def mem_weights(size, reset, rates, g_in, g_out, d_in, d_out, kc, dpre, dback, err, hk, dpred):
    units = hk.shape[1]
    block = D // ROW_STEPS
    unit_block = units // ROW_STEPS
    r, c = row_out(size, units, ROW_STEPS), col_out(size, units)
    return run(
        "mem_weights", lambda *refs: mem_weights_kernel(size, *refs), ROW_STEPS,
        [(reset, SMEM_SPEC), full(rates), rows_of(g_in, block), rows_of(g_out, unit_block), rows_of(d_in, block),
         rows_of(d_out, unit_block), cols_of(kc, block), full(dpre), cols_of(dback, unit_block), full(err),
         cols_of(hk, unit_block), full(dpred)],
        [r, r, c, c], (), 9.4, room=0 if D // size >= 128 else 24,
    )


def weights_kernel(size, n, gma, gmb, att, gq, gk, gv, akeep, asend, bkeep, bsend):
    v_out = dot_tn(gma[...], att[:CH, :]) + dot_tn(gmb[...], att[CH:, :])
    v = jnp.concatenate([v_out, dot_tn(n[...], gv[...])], 1)
    put_rows(akeep, asend, v, wide_bit(0), size, 0)
    v = dot_tn(n[...], jnp.concatenate([gq[...], gk[...]], 1))
    put_rows(bkeep, bsend, v, wide_bit(0), size, 0)


def weights(size, normed, gma, gmb, attended, gq, gk, gv):
    r = row_out(size, 2 * gq.shape[1], 2)
    block = D // 2
    return run(
        "weights", lambda *refs: weights_kernel(size, *refs), 2,
        [cols_of(normed, block), cols_of(gma, block), cols_of(gmb, block), full(attended), full(gq), full(gk), full(gv)],
        [r, r, r, r], (), 9.0, room=4,
    )


def last_kernel(gq, gk, gv, w, heads, gate_t, decay_t, x, gain, keep, send_a, send_b, gain_part):
    step = pl.program_id(0)
    core = my_place()[1]
    width = gq.shape[1]
    grad = dot_nn(heads[:, :HEADS], gate_t[...]) + dot_nn(heads[:, HEADS : HEADS + 2], decay_t[...])
    for i, ref in enumerate((gq, gk, gv)):
        grad = grad + dot_nt(ref[...], w[i])
    xf = x[...].astype(F32)
    inverse = lax.rsqrt(jnp.mean(xf * xf, -1, keepdims=True) + EPS)
    unit = xf * inverse
    add_to(gain_part, step == 0, jnp.sum(grad * unit, 0, keepdims=True))
    back = norm_back(grad, unit, inverse, gain_row(gain)).astype(LOW)
    for i in range(2):
        blocks = [back[:, (2 * i + b) * width : (2 * i + b + 1) * width] for b in range(2)]
        keep[i] = jnp.where(core == 0, blocks[0], blocks[1])
        away = jnp.where(core == 0, blocks[1], blocks[0])
        for part, send in enumerate((send_a, send_b)):

            @pl.when(step // 2 == part)
            def _():
                send[i] = away


def last(gq, gk, gv, w_t, heads, gate_t, decay_t, tokens, gain):
    width = gq.shape[1]
    rows = LEN // 4
    quarter = ((2, LEN, width), LOW, pl.BlockSpec((2, rows, width), lambda i: (0, i, 0)))


    def send(part):
        at = (lambda i: (0, jnp.minimum(i, 1), 0)) if part == 0 else (lambda i: (0, jnp.maximum(i - 2, 0), 0))
        return ((2, CH, width), LOW, pl.BlockSpec((2, rows, width), at))

    return run(
        "last", last_kernel, 4,
        [rows_of(gq, rows), rows_of(gk, rows), rows_of(gv, rows), full(w_t), rows_of(heads, rows),
         full(gate_t), full(decay_t), rows_of(tokens, rows), full(gain)],
        [quarter, send(0), send(1), out_full((1, D), F32)],
        (), 8.5,
    )


def attend_back_kernel(
    doc_ref, q_ref, k_ref, v_ref, pk_ref, pv_ref, gma, gmb, wo_ref, peak_ref, inv_ref,
    dq_ref, dk_ref, dv_ref, dpk_ref, dpv_ref, go_ref,
):
    k = k_ref[0]
    v = v_ref[0]
    keys_t = flat(k)
    pk = pk_ref[0]
    pv = pv_ref[0]
    pk_t = flat(pk)
    for ref in (dk_ref, dv_ref, dpk_ref, dpv_ref):
        ref[...] = jnp.zeros_like(ref)
    for half, gm in enumerate((gma, gmb)):
        rows = pl.ds(half * CH, CH)
        go_ref[rows, :] = dot_nt(gm[...], wo_ref[...]).astype(LOW)
    for block in range(LEN // QB):
        low_key, high_key = key_range(block)
        keys = pl.ds(low_key, high_key - low_key)
        rows = pl.ds(block * QB, QB)
        ok = allowed(doc_ref, block, low_key, high_key)
        q = q_ref[0, rows, :].astype(F32)
        go = go_ref[rows, :].astype(F32)
        outs = []
        for index in range(2):
            q_head = scaled_head(q, index)
            go_head = one_head(go, index)
            peak = peak_ref[0, index : index + 1, rows]
            inv = inv_ref[0, index : index + 1, rows]
            s = jnp.where(ok, dot_nt(k[low_key:high_key], q_head), NEG)
            sp = dot_nt(pk, q_head)
            prob = jnp.exp(s - peak) * inv
            prob_p = jnp.exp(sp - peak) * inv
            gp = dot_nt(v[low_key:high_key], go_head)
            gpp = dot_nt(pv, go_head)
            center = jnp.sum(prob * gp, 0, keepdims=True) + jnp.sum(prob_p * gpp, 0, keepdims=True)
            gs = (prob * (gp - center)).astype(LOW)
            gsp = (prob_p * (gpp - center)).astype(LOW)
            dk_ref[keys, :] += dot_nn(gs, q_head)
            dv_ref[keys, :] += dot_nn(prob.astype(LOW), go_head)
            dpk_ref[...] += dot_nn(gsp, q_head)
            dpv_ref[...] += dot_nn(prob_p.astype(LOW), go_head)
            feats = slice(index * HD, index * HD + HD)
            outs.append(dot_nn(keys_t[feats, low_key:high_key], gs) + dot_nn(pk_t[feats], gsp))
        dq_ref[rows, :] = jnp.concatenate(outs, 0).T * 8.0


def attend_back(doc_len, act, persistent, gma, gmb, w_o, peak, inv):
    width = act.shape[2]
    pairs = width // 128

    def part(i):
        return (act, pl.BlockSpec((1, LEN, 128), lambda g: (i, 0, g)))

    def pers(i):
        return (persistent, pl.BlockSpec((1, NP, 128), lambda g: (i, 0, g)))

    stat = pl.BlockSpec((1, 2, LEN), lambda g: (g, 0, 0))
    cols = near(((LEN, width), F32, pl.BlockSpec((LEN, 128), lambda g: (0, g))))
    small = far(((NP, width), F32, pl.BlockSpec((NP, 128), lambda g: (0, g))))
    return run(
        "attend_back", attend_back_kernel, pairs,
        [(doc_len, SMEM_SPEC), part(0), part(1), part(2), pers(0), pers(1), full(gma), full(gmb),
         rows_of(w_o, 128), (peak, stat), (inv, stat)],
        [cols, cols, cols, small, small],
        [pltpu.VMEM((LEN, 128), LOW)], 15.6,
    )


def conv_back_kernel(part, count, doc_ref, p_ref, taps_ref, datt_ref, *refs):
    extra, (gproj_ref, gtaps_ref, pad, padc) = refs[:count], refs[count:]
    width = p_ref.shape[2]
    pad[pl.ds(0, 8), :] = jnp.zeros((8, width), F32)
    padc[pl.ds(LEN, 8), :] = jnp.zeros((8, width), F32)
    pad[pl.ds(8, LEN), :] = p_ref[0]
    gt = [jnp.zeros((1, width), F32)] * KC
    ones_mat = same_head(width)
    for first in range(0, LEN, PRE_ROWS):
        rows = pl.ds(first, PRE_ROWS)
        age = ages(doc_ref, first, PRE_ROWS, width)
        c = conv_sum(pad, taps_ref, age, first, PRE_ROWS)
        sig = jax.nn.sigmoid(c)
        dy = datt_ref[rows, :]
        for ref in extra:
            if first < ref.shape[0]:
                dy = dy + ref[rows, :].astype(F32)
        if part < 2:
            a = c * sig
            inverse = lax.rsqrt(head_sum(a * a, ones_mat) + EPS)
            y = a * inverse
            dy = inverse * (dy - y * head_sum(dy * y, ones_mat))
        dc = dy * silu_slope(c, sig)
        padc[rows, :] = dc
        gt[0] = gt[0] + jnp.sum(dc * pad[pl.ds(first + 8, PRE_ROWS), :], 0, keepdims=True)
        for i in range(1, KC):
            shifted = jnp.where(age >= i, pad[pl.ds(first + 8 - i, PRE_ROWS), :], 0.0)
            gt[i] = gt[i] + jnp.sum(dc * shifted, 0, keepdims=True)
    gtaps_ref[...] = jnp.concatenate(gt, 0)
    for first in range(0, LEN, PRE_ROWS):
        total = taps_ref[0, 0:1, :].astype(F32) * padc[pl.ds(first, PRE_ROWS), :]
        for i in range(1, KC):
            age = ages(doc_ref, first + i, PRE_ROWS, width)
            total = total + taps_ref[0, i : i + 1, :].astype(F32) * jnp.where(
                age >= i, padc[pl.ds(first + i, PRE_ROWS), :], 0.0
            )
        gproj_ref[pl.ds(first, PRE_ROWS), :] = total.astype(LOW)


def conv_back(part, doc_len, p, taps, datt, extra):
    width = p.shape[2]
    count = len(extra)
    return run(
        "conv_back" + str(part), lambda *refs: conv_back_kernel(part, count, *refs), 1,
        [(doc_len, SMEM_SPEC), (p, pl.BlockSpec((1, LEN, width), lambda i: (part, 0, 0))),
         (taps, pl.BlockSpec((1, KC, width), lambda i: (part, 0, 0))), full(datt)] + [full(e) for e in extra],
        [near(out_full((LEN, width), LOW)), far(out_full((KC, width), F32))],
        [pltpu.VMEM((LEN + 8, width), F32), pltpu.VMEM((LEN + 8, width), F32)], 6.5,
    )


def body(
    tokens,
    gain_in,
    gain_mid,
    w_qkv,
    w_gate,
    w_decay,
    conv_kernel,
    persistent,
    w_out,
    mem_in,
    mem_out,
    w_up,
    w_down,
    doc_len,
    reset,
    cotangent,
):
    assert doc_len.shape[0] == 1 and lax.axis_size("narrow") == 4
    width = w_qkv.shape[2]
    size = lax.axis_size("wide")
    me = lax.axis_index("narrow")
    gain_in_f, gain_mid_f = gain_in.reshape(-1, 128), gain_mid.reshape(-1, 128)
    w_t = w_qkv.transpose(1, 0, 2)
    taps = conv_kernel
    gate_t, decay_t = w_gate.T, w_decay.T
    LAST.clear()
    PLACED.clear()
    for a in (tokens, w_t, w_out, mem_in, mem_out, w_down, persistent, gain_in_f, gain_mid_f, gate_t, decay_t, taps):
        put(a, pltpu.HBM)
    cot = Parts(cotangent)
    normed_in, gates, rates, projected, act, own_q, own_heads = pre(
        doc_len, tokens, gain_in_f, w_t, gate_t, decay_t, taps
    )

    cot.end()
    heads_in = Parts(own_heads)
    query = Parts(own_q)
    attended, peak, inv = attend(doc_len, act, persistent)
    cot_parts = [put(t, pltpu.HBM) for t in cot.settle()]
    w_gate_up = put(tie(w_up.transpose(1, 0, 2)), pltpu.VMEM)
    mem_in, mem_out, w_down = fetch(mem_in, mem_out, w_down)
    heads_in = heads_in.end()
    q_a, kc, vc, hk, ks, kcv, *pred = mem1(heads_in, mem_in, mem_out)
    pred = Halves(*pred)
    query.end()
    pred.middle()
    hid1, slope1, rec1, *join1 = recall1(q_a, gates, attended, w_out, mem_in, mem_out)
    join1 = Halves(*join1)
    pred = pred.end()
    join1.middle()
    q_parts = query.settle()
    q_b, err, slope_low, bcurve, m_in, m_out, hid2, slope2, rec2, *join2 = mem2(
        reset, rates, pred, q_parts, vc, kc, hk, ks, kcv, gates, attended, w_out, mem_in, mem_out
    )
    join2 = Halves(*join2)
    join1 = join1.end()
    join2.middle()
    na, cota, ha, gga, gua, fkeep, fsend, mloca, gain_a, *mid1 = feed(
        0, join1, tokens, gain_mid_f, w_gate_up, w_down, cot_parts
    )
    mid1 = Halves(*mid1)
    join2 = join2.end()
    mid1.middle()
    nb, cotb, hb, ggb, gub, fkeep, fsend, mlocb, gain_b, *mid2 = feed(
        1, join2, tokens, gain_mid_f, w_gate_up, w_down, cot_parts, (fkeep, fsend)
    )
    mid2 = Halves(*mid2)
    outs = Columns(fkeep, fsend)

    mid1.end()
    mid2.middle()
    mid1_terms = mid1.settle()
    ukeep, usend, dkeep, dsend = feed_weights(size, na, nb, gga, ggb, gua, gub, cota, cotb, ha, hb)
    up_sum = Rows(1, ukeep, usend)
    down_sum = Rows(2, dkeep, dsend)
    mid2 = mid2.end()
    gmb, locb, heads_b, d_in, d_out, dpre2, dback, gsb, sums, *gerr = mem2_back(
        width, reset, rates, mid2, cotb, gates, rec2, hid2, slope2, q_b, m_in, m_out, kc, hk, ks, bcurve, slope_low,
        mem_in, mem_out,
    )
    gerr = Halves(*gerr)
    gerr.middle()
    outs.middle()
    gma, loca, heads_a, g_in, g_out, dq1 = recall1_back(
        width, mid1_terms, cota, gates, rec1, hid1, slope1, q_a, mem_in, mem_out
    )
    down_sum.step()
    gerr.end()
    dq, dka, dva, dpk, dpv = attend_back(doc_len, act, persistent, gma, gmb, w_out, peak, inv)
    outs = outs.end()
    gerr_terms = gerr.settle()
    up_sum.step()
    base, sums_out, dq2, dk = mem2_late(reset, rates, err, hk, ks, gsb, slope_low, d_in, d_out, dpre2, m_in)
    down_sum.step()
    dpred, dpre1, v_share, kkeep, *ksends = mem1_back(width, gerr_terms, ks, base, dk, mem_in, mem_out)
    k_share = Columns(kkeep, *ksends)
    ikeep, isend, okeep, osend = mem_weights(
        size, reset, rates, g_in, g_out, d_in, d_out, kc, dpre1, dback, err, hk, dpred
    )
    in_sum = Rows(1, ikeep, isend)
    back_sum = Rows(1, okeep, osend)
    qkeep, qsend_a, qsend_b, heads, small_part = query_split(
        width, reset, normed_in, gates, heads_a, heads_b, sums, sums_out, dq1, dq2
    )
    q_share = Columns(qkeep, qsend_a, qsend_b)
    down_grads = down_sum.end()
    k_share.middle()
    q_share.middle()
    up_sum.step()
    gv, tap_v = conv_back(2, doc_len, projected, taps, dva, [v_share])
    gq, tap_q = conv_back(0, doc_len, projected, taps, dq, q_share.end())
    gk, tap_k = conv_back(1, doc_len, projected, taps, dka, k_share.end())
    in_sum.step()
    akeep, asend, bkeep, bsend = weights(size, normed_in, gma, gmb, attended, gq, gk, gv)
    w_sum = Rows(1, akeep, asend)
    q_sum = Rows(1, bkeep, bsend)
    up_grads = up_sum.end()
    lkeep, *lsends, gain_part = last(gq, gk, gv, w_t, heads, gate_t, decay_t, tokens, gain_in_f)
    in_share = Columns(lkeep, *lsends)
    own = jnp.concatenate([dpk, dpv], 0).reshape(-1, D)
    taps_part = jnp.concatenate([tap_q, tap_k, tap_v], 0).reshape(-1, D)
    late = jnp.concatenate([own, taps_part, gain_a + gain_b, small_part[: HEADS + 2], gain_part], 0)
    in_sum.step()
    back_sum.step()
    in_share.middle()
    up_grads = pinned(up_grads.transpose(1, 0, 2))
    output = pinned((jnp.concatenate([mloca, mlocb], 0) + outs[0].astype(F32) + outs[1].astype(F32)).astype(LOW))
    w_sum.step()
    late = Small(pinned(late), "wide")
    q_sum.step()
    in_grads = in_sum.end()
    late.step()
    back_sum.step()
    late.step()
    w_sum.step()
    late = late.end()
    late = Small(place_own(late, 2 * NP + 3 * KC, width, me), "narrow")
    q_sum.step()
    late.step()
    in_share = in_share.end()
    grad_input = pinned(in_share[0].astype(F32) + in_share[1].astype(F32) + jnp.concatenate([loca, locb], 0))
    back_grads = back_sum.end()
    late = late.end()
    w_grads = w_sum.end()
    q_grads = q_sum.end()
    pers_sum = late[: 2 * NP].reshape(2, NP, D)
    conv_sum = late[2 * NP : 2 * NP + 3 * KC].reshape(3, KC, D)
    vecs = late[2 * NP + 3 * KC :]
    rows = D // size
    gate_shard = cut(vecs[1 : HEADS + 1], lax.axis_index("wide") * rows, rows, 1).T
    return (
        output,
        grad_input,
        vecs[HEADS + 3],
        vecs[0],
        jnp.stack([q_grads[:, :width], q_grads[:, width:], w_grads[:, width:]], 1),
        gate_shard,
        vecs[HEADS + 1 : HEADS + 3].T,
        conv_sum,
        pers_sum,
        w_grads[:, :width].T,
        in_grads,
        back_grads,
        up_grads,
        down_grads,
    )


def solution(mesh):
    in_specs = (
        P("wide", None),
        P(),
        P(),
        P(None, None, "narrow"),
        P(),
        P(),
        P(None, None, "narrow"),
        P(None, None, "narrow"),
        P("narrow", None),
        P(None, "narrow"),
        P("narrow", None),
        P(None, None, "narrow"),
        P("narrow", None),
        P("wide", None),
        P("wide"),
        P("wide", "narrow"),
    )
    out_specs = (
        P("wide", "narrow"),
        P("wide", "narrow"),
        P(),
        P(),
        P("wide", None, "narrow"),
        P("wide", None),
        P(),
        P(),
        P(),
        P("narrow", "wide"),
        P("wide", "narrow"),
        P("narrow", "wide"),
        P("wide", None, "narrow"),
        P("narrow", "wide"),
    )
    return jax.shard_map(body, mesh=mesh, in_specs=in_specs, out_specs=out_specs, check_vma=False)
```
